32 devices in a mesh: seg: 4 (over z), tm: 8 (over y, x, core).
Axes of the slice: x: 2, y: 2, z: 4, core: 2. Of those that a mesh axis runs over, the one named last changes fastest.
Arguments:
- feats: bfloat16 [32, 4096, 192], P('seg', 'tm'), may hold values from -6 to 6
- spectral: bfloat16 [32, 1024, 384], P('seg', 'tm'), may hold values from -6 to 6
- target: bfloat16 [32, 1024, 128], P('seg', 'tm'), may hold values from -6 to 6
- valid_samples: int32 [32], P('seg'), may hold values from 5461 to 16384, as said below
- stem_weights: int32 [32, 4], P('seg'), may hold values from 1 to 4
- conv_weight: float32 [1536, 384], P('tm'), may hold values from -0.15625 to 0.15625
- query_weight: float32 [384, 384], P('tm'), may hold values from -0.046875 to 0.046875
- keyval_weight: float32 [384, 768], P('tm'), may hold values from -0.3125 to 0.3125
- out_weight: float32 [384, 384], P('tm'), may hold values from -6 to 6
- up_weight: float32 [384, 1536], P('tm'), may hold values from -0.3125 to 0.3125
- down_weight: float32 [1536, 384], P('tm'), may hold values from -0.15625 to 0.15625
- head_weight: float32 [384, 128], P('tm'), may hold values from -0.3125 to 0.3125
- gains: float32 [5, 384], P(None, 'tm'), may hold values from 0.5 to 1.5
- conv_first: float32 [1536, 384], P('tm'), as said below
- query_first: float32 [384, 384], P('tm')
- keyval_first: float32 [384, 768], P('tm')
- out_first: float32 [384, 384], P('tm')
- up_first: float32 [384, 1536], P('tm')
- down_first: float32 [1536, 384], P('tm')
- head_first: float32 [384, 128], P('tm')
- gain_first: float32 [5, 384], P(None, 'tm')
- conv_second: float32 [1536, 384], P('tm'), as said below
- query_second: float32 [384, 384], P('tm')
- keyval_second: float32 [384, 768], P('tm')
- out_second: float32 [384, 384], P('tm')
- up_second: float32 [384, 1536], P('tm')
- down_second: float32 [1536, 384], P('tm')
- head_second: float32 [384, 128], P('tm')
- gain_second: float32 [5, 384], P(None, 'tm')
Outputs:
- loss_sum: float32 [], replicated
- sample_count: float32 [], replicated
- grad_norm: float32 [], replicated
- conv_new: float32 [1536, 384], P('tm')
- query_new: float32 [384, 384], P('tm')
- keyval_new: float32 [384, 768], P('tm')
- out_new: float32 [384, 384], P('tm')
- up_new: float32 [384, 1536], P('tm')
- down_new: float32 [1536, 384], P('tm')
- head_new: float32 [384, 128], P('tm')
- gains_new: float32 [5, 384], P(None, 'tm')
- conv_first_new: float32 [1536, 384], P('tm')
- query_first_new: float32 [384, 384], P('tm')
- keyval_first_new: float32 [384, 768], P('tm')
- out_first_new: float32 [384, 384], P('tm')
- up_first_new: float32 [384, 1536], P('tm')
- down_first_new: float32 [1536, 384], P('tm')
- head_first_new: float32 [384, 128], P('tm')
- gain_first_new: float32 [5, 384], P(None, 'tm')
- conv_second_new: float32 [1536, 384], P('tm')
- query_second_new: float32 [384, 384], P('tm')
- keyval_second_new: float32 [384, 768], P('tm')
- out_second_new: float32 [384, 384], P('tm')
- up_second_new: float32 [384, 1536], P('tm')
- down_second_new: float32 [1536, 384], P('tm')
- head_second_new: float32 [384, 128], P('tm')
- gain_second_new: float32 [5, 384], P(None, 'tm')
The draws below stay inside these ranges and needn't reach their ends.
Inputs may be any that keep to these rules, and one draw needn't show every extreme that they name: `valid_samples`: in each aligned run of 8 segments (those of one index of seg) at least one segment has more than 14336 valid samples; some segment is complete. `conv_first`: first moments have both signs. `conv_second`: second moments are positive.
All inputs are finite; a program needn't handle non-finite values.
Results may differ from the reference program's by a relative error of at most 0.005.
The reference program's roundings to bfloat16 on the way (of `queries`, `keyval` and `attended`) count: a program that leaves them out, or rounds other values in their place, can miss the bound.
Values may be sent and summed in bfloat16 or wider, within the bound.
No kernel may reach another device: no remote copies, remote signals or barrier semaphores. Data moves between devices by JAX's collectives and lax.ppermute only.
A program may use at most 320 MiB of HBM per device.

```python
import math
import jax
import jax.numpy as jnp
from jax import lax

D = 384
H = 8
FF = 1536
CIN = 192
STEMS = 4
KER = 8
SUB = 16
STEP = 10
SEG_DEV = 8
TT_DEV = 128
HD = 48
OUTW = 128
SEGS = 32
TT = 1024
FT = 1024
SAMPLES = 16384


clip_limit = 0.001


def grad_scale():
    return clip_limit / math.sqrt(KER * CIN * D + 4 * D * D + 2 * D * FF + D * OUTW + 5 * D)


def first_moment(key, shape, factor):
    return 0.111 * factor * grad_scale() * jax.random.normal(key, shape, jnp.float32)


def second_moment(key, shape, factor):
    spread = jnp.exp(jax.random.uniform(key, shape, jnp.float32, 0.0, math.log(4.0)))
    return 0.001 / 0.999 * (factor * grad_scale()) ** 2 * spread


def draw_valid_samples(key, part):
    key = jax.random.fold_in(key, 11)
    length_key, pick_key, tail_key, full_key = jax.random.split(key, 4)
    lengths = jax.random.randint(length_key, (SEGS,), SAMPLES // 3, SAMPLES + 1)
    tails = jax.random.randint(tail_key, (SEGS,), SAMPLES - TT_DEV * SUB + 1, SAMPLES + 1)
    picked = jax.random.randint(pick_key, (SEGS // SEG_DEV,), 0, SEG_DEV)
    reaching = jnp.arange(SEGS) % SEG_DEV == jnp.repeat(picked, SEG_DEV)
    full_index = jax.random.randint(full_key, (), 0, SEGS)
    chosen = jnp.where(reaching, tails, lengths)
    return jnp.where(jnp.arange(SEGS) == full_index, SAMPLES, chosen).astype(jnp.int32)


def draw_conv_first(key, part):
    key = jax.random.fold_in(key, 21)
    return first_moment(key, (KER * CIN, D), 1.0)


def draw_query_first(key, part):
    key = jax.random.fold_in(key, 22)
    return first_moment(key, (D, D), 1.0)


def draw_keyval_first(key, part):
    key = jax.random.fold_in(key, 23)
    return first_moment(key, (D, 2 * D), 1.0)


def draw_out_first(key, part):
    key = jax.random.fold_in(key, 24)
    return first_moment(key, (D, D), 0.1)


def draw_up_first(key, part):
    key = jax.random.fold_in(key, 25)
    return first_moment(key, (D, FF), 0.15)


def draw_down_first(key, part):
    key = jax.random.fold_in(key, 26)
    return first_moment(key, (FF, D), 1.0)


def draw_head_first(key, part):
    key = jax.random.fold_in(key, 27)
    return first_moment(key, (D, OUTW), 1.0)


def draw_gain_first(key, part):
    key = jax.random.fold_in(key, 28)
    return first_moment(key, (5, D), 3.0)


def draw_conv_second(key, part):
    key = jax.random.fold_in(key, 31)
    return second_moment(key, (KER * CIN, D), 1.0)


def draw_query_second(key, part):
    key = jax.random.fold_in(key, 32)
    return second_moment(key, (D, D), 1.0)


def draw_keyval_second(key, part):
    key = jax.random.fold_in(key, 33)
    return second_moment(key, (D, 2 * D), 1.0)


def draw_out_second(key, part):
    key = jax.random.fold_in(key, 34)
    return second_moment(key, (D, D), 0.1)


def draw_up_second(key, part):
    key = jax.random.fold_in(key, 35)
    return second_moment(key, (D, FF), 0.15)


def draw_down_second(key, part):
    key = jax.random.fold_in(key, 36)
    return second_moment(key, (FF, D), 1.0)


def draw_head_second(key, part):
    key = jax.random.fold_in(key, 37)
    return second_moment(key, (D, OUTW), 1.0)


def draw_gain_second(key, part):
    key = jax.random.fold_in(key, 38)
    return second_moment(key, (5, D), 3.0)


def set_ends(result, rng, smallest, top_value):
    longest = result.shape.index(max(result.shape))
    spots = []
    for shift in (0, 1):
        where = [jax.random.randint(jax.random.fold_in(rng, axis), (), 0, length) for axis, length in enumerate(result.shape)]
        where[longest] = (where[longest] + shift) % result.shape[longest]
        spots.append(tuple(where))
    return result.at[spots[0]].set(smallest).at[spots[1]].set(top_value)


def level_of(rng, extent, pieces, least, high):
    def one(dim, blocks):
        heights = jax.random.uniform(jax.random.fold_in(jax.random.fold_in(rng, 6), dim), (blocks,), jnp.float32, least / len(pieces), high / len(pieces))
        return jnp.repeat(jnp.exp(heights), extent[dim] // blocks).reshape((-1,) + (1,) * (len(extent) - dim - 1))

    level = one(*pieces[0])
    for cut in pieces[1:]:
        level = level * one(*cut)
    return level


def scatter_about(rng, extent, deviation, limit, shards=(), kind=jnp.bfloat16):
    loudness = level_of(rng, extent, shards, -0.22, 0.18) if shards else 1.0
    drawn = jax.random.normal(rng, extent, jnp.float32) * deviation * loudness
    return jnp.minimum(jnp.maximum(drawn, -limit), limit).astype(kind)


def setup_inputs(seed: int = 0) -> dict:
    key_list = jax.random.split(jax.random.key(seed), 30)
    feats = scatter_about(key_list[0], (SEGS, 4 * TT, CIN), 1.0, 6.0, ((0, 4), (1, 8)))
    spectral = scatter_about(key_list[1], (SEGS, FT, D), 1.0, 6.0, ((0, 4), (1, 8)))
    target = scatter_about(key_list[2], (SEGS, TT, OUTW), 1.0, 6.0, ((0, 4), (1, 8)))
    valid_samples = draw_valid_samples(jax.random.fold_in(key_list[29], 71), 0)
    stem_weights = set_ends(jax.random.randint(key_list[4], (SEGS, STEMS), 1, 5), jax.random.fold_in(key_list[4], 1), 1, 4).astype(jnp.int32)
    conv_weight = scatter_about(key_list[5], (KER * CIN, D), (KER * CIN) ** -0.5, 0.15625, ((0, 8),), jnp.float32)
    query_weight = scatter_about(key_list[6], (D, D), (D * HD) ** -0.5, 0.046875, ((0, 8),), jnp.float32)
    keyval_weight = scatter_about(key_list[7], (D, 2 * D), D ** -0.5, 0.3125, ((0, 8),), jnp.float32)
    out_weight = scatter_about(key_list[8], (D, D), (max(1, 3 * D // FT)) ** -0.5, 6.0, ((0, 8),), jnp.float32)
    up_weight = scatter_about(key_list[9], (D, FF), D ** -0.5, 0.3125, ((0, 8),), jnp.float32)
    down_weight = scatter_about(key_list[10], (FF, D), FF ** -0.5, 0.15625, ((0, 8),), jnp.float32)
    head_weight = scatter_about(key_list[11], (D, OUTW), D ** -0.5, 0.3125, ((0, 8),), jnp.float32)
    gains = jnp.clip(1.0 + 0.1 * jax.random.normal(key_list[12], (5, D), jnp.float32), 0.5, 1.5)
    conv_first = draw_conv_first(jax.random.fold_in(key_list[29], 71), 0)
    query_first = draw_query_first(jax.random.fold_in(key_list[29], 71), 0)
    keyval_first = draw_keyval_first(jax.random.fold_in(key_list[29], 71), 0)
    out_first = draw_out_first(jax.random.fold_in(key_list[29], 71), 0)
    up_first = draw_up_first(jax.random.fold_in(key_list[29], 71), 0)
    down_first = draw_down_first(jax.random.fold_in(key_list[29], 71), 0)
    head_first = draw_head_first(jax.random.fold_in(key_list[29], 71), 0)
    gain_first = draw_gain_first(jax.random.fold_in(key_list[29], 71), 0)
    conv_second = draw_conv_second(jax.random.fold_in(key_list[29], 71), 0)
    query_second = draw_query_second(jax.random.fold_in(key_list[29], 71), 0)
    keyval_second = draw_keyval_second(jax.random.fold_in(key_list[29], 71), 0)
    out_second = draw_out_second(jax.random.fold_in(key_list[29], 71), 0)
    up_second = draw_up_second(jax.random.fold_in(key_list[29], 71), 0)
    down_second = draw_down_second(jax.random.fold_in(key_list[29], 71), 0)
    head_second = draw_head_second(jax.random.fold_in(key_list[29], 71), 0)
    gain_second = draw_gain_second(jax.random.fold_in(key_list[29], 71), 0)
    return dict(feats=feats, spectral=spectral, target=target, valid_samples=valid_samples, stem_weights=stem_weights, conv_weight=conv_weight, query_weight=query_weight, keyval_weight=keyval_weight, out_weight=out_weight, up_weight=up_weight, down_weight=down_weight, head_weight=head_weight, gains=gains, conv_first=conv_first, query_first=query_first, keyval_first=keyval_first, out_first=out_first, up_first=up_first, down_first=down_first, head_first=head_first, gain_first=gain_first, conv_second=conv_second, query_second=query_second, keyval_second=keyval_second, out_second=out_second, up_second=up_second, down_second=down_second, head_second=head_second, gain_second=gain_second)


highest = lax.Precision.HIGHEST
clip_limit = 0.001
beta_first = 0.9
beta_second = 0.999
learn_rate = 0.03
fast_rate = 0.5
weight_decay = 0.05
adam_epsilon = 1e-08
norm_epsilon = 1e-05

@jax.custom_vjp
def low(v):
    return lax.optimization_barrier(v.astype(jnp.bfloat16)).astype(jnp.float32)

@jax.custom_vjp
def low_back(v):
    return v

def low_keep(v):
    return (low(v), None)

def low_pass(kept, grad):
    return (grad,)

def back_keep(v):
    return (v, None)

def back_low(kept, grad):
    return (low(grad),)
low.defvjp(low_keep, low_pass)
low_back.defvjp(back_keep, back_low)

def round_both(value):
    return low(low_back(value))

def product(left, right):
    return jnp.dot(left, right, precision=highest)

def layer_norm(values, gain):
    centred = values - lax.optimization_barrier(jnp.mean(values, -1, keepdims=True))
    return centred * lax.rsqrt(lax.optimization_barrier(jnp.mean(centred * centred, -1, keepdims=True)) + norm_epsilon) * gain

def gelu_exact(values):
    return jax.nn.gelu(values, approximate=False)

def unfold_frames(frames):
    segments, length, channels = frames.shape
    padded = jnp.pad(frames, ((0, 0), (2, 2), (0, 0)))
    front = padded[:, :length].reshape(segments, length // 4, 4 * channels)
    behind = padded[:, 4:length + 4].reshape(segments, length // 4, 4 * channels)
    return jnp.concatenate([front, behind], -1)

def attend_segment(operands):
    queries, keys, values = operands
    scores = low_back(jnp.einsum('qhd,khd->hqk', queries, keys, precision=highest))
    weights = low(jax.nn.softmax(scores, -1))
    return round_both(jnp.einsum('hqk,khd->qhd', weights, values, precision=highest))

def loss_weights(valid_samples, stem_weights):
    columns = jnp.arange(OUTW)
    position = jnp.arange(TT)[:, None] * SUB + (columns % SUB)[None, :]
    live = (position[None] < valid_samples[:, None, None]).astype(jnp.float32)
    chosen = ((columns // (2 * SUB))[:, None] == jnp.arange(STEMS)[None, :]).astype(jnp.float32)
    per_column = lax.optimization_barrier(jnp.sum(stem_weights.astype(jnp.float32)[:, None, :] * chosen[None], -1))
    return live * per_column[:, None, :]

def forward(params, frames, spectral, target, mask_weights, sample_count):
    conv_weight, query_weight, keyval_weight, out_weight, up_weight, down_weight, head_weight, gain_rows = params
    gain_low = low(gain_rows)
    conv_out = low_back(product(unfold_frames(frames), low(conv_weight)))
    stream = gelu_exact(conv_out)
    normed = low(layer_norm(stream, gain_low[0]))
    queries = round_both(product(normed, low(query_weight))).reshape(SEGS, TT, H, HD)
    spectral_normed = low(layer_norm(spectral, gain_low[1]))
    keyval = round_both(product(spectral_normed, low(keyval_weight)))
    keys = keyval[..., :D].reshape(SEGS, FT, H, HD)
    values = keyval[..., D:].reshape(SEGS, FT, H, HD)
    attended = lax.map(jax.checkpoint(attend_segment), (queries, keys, values)).reshape(SEGS, TT, D)
    branch = low_back(product(attended, low(out_weight)))
    stream_mid = stream + gain_low[3] * branch
    ffn_in = low(layer_norm(stream_mid, gain_low[2]))
    hidden = low_back(product(ffn_in, low(up_weight)))
    ffn_out = low_back(product(low(gelu_exact(hidden)), low(down_weight)))
    stream_end = stream_mid + gain_low[4] * ffn_out
    predicted = low_back(product(low(stream_end), low(head_weight)))
    error = predicted - target
    loss_sum = jnp.sum(mask_weights * (jnp.sqrt(error * error + 1.0) - 1.0))
    return (loss_sum / sample_count, loss_sum)

def adam_update(master, first, second, grad, factor, rate):
    clipped = grad * factor
    first_new = beta_first * first + (1.0 - beta_first) * clipped
    second_new = beta_second * second + (1.0 - beta_second) * clipped * clipped
    moment_hat = first_new / (1.0 - beta_first ** STEP)
    square_hat = second_new / (1.0 - beta_second ** STEP)
    master_new = master - rate * (moment_hat / (jnp.sqrt(square_hat) + adam_epsilon) + weight_decay * master)
    return (master_new, first_new, second_new)

def reference(feats, spectral, target, valid_samples, stem_weights, conv_weight, query_weight, keyval_weight, out_weight, up_weight, down_weight, head_weight, gains, conv_first, query_first, keyval_first, out_first, up_first, down_first, head_first, gain_first, conv_second, query_second, keyval_second, out_second, up_second, down_second, head_second, gain_second):
    params = (conv_weight, query_weight, keyval_weight, out_weight, up_weight, down_weight, head_weight, gains)
    firsts = (conv_first, query_first, keyval_first, out_first, up_first, down_first, head_first, gain_first)
    seconds = (conv_second, query_second, keyval_second, out_second, up_second, down_second, head_second, gain_second)
    rates = (learn_rate, learn_rate, learn_rate, fast_rate, learn_rate, learn_rate, learn_rate, fast_rate)
    mask_weights = loss_weights(valid_samples, stem_weights)
    sample_count = jnp.sum(valid_samples).astype(jnp.float32)
    inputs = (feats.astype(jnp.float32), spectral.astype(jnp.float32), target.astype(jnp.float32), mask_weights, sample_count)

    def objective(*weights):
        return forward(weights, *inputs)
    scaled_loss, pullback, loss_sum = jax.vjp(objective, *params, has_aux=True)
    grads = pullback(jnp.ones((), jnp.float32))
    squares = jnp.zeros((), jnp.float32)
    for grad in grads:
        squares = squares + jnp.sum(grad * grad)
    grad_norm = jnp.sqrt(squares)
    factor = jnp.minimum(1.0, clip_limit / (grad_norm + 1e-06))
    updated = [adam_update(m, f, s, g, factor, r) for m, f, s, g, r in zip(params, firsts, seconds, grads, rates)]
    return (loss_sum, sample_count, grad_norm, updated[0][0], updated[1][0], updated[2][0], updated[3][0], updated[4][0], updated[5][0], updated[6][0], updated[7][0], updated[0][1], updated[1][1], updated[2][1], updated[3][1], updated[4][1], updated[5][1], updated[6][1], updated[7][1], updated[0][2], updated[1][2], updated[2][2], updated[3][2], updated[4][2], updated[5][2], updated[6][2], updated[7][2])
```

```python
import functools
import jax
import jax.numpy as jnp
from jax import lax
from jax.experimental import pallas as pl
from jax.experimental.pallas import tpu as pltpu
from jax.sharding import PartitionSpec as P

H = 8
STEMS = 4
SUB = 16
STEP = 10
LANES = 128

clip_limit = 0.001
beta_first = 0.9
beta_second = 0.999
learn_rate = 0.03
fast_rate = 0.5
weight_decay = 0.05
adam_epsilon = 1e-08
norm_epsilon = 1e-05

bfloat = jnp.bfloat16
float32 = jnp.float32
VMEM_LIMIT = 60 * 1024 * 1024


def mm(left, right):
    return lax.dot_general(left, right, (((1,), (0,)), ((), ())), preferred_element_type=float32)


def nt(left, right):
    return lax.dot_general(left, right, (((1,), (1,)), ((), ())), preferred_element_type=float32)


def tn(left, right):
    return lax.dot_general(left, right, (((0,), (0,)), ((), ())), preferred_element_type=float32)


def iota(shape, dim):
    return lax.broadcasted_iota(jnp.int32, shape, dim)


def norm_parts(values):
    centred = values - jnp.mean(values, -1, keepdims=True)
    scale = lax.rsqrt(jnp.mean(centred * centred, -1, keepdims=True) + norm_epsilon)
    return centred * scale, scale


def norm_back(unit, scale, gain, upstream):
    inner = upstream * gain
    value_grad = scale * (
        inner
        - jnp.mean(inner, -1, keepdims=True)
        - unit * jnp.mean(inner * unit, -1, keepdims=True)
    )
    return value_grad, jnp.sum(upstream * unit, 0, keepdims=True)


def gelu_both(values):
    upper = 0.5 * (1.0 + lax.erf(values * 0.7071067811865476))
    density = jnp.exp(-0.5 * values * values) * 0.3989422804014327
    return values * upper, upper + values * density


def spread_matrix(width, head_size):
    shape = (width, width // head_size * LANES)
    lane = iota(shape, 1)
    inside = lane % LANES
    source = (lane // LANES) * head_size + inside
    hit = jnp.logical_and(iota(shape, 0) == source, inside < head_size)
    return jnp.where(hit, 1.0, 0.0).astype(bfloat)


def with_column(block, column, head_size):
    lane = iota(block.shape, 1)
    high = column.astype(bfloat).astype(float32)
    rest = column - high
    middle = rest.astype(bfloat).astype(float32)
    low = rest - middle
    pieces = jnp.where(lane == head_size, high, jnp.where(lane == head_size + 1, middle, low))
    spare = jnp.logical_and(lane >= head_size, lane < head_size + 3)
    return jnp.where(spare, pieces, block.astype(float32)).astype(bfloat)


class Sizes:
    def __init__(self, n, feats, spectral, target, conv_weight, up_weight):
        self.n = n
        self.segments = feats.shape[0]
        self.parts = n // self.segments
        self.tokens_dev = spectral.shape[1]
        self.D = spectral.shape[2]
        self.taps = conv_weight.shape[0] * n
        self.frame = self.taps // 2
        self.F = up_weight.shape[1]
        self.out = target.shape[2]
        self.tokens = self.segments * self.tokens_dev
        self.keys = self.tokens * self.parts
        self.hd = self.D // H
        self.wide = H * LANES
        self.w = self.D // n
        self.cw = self.taps // n
        self.uw = self.w * (self.F // self.D)
        self.fw = self.F // n
        self.hw = self.w * self.out // self.D
        self.direct = self.parts == 1 and self.w % 16 == 0 and self.hw % 16 == 0 and self.hw > 0
        self.first_rows = self.cw + 3 * self.w + 16
        self.second_rows = self.w + self.uw + self.fw + self.hw
        self.block = 256
        self.query_block = 256 if self.keys <= 1024 else 128


def pack_weights(z, tm_place, conv, query, keyval, out, up, down, head, gains):
    D, w = z.D, z.w

    def kernel(place_ref, conv_r, query_r, keyval_r, out_r, up_r, down_r, head_r, gains_r, o_ref):
        row = 0

        def put(value):
            nonlocal row
            o_ref[row : row + value.shape[0], :] = value.astype(bfloat)
            row += value.shape[0]

        put(conv_r[...])
        put(query_r[...])
        put(keyval_r[:, :D])
        put(keyval_r[:, D:])
        start = place_ref[0] * w
        shift = jnp.where(iota((w, D), 1) == iota((w, D), 0) + start, 1.0, 0.0).astype(bfloat)
        placed = mm(gains_r[...].astype(bfloat), shift)
        put(jnp.concatenate([placed, jnp.zeros((16 - placed.shape[0], D), float32)], 0))
        put(out_r[...])
        for c in range(z.F // D):
            put(up_r[:, c * D : (c + 1) * D])
        put(down_r[...])
        rows = z.hw
        put(jnp.concatenate([head_r[g * rows : (g + 1) * rows, :] for g in range(D // z.out)], 1))

    vmem = pl.BlockSpec(memory_space=pltpu.VMEM)
    return pl.pallas_call(
        kernel,
        out_shape=jax.ShapeDtypeStruct((z.first_rows + z.second_rows, D), bfloat),
        in_specs=[pl.BlockSpec(memory_space=pltpu.SMEM)] + [vmem] * 8,
        out_specs=vmem,
        name="pack_weights",
    )(tm_place, conv, query, keyval, out, up, down, head, gains)


def pack_tokens(z, feats, spectral, target):
    channels = feats.shape[2]
    rows = z.tokens_dev
    width = z.frame + z.D + z.out

    def kernel(f_ref, s_ref, t_ref, o_ref, scratch):
        frames = f_ref[0].astype(float32)
        pieces = []
        for c in range(0, channels, LANES):
            scratch[c // LANES, :, : min(LANES, channels - c)] = frames[:, c : c + LANES]
        for j in range(4):
            for c in range(0, channels, LANES):
                piece = scratch[c // LANES, pl.ds(j, rows, stride=4), :]
                pieces.append(piece[:, : min(LANES, channels - c)])
        o_ref[0, :, : z.frame] = jnp.concatenate(pieces, 1).astype(bfloat)
        o_ref[0, :, z.frame : z.frame + z.D] = s_ref[0]
        o_ref[0, :, z.frame + z.D :] = t_ref[0]

    return pl.pallas_call(
        kernel,
        grid=(z.segments,),
        out_shape=jax.ShapeDtypeStruct((z.segments, rows, width), bfloat),
        in_specs=[
            pl.BlockSpec((1, 4 * rows, channels), lambda i: (i, 0, 0)),
            pl.BlockSpec((1, rows, z.D), lambda i: (i, 0, 0)),
            pl.BlockSpec((1, rows, z.out), lambda i: (i, 0, 0)),
        ],
        out_specs=pl.BlockSpec((1, rows, width), lambda i: (i, 0, 0)),
        scratch_shapes=[pltpu.VMEM((pl.cdiv(channels, LANES), 4 * rows, LANES), float32)],
        name="pack_tokens",
    )(feats, spectral, target)


def front(z, moved, spectral_all, halo, weights):
    D, T, K, W, B = z.D, z.tokens, z.keys, z.wide, z.block
    frame, taps, hd = z.frame, z.taps, z.hd
    half = frame // 2
    QB = z.query_block

    def kernel(*refs):
        refs = list(refs)
        x_ref, sp_ref = refs[:2]
        refs = refs[2:]
        if z.parts > 1:
            before_ref, after_ref = refs[:2]
            refs = refs[2:]
        if z.direct:
            blob_ref = refs[0]
            refs = refs[1:]
        else:
            wc, wq, wkv, gains_ref = refs[:4]
            refs = refs[4:]
        (stream_o, slope_o, normed_o, sn_o, q_o, k_o, v_o, att_o) = refs[:8]
        refs = refs[8:]
        conv_s, wq_s, wk_s, wv_s = refs[:4]
        refs = refs[4:]
        if z.direct:
            blob_s, wc, wqkv, sem = refs
            copy = pltpu.make_async_copy(blob_ref.at[:, 0 : z.first_rows], blob_s, sem)
            copy.start()
            copy.wait()
            w, cw = z.w, z.cw
            total = jnp.zeros((16, D), float32)
            for j in range(z.n):
                wc[j * cw : (j + 1) * cw, :] = blob_s[j, 0:cw, :]
                for c in range(3):
                    first = cw + c * w
                    wqkv[j * w : (j + 1) * w, c * D : (c + 1) * D] = blob_s[j, first : first + w, :]
                total = total + blob_s[j, cw + 3 * w : cw + 3 * w + 16, :].astype(float32)
            gain_query, gain_keys = total[0:1, :], total[1:2, :]
            parts_w = [wqkv[:, c * D : (c + 1) * D] for c in range(3)]
        else:
            gain_query, gain_keys = gains_ref[0:1, :], gains_ref[1:2, :]
            parts_w = [wq[...], wkv[:, :D], wkv[:, D:]]
        spread = spread_matrix(D, hd)
        for target_s, part in zip((wq_s, wk_s, wv_s), parts_w):
            target_s[...] = mm(part, spread).astype(bfloat)

        conv_s[...] = mm(x_ref[...], wc[half : half + frame, :])
        row = iota((T, D), 0)
        older = pltpu.roll(mm(x_ref[:, half:], wc[:half, :]), 1, 0)
        first_row, last_row = 0.0, 0.0
        if z.parts > 1:
            first_row = mm(before_ref[...], wc[:half, :])[0:1, :]
            last_row = mm(after_ref[...], wc[half + frame :, :])[0:1, :]
        conv_s[...] += jnp.where(row == 0, first_row, older)
        newer = pltpu.roll(mm(x_ref[:, :half], wc[half + frame :, :]), T - 1, 0)
        conv_s[...] += jnp.where(row == T - 1, last_row, newer)

        def token_block(i, carry):
            rows = pl.ds(pl.multiple_of(i * B, B), B)
            stream, slope = gelu_both(conv_s[rows, :])
            stream_o[rows, :] = stream
            slope_o[rows, :] = slope
            unit, _ = norm_parts(stream)
            normed = (unit * gain_query).astype(bfloat)
            normed_o[rows, :] = normed
            q_o[rows, :] = mm(normed, wq_s[...]).astype(bfloat)
            return carry

        lax.fori_loop(0, T // B, token_block, 0)

        def key_block(i, carry):
            rows = pl.ds(pl.multiple_of(i * B, B), B)
            unit, _ = norm_parts(sp_ref[rows, :].astype(float32))
            normed = (unit * gain_keys).astype(bfloat)
            sn_o[rows, :] = normed
            inside = iota((B, W), 1) % LANES
            spare = jnp.logical_and(inside >= hd, inside < hd + 3)
            k_o[rows, :] = jnp.where(spare, -1.0, mm(normed, wk_s[...])).astype(bfloat)
            v_o[rows, :] = jnp.where(spare, -1.0, mm(normed, wv_s[...])).astype(bfloat)
            return carry

        lax.fori_loop(0, K // B, key_block, 0)

        def head(h, carry):
            lanes = pl.ds(pl.multiple_of(h * LANES, LANES), LANES)
            for b in range(T // QB):
                rows = slice(b * QB, (b + 1) * QB)
                q = q_o[rows, lanes]
                scores = nt(q, k_o[:, lanes])
                top = jnp.max(scores, -1, keepdims=True)
                grown = jnp.exp(scores - top)
                mass = jnp.sum(grown, -1, keepdims=True)
                probs = (grown * (1.0 / mass)).astype(bfloat)
                att_o[rows, lanes] = mm(probs, v_o[:, lanes]).astype(bfloat)
                q_o[rows, lanes] = with_column(q, top + jnp.log(mass), hd)
            return carry

        lax.fori_loop(0, H, head, 0)

    vmem = pl.BlockSpec(memory_space=pltpu.VMEM)
    in_specs = [pl.BlockSpec((T, frame), lambda i: (0, 0))]
    args = [moved]
    if z.parts > 1:
        args += [spectral_all, halo[0], halo[1]]
        in_specs += [pl.BlockSpec((K, D), lambda i: (0, 0))] + [pl.BlockSpec((16, D), lambda i: (0, 0))] * 2
    else:
        args.append(moved)
        in_specs.append(pl.BlockSpec((T, D), lambda i: (0, frame // D)))
    scratch = [
        pltpu.VMEM((T, D), float32),
        pltpu.VMEM((D, W), bfloat),
        pltpu.VMEM((D, W), bfloat),
        pltpu.VMEM((D, W), bfloat),
    ]
    if z.direct:
        args.append(weights[0])
        in_specs.append(pl.BlockSpec(memory_space=pl.ANY))
        scratch += [
            pltpu.VMEM((z.n, z.first_rows, D), bfloat),
            pltpu.VMEM((taps, D), bfloat),
            pltpu.VMEM((D, 3 * D), bfloat),
            pltpu.SemaphoreType.DMA,
        ]
    else:
        for array in (weights[0], weights[1], weights[2], weights[7]):
            args.append(array)
            in_specs.append(pl.BlockSpec(array.shape, lambda i: (0, 0)))
    shapes = [
        ((T, D), float32),
        ((T, D), float32),
        ((T, D), bfloat),
        ((K, D), bfloat),
        ((T, W), bfloat),
        ((K, W), bfloat),
        ((K, W), bfloat),
        ((T, W), bfloat),
    ]
    return pl.pallas_call(
        kernel,
        grid=(1,),
        out_shape=[jax.ShapeDtypeStruct(s, d) for s, d in shapes],
        in_specs=in_specs,
        out_specs=[pl.BlockSpec(s, lambda i: (0, 0)) for s, d in shapes],
        scratch_shapes=scratch,
        compiler_params=pltpu.CompilerParams(vmem_limit_bytes=VMEM_LIMIT),
        cost_estimate=pl.CostEstimate(flops=30_000_000_000, bytes_accessed=20_000_000, transcendentals=10_000_000),
        name="front",
    )(*args)


def emit_blocks(z, meta_ref, keep_o, send_o, sources):
    chip, core = meta_ref[6], meta_ref[7]
    for m in range(z.n // 2):
        owner = (chip ^ m) * 2
        for out, place in ((keep_o, owner + core), (send_o, owner + 1 - core)):
            row = 0
            for ref, rows, pieces in sources:
                for lane in range(0, ref.shape[-1], z.D):
                    if ref.shape[-1] >= z.D:
                        here = ref[pl.ds(pl.multiple_of(place * rows, 16), rows), lane : lane + z.D]
                        out[m, row : row + rows, :] = here.astype(out.dtype)
                        row += rows
                    else:
                        size = rows // pieces
                        for g in range(pieces):
                            start = pl.multiple_of(place * rows + g * size, 16)
                            here = ref[pl.ds(start, size), :]
                            lanes = slice(g * ref.shape[-1], (g + 1) * ref.shape[-1])
                            out[m, row : row + size, lanes] = here.astype(out.dtype)
                        row += size


def middle(z, meta, count, stream, att, moved, target, weights):
    D, T, W, B, F, O = z.D, z.tokens, z.wide, z.block, z.F, z.out
    hd = z.hd

    def kernel(meta_ref, count_ref, stream_ref, att_ref, target_ref, *refs):
        refs = list(refs)
        if z.direct:
            blob_ref = refs[0]
            refs = refs[1:]
        else:
            wo, wu, wd, wh, gains_ref = refs[:5]
            refs = refs[5:]
        if z.direct:
            do_o, mid_o, misc_o, keep_o, send_o = refs[:5]
            refs = refs[5:]
        else:
            do_o, mid_o, misc_o, go_o, gu_o, gd_o, gh_o = refs[:7]
            refs = refs[7:]
        wop, act_s, hg_s, fin_s, fg_s, low_s, pg_s, bg_s, go_s, gu_s, gd_s, gh_s = refs[:12]
        refs = refs[12:]
        if z.direct:
            blob_s, gain_s, wo, wu, wd, wh, sem, sem2 = refs
            w, uw, fw, hw = z.w, z.uw, z.fw, z.hw
            copy = pltpu.make_async_copy(blob_ref.at[:, z.first_rows :], blob_s, sem)
            copy.start()
            copy2 = pltpu.make_async_copy(blob_ref.at[:, z.first_rows - 16 : z.first_rows], gain_s, sem2)
            copy2.start()
            copy.wait()
            copy2.wait()
            total = jnp.zeros((16, D), float32)
            for j in range(z.n):
                wo[j * w : (j + 1) * w, :] = blob_s[j, 0:w, :]
                for c in range(F // D):
                    first = w + c * w
                    wu[j * w : (j + 1) * w, c * D : (c + 1) * D] = blob_s[j, first : first + w, :]
                wd[j * fw : (j + 1) * fw, :] = blob_s[j, w + uw : w + uw + fw, :]
                for g in range(D // O):
                    start = j * w + g * hw
                    wh[start : start + hw, :] = blob_s[j, w + uw + fw :, g * O : (g + 1) * O]
                total = total + gain_s[j].astype(float32)
        else:
            total = gains_ref[...]
        gain_ffn, scale_attn, scale_ffn = total[2:3, :], total[3:4, :], total[4:5, :]
        spread = spread_matrix(D, hd)
        wop[...] = tn(spread, wo[...]).astype(bfloat)
        misc_o[...] = jnp.zeros_like(misc_o)
        base, valid = meta_ref[0], meta_ref[1]
        samples = count_ref[0]

        def block(i, carry):
            rows = pl.ds(pl.multiple_of(i * B, B), B)
            att = att_ref[rows, :]
            branch = mm(att, wop[...])
            stream_mid = stream_ref[rows, :] + scale_attn * branch
            unit, scale = norm_parts(stream_mid)
            ffn_in = (unit * gain_ffn).astype(bfloat)
            fin_s[rows, :] = ffn_in
            hidden = mm(ffn_in, wu[...])
            active, slope = gelu_both(hidden)
            active = active.astype(bfloat)
            act_s[rows, :] = active
            ffn_out = mm(active, wd[...])
            stream_low = (stream_mid + scale_ffn * ffn_out).astype(bfloat)
            low_s[rows, :] = stream_low
            predicted = mm(stream_low, wh[...])
            column = iota((B, O), 1)
            position = (base + i * B + iota((B, O), 0)) * SUB + column % SUB
            stem = column // (2 * SUB)
            weight = jnp.zeros((B, O), float32)
            for k in range(STEMS):
                weight = jnp.where(stem == k, meta_ref[2 + k].astype(float32), weight)
            weight = jnp.where(position < valid, weight, 0.0)
            error = predicted - target_ref[rows, :].astype(float32)
            root = jnp.sqrt(error * error + 1.0)
            misc_o[5:6, :O] += jnp.sum(weight * (root - 1.0), 0, keepdims=True)
            predicted_grad = (weight * error / root / samples).astype(bfloat)
            pg_s[rows, :] = predicted_grad
            end_grad = nt(predicted_grad, wh[...])
            misc_o[4:5, :] += jnp.sum(end_grad * ffn_out, 0, keepdims=True)
            ffn_grad = (scale_ffn * end_grad).astype(bfloat)
            fg_s[rows, :] = ffn_grad
            hidden_grad = (nt(ffn_grad, wd[...]) * slope).astype(bfloat)
            hg_s[rows, :] = hidden_grad
            mid_part, gain_grad = norm_back(unit, scale, gain_ffn, nt(hidden_grad, wu[...]))
            misc_o[2:3, :] += gain_grad
            mid_grad = end_grad + mid_part
            mid_o[rows, :] = mid_grad
            misc_o[3:4, :] += jnp.sum(mid_grad * branch, 0, keepdims=True)
            branch_grad = (scale_attn * mid_grad).astype(bfloat)
            bg_s[rows, :] = branch_grad
            att_grad = nt(branch_grad, wop[...]).astype(bfloat)
            for h in range(H):
                lanes = slice(h * LANES, (h + 1) * LANES)
                one = att_grad[:, lanes].astype(float32)
                delta = jnp.sum(one * att[:, lanes].astype(float32), -1, keepdims=True)
                do_o[rows, lanes] = with_column(one, delta, hd)
            return carry

        lax.fori_loop(0, T // B, block, 0)
        spare_grad = tn(att_ref[...], bg_s[...])
        for h in range(H):
            go_s[h * hd : (h + 1) * hd, :] = spare_grad[h * LANES : h * LANES + hd, :]
        gu_s[...] = tn(fin_s[...], hg_s[...])
        gd_s[...] = tn(act_s[...], fg_s[...])
        gh_s[...] = tn(low_s[...], pg_s[...])
        if z.direct:
            emit_blocks(
                z,
                meta_ref,
                keep_o,
                send_o,
                ((go_s, z.w, 1), (gu_s, z.w, 1), (gd_s, z.fw, 1), (gh_s, z.w, D // O)),
            )
        else:
            go_o[...] = go_s[...]
            gu_o[...] = gu_s[...]
            gd_o[...] = gd_s[...]
            gh_o[...] = gh_s[...]

    def whole(shape):
        return pl.BlockSpec(shape, lambda i: (0,) * len(shape))

    smem = pl.BlockSpec(memory_space=pltpu.SMEM)
    in_specs = [smem, smem, whole((T, D)), whole((T, W))]
    args = [meta, count, stream, att, target]
    in_specs.append(pl.BlockSpec((T, O), lambda i: (0, (z.frame + D) // O)))
    scratch = [
        pltpu.VMEM((W, D), bfloat),
        pltpu.VMEM((T, F), bfloat),
        pltpu.VMEM((T, F), bfloat),
        pltpu.VMEM((T, D), bfloat),
        pltpu.VMEM((T, D), bfloat),
        pltpu.VMEM((T, D), bfloat),
        pltpu.VMEM((T, O), bfloat),
        pltpu.VMEM((T, D), bfloat),
        pltpu.VMEM((D, D), float32),
        pltpu.VMEM((D, F), float32),
        pltpu.VMEM((F, D), float32),
        pltpu.VMEM((D, O), float32),
    ]
    shapes = [((T, W), bfloat), ((T, D), float32), ((8, D), float32)]
    if z.direct:
        args.append(weights[0])
        in_specs.append(pl.BlockSpec(memory_space=pl.ANY))
        scratch += [
            pltpu.VMEM((z.n, z.second_rows, D), bfloat),
            pltpu.VMEM((z.n, 16, D), bfloat),
            pltpu.VMEM((D, D), bfloat),
            pltpu.VMEM((D, F), bfloat),
            pltpu.VMEM((F, D), bfloat),
            pltpu.VMEM((D, O), bfloat),
            pltpu.SemaphoreType.DMA,
            pltpu.SemaphoreType.DMA,
        ]
        shapes += [
            ((z.n // 2, z.second_rows, D), float32),
            ((z.n // 2, z.second_rows, D), bfloat),
        ]
    else:
        for array in (weights[3], weights[4], weights[5], weights[6], weights[7]):
            args.append(array)
            in_specs.append(whole(array.shape))
        shapes += [((D, D), float32), ((D, F), float32), ((F, D), float32), ((D, O), float32)]
    return pl.pallas_call(
        kernel,
        grid=(1,),
        out_shape=[jax.ShapeDtypeStruct(s, d) for s, d in shapes],
        in_specs=in_specs,
        out_specs=[whole(s) for s, d in shapes],
        scratch_shapes=scratch,
        compiler_params=pltpu.CompilerParams(vmem_limit_bytes=VMEM_LIMIT),
        cost_estimate=pl.CostEstimate(flops=15_000_000_000, bytes_accessed=20_000_000, transcendentals=4_000_000),
        name="middle",
    )(*args)


def attend_back(z, q, k, v, do):
    T, K, W, D = z.tokens, z.keys, z.wide, z.D
    hd, QB = z.hd, z.query_block

    def kernel(q_ref, k_ref, v_ref, do_ref, dq_o, dkv_o):
        for b in range(T // QB):
            rows = slice(b * QB, (b + 1) * QB)
            q, do = q_ref[rows, :], do_ref[rows, :]
            probs = jnp.exp(nt(q, k_ref[...]))
            score_grad = (probs * nt(do, v_ref[...])).astype(bfloat)
            low = probs.astype(bfloat)
            dq_o[rows, :] = mm(score_grad, k_ref[...]).astype(bfloat)
            dk = tn(q, score_grad)
            dv = tn(do, low)
            if b == 0:
                dk_sum, dv_sum = dk, dv
            else:
                dk_sum, dv_sum = dk_sum + dk, dv_sum + dv
        dkv_o[0] = dk_sum[:hd, :].astype(bfloat)
        dkv_o[1] = dv_sum[:hd, :].astype(bfloat)

    def lanes(rows):
        return pl.BlockSpec((rows, LANES), lambda h: (0, h))

    return pl.pallas_call(
        kernel,
        grid=(H,),
        out_shape=[
            jax.ShapeDtypeStruct((T, W), bfloat),
            jax.ShapeDtypeStruct((2, D, K), bfloat),
        ],
        in_specs=[lanes(T), lanes(K), lanes(K), lanes(T)],
        out_specs=[lanes(T), pl.BlockSpec((2, hd, K), lambda h: (0, h, 0))],
        compiler_params=pltpu.CompilerParams(vmem_limit_bytes=VMEM_LIMIT),
        cost_estimate=pl.CostEstimate(flops=40_000_000_000, bytes_accessed=12_000_000, transcendentals=10_000_000),
        name="attend_back",
    )(q, k, v, do)


def back(z, meta, moved, spectral_all, halo, stream, slope, normed, sn, mid, dq, dkv, misc, weights):
    D, T, K, W, B, O = z.D, z.tokens, z.keys, z.wide, z.block, z.out
    frame, taps, hd = z.frame, z.taps, z.hd
    half = frame // 2

    def kernel(meta_ref, x_ref, sp_ref, stream_ref, slope_ref, normed_ref, sn_ref, mid_ref, dq_ref, dkv_ref, misc_ref, *refs):
        refs = list(refs)
        if z.parts > 1:
            before_ref, after_ref = refs[:2]
            refs = refs[2:]
        if z.direct:
            blob_ref = refs[0]
            keep_o, send_o = refs[1:3]
            refs = refs[3:]
        else:
            wq, wkv, gains_ref = refs[:3]
            gc_o, gq_o, gkv_o, misc_o = refs[3:7]
            refs = refs[7:]
        gc_s, gq_s, gkv_s, misc_s, cg_s, dqc_s, dkvt_s = refs[:7]
        refs = refs[7:]
        if z.direct:
            blob_s, wq, wkv, place_s, sem = refs
            w, cw = z.w, z.cw
            copy = pltpu.make_async_copy(blob_ref.at[:, cw : z.first_rows], blob_s, sem)
            copy.start()
            copy.wait()
            total = jnp.zeros((16, D), float32)
            for j in range(z.n):
                here = slice(j * w, (j + 1) * w)
                wq[here, :] = blob_s[j, 0:w, :]
                wkv[here, :D] = blob_s[j, w : 2 * w, :]
                wkv[here, D:] = blob_s[j, 2 * w : 3 * w, :]
                total = total + blob_s[j, 3 * w :, :].astype(float32)
        else:
            total = gains_ref[...]
        gain_query = total[0:1, :]
        misc_s[...] = misc_ref[...]
        spread = spread_matrix(D, hd)
        dqc_s[...] = nt(dq_ref[...], spread).astype(bfloat)
        dkvt_s[:, :D] = dkv_ref[0].T
        dkvt_s[:, D:] = dkv_ref[1].T
        gkv_s[...] = tn(sn_ref[...], dkvt_s[...])
        gq_s[...] = tn(normed_ref[...], dqc_s[...])

        def key_block(i, carry):
            rows = pl.ds(pl.multiple_of(i * B, B), B)
            unit, _ = norm_parts(sp_ref[rows, :].astype(float32))
            misc_s[1:2, :] += jnp.sum(nt(dkvt_s[rows, :], wkv[...]) * unit, 0, keepdims=True)
            return carry

        lax.fori_loop(0, K // B, key_block, 0)

        def token_block(i, carry):
            rows = pl.ds(pl.multiple_of(i * B, B), B)
            unit, scale = norm_parts(stream_ref[rows, :])
            part, gain_grad = norm_back(unit, scale, gain_query, nt(dqc_s[rows, :], wq[...]))
            misc_s[0:1, :] += gain_grad
            conv_grad = (mid_ref[rows, :] + part) * slope_ref[rows, :]
            cg_s[rows, :] = conv_grad.astype(bfloat).astype(float32)
            return carry

        lax.fori_loop(0, T // B, token_block, 0)
        conv_grad = cg_s[...]
        gc_s[half : half + frame, :] = tn(x_ref[...], conv_grad.astype(bfloat))
        row = iota((T, D), 0)
        later = jnp.where(row == T - 1, 0.0, pltpu.roll(conv_grad, T - 1, 0)).astype(bfloat)
        gc_s[:half, :] = tn(x_ref[:, half:], later)
        sooner = jnp.where(row == 0, 0.0, pltpu.roll(conv_grad, 1, 0)).astype(bfloat)
        gc_s[half + frame :, :] = tn(x_ref[:, :half], sooner)
        if z.parts > 1:
            top = jnp.where(iota((16, D), 0) == 0, conv_grad[0:16, :], 0.0).astype(bfloat)
            gc_s[:half, :] += tn(before_ref[...], top)
            tail = jnp.where(iota((16, D), 0) == 0, pltpu.roll(conv_grad[T - 16 :, :], 1, 0), 0.0)
            gc_s[half + frame :, :] += tn(after_ref[...], tail.astype(bfloat))
        if z.direct:
            for j in range(z.n):
                pick = jnp.where(iota((D, LANES), 0) == iota((D, LANES), 1) + j * z.w, 1.0, 0.0)
                pick = jnp.where(iota((D, LANES), 1) < z.w, pick, 0.0)
                chosen = lax.dot_general(
                    misc_s[...], pick, (((1,), (0,)), ((), ())),
                    precision=lax.Precision.HIGHEST, preferred_element_type=float32,
                )
                low_rows = jnp.where(iota((8, LANES), 0) == 5, misc_s[:, :LANES], chosen)
                place_s[j * 16 : (j + 1) * 16, :] = jnp.zeros((16, D), float32)
                place_s[j * 16 : j * 16 + 8, :LANES] = low_rows
            emit_blocks(
                z, meta_ref, keep_o, send_o,
                ((gc_s, z.cw, 1), (gq_s, z.w, 1), (gkv_s, z.w, 1), (place_s, 16, 1)),
            )
        else:
            gc_o[...] = gc_s[...]
            gq_o[...] = gq_s[...]
            gkv_o[...] = gkv_s[...]
            misc_o[...] = misc_s[...]

    def whole(shape):
        return pl.BlockSpec(shape, lambda i: (0,) * len(shape))

    args = [meta, moved, moved if z.parts == 1 else spectral_all]
    in_specs = [
        pl.BlockSpec(memory_space=pltpu.SMEM),
        whole((T, frame)),
        pl.BlockSpec((T, D), lambda i: (0, frame // D)) if z.parts == 1 else whole((K, D)),
    ]
    for array in (stream, slope, normed, sn, mid, dq, dkv, misc):
        args.append(array)
        in_specs.append(whole(array.shape))
    if z.parts > 1:
        args += list(halo)
        in_specs += [whole((16, D))] * 2
    scratch = [
        pltpu.VMEM((taps, D), float32),
        pltpu.VMEM((D, D), float32),
        pltpu.VMEM((D, 2 * D), float32),
        pltpu.VMEM((8, D), float32),
        pltpu.VMEM((T, D), float32),
        pltpu.VMEM((T, D), bfloat),
        pltpu.VMEM((K, 2 * D), bfloat),
    ]
    if z.direct:
        args.append(weights[0])
        in_specs.append(pl.BlockSpec(memory_space=pl.ANY))
        scratch += [
            pltpu.VMEM((z.n, z.first_rows - z.cw, D), bfloat),
            pltpu.VMEM((D, D), bfloat),
            pltpu.VMEM((D, 2 * D), bfloat),
            pltpu.VMEM((z.n * 16, D), float32),
            pltpu.SemaphoreType.DMA,
        ]
        shapes = [
            ((z.n // 2, z.first_rows, D), float32),
            ((z.n // 2, z.first_rows, D), bfloat),
        ]
    else:
        for array in (weights[1], weights[2], weights[7]):
            args.append(array)
            in_specs.append(whole(array.shape))
        shapes = [((taps, D), float32), ((D, D), float32), ((D, 2 * D), float32), ((8, D), float32)]
    return pl.pallas_call(
        kernel,
        grid=(1,),
        out_shape=[jax.ShapeDtypeStruct(s, d) for s, d in shapes],
        in_specs=in_specs,
        out_specs=[whole(s) for s, d in shapes],
        scratch_shapes=scratch,
        compiler_params=pltpu.CompilerParams(vmem_limit_bytes=VMEM_LIMIT),
        cost_estimate=pl.CostEstimate(flops=12_000_000_000, bytes_accessed=20_000_000, transcendentals=10_000),
        name="back",
    )(*args)


def pairs(count, mask):
    return [(i, i ^ mask) for i in range(count)]


def tree_sum(values):
    while len(values) > 1:
        values = [values[i] + values[i + 1] for i in range(0, len(values), 2)]
    return values[0]


def reduce_blocks(z, keep, send, planes):
    blocks = keep + lax.ppermute(send, "tm", pairs(z.n, 1)).astype(float32)
    mine = [blocks[0]]
    for m in range(1, z.n // 2):
        there = lax.ppermute(blocks[m].astype(bfloat), "tm", pairs(z.n, 2 * m))
        mine.append(there.astype(float32))
    low = tree_sum(mine).astype(bfloat)
    spread = [low] + [lax.ppermute(low, "seg", pairs(planes, m)) for m in range(1, planes)]
    return tree_sum([value.astype(float32) for value in spread])


def adam_update(master, first, second, grad, factor, rate):
    clipped = grad * factor
    first_new = beta_first * first + (1.0 - beta_first) * clipped
    second_new = beta_second * second + (1.0 - beta_second) * clipped * clipped
    moment_hat = first_new / (1.0 - beta_first**STEP)
    square_hat = second_new / (1.0 - beta_second**STEP)
    master_new = master - rate * (
        moment_hat / (jnp.sqrt(square_hat) + adam_epsilon) + weight_decay * master
    )
    return (master_new, first_new, second_new)


RATES = (
    learn_rate, learn_rate, learn_rate, fast_rate, learn_rate, learn_rate, learn_rate, fast_rate,
)


def update(z, squares, first_sum, second_sum, masters, firsts, seconds):
    D, O, w, cw = z.D, z.out, z.w, z.cw

    def kernel(*refs):
        sq_ref, a_ref, b_ref = refs[:3]
        ins = refs[3:27]
        loss_o, norm_o = refs[27:29]
        outs = refs[29:]
        norm = jnp.sqrt(jnp.sum(sq_ref[0:8, :], keepdims=True))
        loss_o[...] = jnp.sum(sq_ref[8:16, :], keepdims=True)
        norm_o[...] = norm
        factor = jnp.minimum(1.0, clip_limit / (norm + 1e-06))

        def rows_of(ref, start, count):
            return ref[start : start + count, :]

        base = w
        places = {
            0: [(a_ref, 0, cw, 0)],
            1: [(a_ref, cw, w, 0)],
            2: [(a_ref, cw + w + c * w, w, c * D) for c in range(2)],
            3: [(b_ref, 0, w, 0)],
            4: [(b_ref, base + c * w, w, c * D) for c in range(z.F // D)],
            5: [(b_ref, base + z.uw, z.fw, 0)],
        }

        def step(index, here, grad):
            values = adam_update(
                ins[index][here], ins[8 + index][here], ins[16 + index][here], grad, factor, RATES[index]
            )
            for kind, value in enumerate(values):
                outs[8 * kind + index][here] = value

        for index, pieces in places.items():
            for ref, start, count, lane in pieces:
                step(index, (slice(0, count), slice(lane, lane + D)), rows_of(ref, start, count))
        start = base + z.uw + z.fw
        for g in range(D // O):
            here = (slice(g * z.hw, (g + 1) * z.hw), slice(0, O))
            step(6, here, b_ref[start : start + z.hw, g * O : (g + 1) * O])
        gains = a_ref[cw + 3 * w : cw + 3 * w + 8, :][:5, :w]
        step(7, (slice(0, 5), slice(0, w)), gains)

    vmem = pl.BlockSpec(memory_space=pltpu.VMEM)
    outs = [jax.ShapeDtypeStruct((1, 1), float32)] * 2
    outs += [jax.ShapeDtypeStruct(m.shape, float32) for m in masters] * 3
    return pl.pallas_call(
        kernel,
        out_shape=outs,
        in_specs=[vmem] * 27,
        out_specs=[vmem] * 26,
        compiler_params=pltpu.CompilerParams(vmem_limit_bytes=VMEM_LIMIT),
        name="update",
    )(squares, first_sum, second_sum, *masters, *firsts, *seconds)


def on_device(*arguments):
    feats, spectral, target, valid_samples, stem_weights = arguments[:5]
    masters, firsts, seconds = arguments[5:13], arguments[13:21], arguments[21:29]
    n = lax.axis_size("tm")
    planes = lax.axis_size("seg")
    z = Sizes(n, feats, spectral, target, masters[0], masters[4])
    S, T, D = z.segments, z.tokens, z.D
    place = lax.axis_index("tm")
    portion, member = place // S, place % S

    if z.direct:
        blob = pack_weights(z, jnp.reshape(place, (1,)).astype(jnp.int32), *masters)
        weights = (lax.all_gather(blob, "tm", axis=0),)
    else:
        weights = [lax.all_gather(a.astype(bfloat), "tm", axis=0, tiled=True) for a in masters[:7]]
        gains = lax.all_gather(masters[7].astype(bfloat), "tm", axis=1, tiled=True)
        weights.append(jnp.pad(gains.astype(float32), ((0, 3), (0, 0))))
    groups = [[p * S + i for i in range(S)] for p in range(z.parts)]
    moved = lax.all_to_all(
        pack_tokens(z, feats, spectral, target),
        "tm", 0, 0, axis_index_groups=None if z.parts == 1 else groups, tiled=True,
    ).reshape(T, -1)
    spectral_all, halo = None, None
    if z.parts > 1:
        spectral_all = lax.all_gather(
            moved[:, z.frame : z.frame + D], "tm", axis=0, tiled=True,
            axis_index_groups=[[p * S + i for p in range(z.parts)] for i in range(S)],
        )
        tail = jnp.pad(moved[T - 1 :, z.frame // 2 : z.frame], ((0, 15), (0, 0)))
        lead = jnp.pad(moved[:1, : z.frame // 2], ((0, 15), (0, 0)))
        halo = (
            lax.ppermute(tail, "tm", [(i, i + S) for i in range(n - S)]),
            lax.ppermute(lead, "tm", [(i + S, i) for i in range(n - S)]),
        )
    local_count = jnp.sum(valid_samples)[None]
    if z.direct:
        counts = [local_count] + [lax.ppermute(local_count, "seg", pairs(planes, m)) for m in range(1, planes)]
        sample_count = tree_sum(counts).astype(float32)
    else:
        sample_count = lax.psum(local_count, "seg").astype(float32)
    meta = jnp.concatenate(
        [
            jnp.stack([portion * T, lax.dynamic_index_in_dim(valid_samples, member, keepdims=False)]),
            lax.dynamic_index_in_dim(stem_weights, member, keepdims=False),
            jnp.stack([place // 2, place % 2]),
        ]
    ).astype(jnp.int32)

    stream, slope, normed, sn, q, k, v, att = front(z, moved, spectral_all, halo, weights)
    second = middle(z, meta, sample_count, stream, att, moved, moved, weights)
    do, mid, misc = second[:3]
    dq, dkv = attend_back(z, q, k, v, do)
    first = back(z, meta, moved, spectral_all, halo, stream, slope, normed, sn, mid, dq, dkv, misc, weights)

    if z.direct:
        second_sum = reduce_blocks(z, second[3], second[4], planes)
        first_sum = reduce_blocks(z, first[0], first[1], planes)
        loss_row = z.first_rows - 16 + 5
        real = (iota(first_sum.shape, 0) != loss_row).astype(float32)
        masked = first_sum * real
        squares = jnp.sum((masked * masked).reshape(-1, 8, D), 0) + jnp.sum(
            (second_sum * second_sum).reshape(-1, 8, D), 0
        )
        squares = squares[:, :LANES] + squares[:, LANES : 2 * LANES] + squares[:, 2 * LANES :]
        loss = jnp.pad(first_sum[loss_row : loss_row + 1, :LANES] * (1.0 / n), ((0, 7), (0, 0)))
        both = jnp.concatenate([squares, loss], 0)
        both = both + lax.ppermute(both, "tm", pairs(n, 1))
        both = tree_sum([both] + [lax.ppermute(both, "tm", pairs(n, 2 * m)) for m in range(1, n // 2)])
        result = update(z, both, first_sum, second_sum, masters, firsts, seconds)
        return (result[0].reshape(()), sample_count.reshape(()), result[1].reshape(()), *result[2:])

    grads = (first[0], first[1], first[2], second[3], second[4], second[5], second[6])
    shards = [lax.psum_scatter(g, "tm", scatter_dimension=0, tiled=True) for g in grads]
    shards.append(lax.psum_scatter(first[3][:5], "tm", scatter_dimension=1, tiled=True))
    reduced = lax.psum(tuple(shards), "seg")
    loss_sum = lax.psum(jnp.sum(first[3][5]), ("seg", "tm"))
    squares = lax.psum(sum(jnp.sum(shard * shard) for shard in reduced), "tm")
    grad_norm = jnp.sqrt(squares)
    factor = jnp.minimum(1.0, clip_limit / (grad_norm + 1e-06))
    updated = [
        adam_update(m, f, s, g, factor, r)
        for m, f, s, g, r in zip(masters, firsts, seconds, reduced, RATES)
    ]
    return (
        loss_sum, sample_count.reshape(()), grad_norm,
        *[u[0] for u in updated], *[u[1] for u in updated], *[u[2] for u in updated],
    )


def solution(mesh):
    rows, columns = P("tm", None), P(None, "tm")
    leaves = (rows,) * 7 + (columns,)
    tokens = P("seg", "tm", None)
    return jax.shard_map(
        on_device,
        mesh=mesh,
        in_specs=(tokens, tokens, tokens, P("seg"), P("seg", None)) + leaves * 3,
        out_specs=(P(), P(), P()) + leaves * 3,
        check_vma=False,
    )
```

```python
import functools
import jax
import jax.numpy as jnp
from jax import lax
from jax.experimental import pallas as pl
from jax.experimental.pallas import tpu as pltpu
from jax.sharding import PartitionSpec as P

H = 8
STEMS = 4
SUB = 16
STEP = 10
LANES = 128

clip_limit = 0.001
beta_first = 0.9
beta_second = 0.999
learn_rate = 0.03
fast_rate = 0.5
weight_decay = 0.05
adam_epsilon = 1e-08
norm_epsilon = 1e-05

bfloat = jnp.bfloat16
float32 = jnp.float32
VMEM_LIMIT = 60 * 1024 * 1024


def mm(left, right):
    return lax.dot_general(left, right, (((1,), (0,)), ((), ())), preferred_element_type=float32)


def nt(left, right):
    return lax.dot_general(left, right, (((1,), (1,)), ((), ())), preferred_element_type=float32)


def tn(left, right):
    return lax.dot_general(left, right, (((0,), (0,)), ((), ())), preferred_element_type=float32)


def iota(shape, dim):
    return lax.broadcasted_iota(jnp.int32, shape, dim)


def norm_parts(values):
    centred = values - jnp.mean(values, -1, keepdims=True)
    scale = lax.rsqrt(jnp.mean(centred * centred, -1, keepdims=True) + norm_epsilon)
    return centred * scale, scale


def norm_back(unit, scale, gain, upstream):
    inner = upstream * gain
    value_grad = scale * (
        inner
        - jnp.mean(inner, -1, keepdims=True)
        - unit * jnp.mean(inner * unit, -1, keepdims=True)
    )
    return value_grad, jnp.sum(upstream * unit, 0, keepdims=True)


def gelu_both(values):
    upper = 0.5 * (1.0 + lax.erf(values * 0.7071067811865476))
    density = jnp.exp(-0.5 * values * values) * 0.3989422804014327
    return values * upper, upper + values * density


def spread_matrix(width, head_size):
    shape = (width, width // head_size * LANES)
    lane = iota(shape, 1)
    inside = lane % LANES
    source = (lane // LANES) * head_size + inside
    hit = jnp.logical_and(iota(shape, 0) == source, inside < head_size)
    return jnp.where(hit, 1.0, 0.0).astype(bfloat)


def with_column(block, column, head_size):
    lane = iota(block.shape, 1)
    high = column.astype(bfloat).astype(float32)
    rest = column - high
    middle = rest.astype(bfloat).astype(float32)
    low = rest - middle
    pieces = jnp.where(lane == head_size, high, jnp.where(lane == head_size + 1, middle, low))
    spare = jnp.logical_and(lane >= head_size, lane < head_size + 3)
    return jnp.where(spare, pieces, block.astype(float32)).astype(bfloat)


class Sizes:
    def __init__(self, n, planes, feats, spectral, target, conv_weight, up_weight):
        self.n = n
        self.planes = planes
        self.segments = feats.shape[0]
        self.parts = n // self.segments
        self.channels = feats.shape[2]
        self.tokens_dev = spectral.shape[1]
        self.D = spectral.shape[2]
        self.taps = conv_weight.shape[0] * n
        self.frame = self.taps // 2
        self.F = up_weight.shape[1]
        self.out = target.shape[2]
        self.tokens = self.segments * self.tokens_dev
        self.keys = self.tokens * self.parts
        self.hd = self.D // H
        self.wide = H * LANES
        self.w = self.D // n
        self.cw = self.taps // n
        self.uw = self.w * (self.F // self.D)
        self.fw = self.F // n
        self.hw = self.w * self.out // self.D
        self.first_rows = self.cw + 3 * self.w + 16
        self.second_rows = self.w + self.uw + self.fw + self.hw
        step = 16 * planes
        self.first_grads = -(-self.first_rows // step) * step
        self.second_grads = -(-self.second_rows // step) * step
        self.direct = self.parts == 1 and self.w % 16 == 0 and self.hw % 16 == 0 and self.hw > 0
        self.block = 256
        self.query_block = 1024 if self.keys <= 1024 else 256


def smem():
    return pl.BlockSpec(memory_space=pltpu.SMEM)


def anywhere():
    return pl.BlockSpec(memory_space=pl.ANY)


def whole(shape):
    return pl.BlockSpec(shape, lambda i: (0,) * len(shape))


def pack_weights(z, tm_place, masters):
    D, w, O, cw = z.D, z.w, z.out, z.cw

    def kernel(place_ref, conv_r, query_r, keyval_r, out_r, up_r, down_r, head_r, gains_r, first_o, second_o):
        first_o[:cw, :] = conv_r[...].astype(bfloat)
        first_o[cw : cw + w, :] = query_r[...].astype(bfloat)
        first_o[cw + w : cw + 2 * w, :] = keyval_r[:, :D].astype(bfloat)
        first_o[cw + 2 * w : cw + 3 * w, :] = keyval_r[:, D:].astype(bfloat)
        start = place_ref[0] * w
        shift = jnp.where(iota((w, D), 1) == iota((w, D), 0) + start, 1.0, 0.0).astype(bfloat)
        placed = mm(gains_r[...].astype(bfloat), shift)
        padded = jnp.concatenate([placed, jnp.zeros((16 - placed.shape[0], D), float32)], 0)
        first_o[cw + 3 * w :, :] = padded.astype(bfloat)
        second_o[:w, :] = out_r[...].astype(bfloat)
        for c in range(z.F // D):
            second_o[w + c * w : 2 * w + c * w, :] = up_r[:, c * D : (c + 1) * D].astype(bfloat)
        row = w + z.uw
        second_o[row : row + z.fw, :] = down_r[...].astype(bfloat)
        row += z.fw
        for g in range(D // O):
            here = head_r[g * z.hw : (g + 1) * z.hw, :]
            second_o[row : row + z.hw, g * O : (g + 1) * O] = here.astype(bfloat)

    vmem = pl.BlockSpec(memory_space=pltpu.VMEM)
    return pl.pallas_call(
        kernel,
        out_shape=[
            jax.ShapeDtypeStruct((z.first_rows, D), bfloat),
            jax.ShapeDtypeStruct((z.second_rows, D), bfloat),
        ],
        in_specs=[smem()] + [vmem] * 8,
        out_specs=[vmem] * 2,
        name="pack_weights",
    )(tm_place, *masters)


def pack_tokens(z, feats, spectral, target):
    rows, D, C = z.tokens_dev, z.D, z.channels

    def kernel(f_ref, s_ref, t_ref, o_ref, buffer, in_sem, out_sem):
        arriving, leaving = [], []
        for i in range(z.segments):
            arriving.append(
                [
                    pltpu.make_async_copy(f_ref.at[i], buffer.at[i, rows:, :], in_sem.at[i, 0]),
                    pltpu.make_async_copy(s_ref.at[i], buffer.at[i, :rows, :D], in_sem.at[i, 1]),
                    pltpu.make_async_copy(t_ref.at[i], buffer.at[i, :rows, D:], in_sem.at[i, 2]),
                ]
            )
            leaving.append(pltpu.make_async_copy(buffer.at[i], o_ref.at[i], out_sem.at[i]))
            for copy in arriving[i]:
                copy.start()
        for i in range(z.segments):
            for copy in arriving[i]:
                copy.wait()
            leaving[i].start()
        for copy in leaving:
            copy.wait()

    shape = (z.segments, rows + C, 4 * rows)
    return pl.pallas_call(
        kernel,
        out_shape=jax.ShapeDtypeStruct(shape, bfloat),
        in_specs=[anywhere()] * 3,
        out_specs=anywhere(),
        scratch_shapes=[
            pltpu.VMEM(shape, bfloat),
            pltpu.SemaphoreType.DMA((z.segments, 3)),
            pltpu.SemaphoreType.DMA((z.segments,)),
        ],
        compiler_params=pltpu.CompilerParams(vmem_limit_bytes=VMEM_LIMIT),
        name="pack_tokens",
    )(feats, spectral, target)


def spectral_copies(z, source, home, sem, first):
    if z.parts > 1:
        return [pltpu.make_async_copy(source, home, sem.at[first])]
    rows = z.tokens_dev
    return [
        pltpu.make_async_copy(source.at[i, :rows, : z.D], home.at[i * rows : (i + 1) * rows, :], sem.at[first + i])
        for i in range(z.segments)
    ]


def front(z, moved, spectral, halo, weights):
    D, T, K, W, B = z.D, z.tokens, z.keys, z.wide, z.block
    frame, taps, hd = z.frame, z.taps, z.hd
    half = frame // 2
    QB = z.query_block
    count = z.tokens_dev
    CB = 2 * LANES
    extra = 2 if z.parts > 1 else 0
    n_weights = 1 if z.direct else 4

    def kernel(*refs):
        refs = list(refs)
        frames_ref, sp_ref = refs[:2]
        before_after = refs[2 : 2 + extra]
        weight_refs = refs[2 + extra : 2 + extra + n_weights]
        refs = refs[2 + extra + n_weights :]
        (x_o, stream_o, slope_o, normed_o, sn_o, q_o, k_o, v_o, att_o) = refs[:9]
        (frames_s, sp_s, x_s, stream_s, slope_s, normed_s, sn_s) = refs[9:16]
        (conv_s, wq_s, wk_s, wv_s, q_s, k_s, v_s, in_sem, out_sem) = refs[16:25]
        refs = refs[25:]
        h = pl.program_id(0)
        outgoing = [
            pltpu.make_async_copy(src, dst, out_sem.at[i])
            for i, (src, dst) in enumerate(
                ((x_s, x_o), (stream_s, stream_o), (slope_s, slope_o), (normed_s, normed_o), (sn_s, sn_o))
            )
        ]

        @pl.when(h == 0)
        def _():
            frames_copy = pltpu.make_async_copy(frames_ref.at[:, count:, :], frames_s, in_sem.at[0])
            spectral_in = spectral_copies(z, sp_ref, sp_s, in_sem, 2)
            if z.direct:
                blob_s, wc, wqkv = refs
                blob_copy = pltpu.make_async_copy(weight_refs[0], blob_s, in_sem.at[1])
                blob_copy.start()
            for copy in spectral_in:
                copy.start()
            frames_copy.start()
            if z.direct:
                blob_copy.wait()
                w, cw = z.w, z.cw
                total = jnp.zeros((16, D), float32)
                for j in range(z.n):
                    wc[j * cw : (j + 1) * cw, :] = blob_s[j, 0:cw, :]
                    for c in range(3):
                        first = cw + c * w
                        wqkv[j * w : (j + 1) * w, c * D : (c + 1) * D] = blob_s[j, first : first + w, :]
                    total = total + blob_s[j, cw + 3 * w : cw + 3 * w + 16, :].astype(float32)
                gain_query, gain_keys = total[0:1, :], total[1:2, :]
                parts_w = [wqkv[:, c * D : (c + 1) * D] for c in range(3)]
            else:
                wc, wq, wkv, gains_ref = weight_refs
                gain_query, gain_keys = gains_ref[0:1, :], gains_ref[1:2, :]
                parts_w = [wq[...], wkv[:, :D], wkv[:, D:]]
            spread = spread_matrix(D, hd)
            for target_s, part in zip((wq_s, wk_s, wv_s), parts_w):
                target_s[...] = mm(part, spread).astype(bfloat)
            for copy in spectral_in:
                copy.wait()
            for i in range(K // B):
                rows = slice(i * B, (i + 1) * B)
                unit, _ = norm_parts(sp_s[rows, :].astype(float32))
                sn_s[rows, :] = (unit * gain_keys).astype(bfloat)
            outgoing[4].start()
            inside = iota((K, CB), 1) % LANES
            spare = jnp.logical_and(inside >= hd, inside < hd + 3)
            for home, part in ((k_s, wk_s), (v_s, wv_s)):
                for c in range(0, W, CB):
                    product = mm(sn_s[...], part[:, c : c + CB])
                    home[:, c : c + CB] = jnp.where(spare, -1.0, product).astype(bfloat)
            frames_copy.wait()
            shape = (4 * count, 4 * count)
            row, column = iota(shape, 0), iota(shape, 1)
            order = jnp.where(column == (row % count) * 4 + row // count, 1.0, 0.0).astype(bfloat)
            for i in range(z.segments):
                taps_rows = nt(order, frames_s[i])
                x_s[i * count : (i + 1) * count, :] = jnp.concatenate(
                    [taps_rows[j * count : (j + 1) * count, :] for j in range(4)], 1
                ).astype(bfloat)
            outgoing[0].start()
            conv_s[...] = mm(x_s[...], wc[half : half + frame, :])
            row = iota((T, D), 0)
            older = pltpu.roll(mm(x_s[:, half:], wc[:half, :]), 1, 0)
            first_row, last_row = 0.0, 0.0
            if z.parts > 1:
                first_row = mm(before_after[0][...], wc[:half, :])[0:1, :]
                last_row = mm(before_after[1][...], wc[half + frame :, :])[0:1, :]
            conv_s[...] += jnp.where(row == 0, first_row, older)
            newer = pltpu.roll(mm(x_s[:, :half], wc[half + frame :, :]), T - 1, 0)
            conv_s[...] += jnp.where(row == T - 1, last_row, newer)

            for i in range(T // B):
                rows = slice(i * B, (i + 1) * B)
                stream, slope = gelu_both(conv_s[rows, :])
                stream_s[rows, :] = stream
                slope_s[rows, :] = slope
                unit, _ = norm_parts(stream)
                normed = (unit * gain_query).astype(bfloat)
                normed_s[rows, :] = normed
            for c in range(0, W, CB):
                q_s[:, c : c + CB] = mm(normed_s[...], wq_s[:, c : c + CB]).astype(bfloat)
            for copy in outgoing[1:4]:
                copy.start()

        lanes = pl.ds(pl.multiple_of(h * LANES, LANES), LANES)
        k_o[...] = k_s[:, lanes]
        v_o[...] = v_s[:, lanes]
        for b in range(T // QB):
            rows = slice(b * QB, (b + 1) * QB)
            q = q_s[rows, lanes]

            def finish(grown, top, rows=rows, q=q):
                mass = jnp.sum(grown, 0, keepdims=True)
                probs = (grown * (1.0 / mass)).astype(bfloat)
                total = top + jnp.log(mass)
                result = tn(v_o[...], probs)
                high = total.astype(bfloat).astype(float32)
                rest = total - high
                mid = rest.astype(bfloat).astype(float32)
                sub = iota((LANES, QB), 0)
                spare = jnp.where(sub == hd, high, jnp.where(sub == hd + 1, mid, rest - mid))
                spare = jnp.where(sub < hd + 3, spare, 0.0)
                both = jnp.where(sub < hd, result, spare).T
                att_o[rows, :] = both.astype(bfloat)
                lane = iota((QB, LANES), 1)
                q_o[rows, :] = jnp.where(lane < hd, q.astype(float32), both).astype(bfloat)
                return mass

            mass = finish(jnp.exp(nt(k_o[...], q)), 0.0)
            safe = jnp.logical_and(jnp.min(mass) > 1e-20, jnp.max(mass) < 1e30)

            @pl.when(jnp.logical_not(safe))
            def _(q=q, finish=finish):
                scores = nt(k_o[...], q)
                top = jnp.max(scores, 0, keepdims=True)
                finish(jnp.exp(scores - top), top)

        @pl.when(h == H - 1)
        def _():
            for copy in outgoing:
                copy.wait()

    def lanes_of(rows):
        return pl.BlockSpec((rows, LANES), lambda h: (0, h))

    in_specs = [anywhere(), anywhere()]
    args = [moved, moved if z.parts == 1 else spectral]
    if z.parts > 1:
        args += list(halo)
        in_specs += [whole((16, D))] * 2
    scratch = [
        pltpu.VMEM((z.segments, z.channels, 4 * count), bfloat),
        pltpu.VMEM((K, D), bfloat),
        pltpu.VMEM((T, frame), bfloat),
        pltpu.VMEM((T, D), float32),
        pltpu.VMEM((T, D), float32),
        pltpu.VMEM((T, D), bfloat),
        pltpu.VMEM((K, D), bfloat),
        pltpu.VMEM((T, D), float32),
        pltpu.VMEM((D, W), bfloat),
        pltpu.VMEM((D, W), bfloat),
        pltpu.VMEM((D, W), bfloat),
        pltpu.VMEM((T, W), bfloat),
        pltpu.VMEM((K, W), bfloat),
        pltpu.VMEM((K, W), bfloat),
        pltpu.SemaphoreType.DMA((2 + z.segments,)),
        pltpu.SemaphoreType.DMA((5,)),
    ]
    if z.direct:
        args.append(weights[0])
        in_specs.append(anywhere())
        scratch += [
            pltpu.VMEM((z.n, z.first_rows, D), bfloat),
            pltpu.VMEM((taps, D), bfloat),
            pltpu.VMEM((D, 3 * D), bfloat),
        ]
    else:
        for array in (weights[0], weights[1], weights[2], weights[7]):
            args.append(array)
            in_specs.append(whole(array.shape))
    shapes = [
        ((T, frame), bfloat),
        ((T, D), float32),
        ((T, D), float32),
        ((T, D), bfloat),
        ((K, D), bfloat),
        ((T, W), bfloat),
        ((K, W), bfloat),
        ((K, W), bfloat),
        ((T, W), bfloat),
    ]
    return pl.pallas_call(
        kernel,
        grid=(H,),
        out_shape=[jax.ShapeDtypeStruct(s, d) for s, d in shapes],
        in_specs=in_specs,
        out_specs=[anywhere()] * 5 + [lanes_of(T), lanes_of(K), lanes_of(K), lanes_of(T)],
        scratch_shapes=scratch,
        compiler_params=pltpu.CompilerParams(vmem_limit_bytes=VMEM_LIMIT),
        cost_estimate=pl.CostEstimate(flops=20_000_000_000, bytes_accessed=20_000_000, transcendentals=10_000_000),
        name="front",
    )(*args)


def emit_blocks(z, meta_ref, keep_o, send_o, sources):
    chip, core, plane = meta_ref[6], meta_ref[7], meta_ref[8]
    quarter = keep_o.shape[2]

    def write(out, m, row, here, lanes):
        first = 0
        while first < here.shape[0]:
            part, inside = divmod(row + first, quarter)
            size = min(here.shape[0] - first, quarter - inside)
            out[m, part ^ plane, inside : inside + size, lanes] = here[first : first + size].astype(out.dtype)
            first += size

    for m in range(z.n // 2):
        owner = (chip ^ m) * 2
        for out, place in ((keep_o, owner + core), (send_o, owner + 1 - core)):
            row = 0
            for ref, rows, pieces in sources:
                width = ref.shape[-1]
                if width >= z.D:
                    start = pl.multiple_of(place * rows, 16)
                    for lane in range(0, width, z.D):
                        write(out, m, row, ref[pl.ds(start, rows), lane : lane + z.D], slice(0, z.D))
                        row += rows
                else:
                    size = rows // pieces
                    for g in range(pieces):
                        start = pl.multiple_of(place * rows + g * size, 16)
                        write(out, m, row, ref[pl.ds(start, size), :], slice(g * width, (g + 1) * width))
                    row += size
            if row < quarter * z.planes:
                rest = quarter * z.planes - row
                write(out, m, row, jnp.zeros((rest, z.D), float32), slice(0, z.D))


def block_shapes(z, rows):
    shape = (z.n // 2, z.planes, rows // z.planes, z.D)
    return [(shape, float32), (shape, bfloat)]


def middle(z, meta, count, stream, att, target, weights):
    D, T, W, F, O = z.D, z.tokens, z.wide, z.F, z.out
    B = T
    hd = z.hd

    def kernel(meta_ref, count_ref, stream_ref, att_ref, target_ref, *refs):
        refs = list(refs)
        if z.direct:
            first_ref, second_ref = refs[:2]
            do_out, mid_out, misc_o, keep_o, send_o = refs[2:7]
            refs = refs[7:]
        else:
            wo, wu, wd, wh, gains_ref = refs[:5]
            do_out, mid_out, misc_o, go_s, gu_s, gd_s, gh_s = refs[5:12]
            refs = refs[12:]
        wop, att_s, stream_s, do_o, mid_o, act_s, hg_s, fin_s, fg_s, low_s, pg_s, bg_s, sem = refs[:13]
        refs = refs[13:]
        if z.direct:
            go_s, gu_s, gd_s, gh_s, blob_s, gain_s, wo, wu, wd, wh = refs

        att_copy = pltpu.make_async_copy(att_ref, att_s, sem.at[0])
        stream_copy = pltpu.make_async_copy(stream_ref, stream_s, sem.at[1])
        if z.direct:
            w, uw, fw, hw = z.w, z.uw, z.fw, z.hw
            ends = (0, w, w + uw, w + uw + fw, z.second_rows)
            pieces = [
                pltpu.make_async_copy(second_ref.at[:, p:q], blob_s.at[:, p:q], sem.at[2 + c])
                for c, (p, q) in enumerate(zip(ends[:-1], ends[1:]))
            ]
            gain_copy = pltpu.make_async_copy(first_ref.at[:, z.first_rows - 16 :], gain_s, sem.at[6])
            pieces[0].start()
            gain_copy.start()
        att_copy.start()
        stream_copy.start()
        if z.direct:
            for piece in pieces[1:]:
                piece.start()
            pieces[0].wait()
            gain_copy.wait()
            total = jnp.zeros((16, D), float32)
            for j in range(z.n):
                wo[j * w : (j + 1) * w, :] = blob_s[j, 0:w, :]
                total = total + gain_s[j].astype(float32)
        else:
            total = gains_ref[...]
        wop[...] = tn(spread_matrix(D, hd), wo[...]).astype(bfloat)
        misc_o[...] = jnp.zeros_like(misc_o)
        gain_ffn, scale_attn, scale_ffn = total[2:3, :], total[3:4, :], total[4:5, :]
        base, valid = meta_ref[0], meta_ref[1]
        samples = count_ref[0]
        rows = slice(0, B)
        att_copy.wait()
        att = att_s
        branch = mm(att[...], wop[...])
        stream_copy.wait()
        stream_mid = stream_s[...] + scale_attn * branch
        unit, scale = norm_parts(stream_mid)
        ffn_in = (unit * gain_ffn).astype(bfloat)
        fin_s[rows, :] = ffn_in
        if z.direct:
            pieces[1].wait()
            for j in range(z.n):
                for c in range(F // D):
                    first = w + c * w
                    wu[j * w : (j + 1) * w, c * D : (c + 1) * D] = blob_s[j, first : first + w, :]
        hidden = mm(ffn_in, wu[...])
        active, slope = gelu_both(hidden)
        active = active.astype(bfloat)
        act_s[rows, :] = active
        if z.direct:
            pieces[2].wait()
            pieces[3].wait()
            for j in range(z.n):
                wd[j * fw : (j + 1) * fw, :] = blob_s[j, w + uw : w + uw + fw, :]
                for g in range(D // O):
                    start = j * w + g * hw
                    wh[start : start + hw, :] = blob_s[j, w + uw + fw :, g * O : (g + 1) * O]
        ffn_out = mm(active, wd[...])
        stream_low = (stream_mid + scale_ffn * ffn_out).astype(bfloat)
        low_s[rows, :] = stream_low
        predicted = mm(stream_low, wh[...])
        column = iota((B, O), 1)
        position = (base + iota((B, O), 0)) * SUB + column % SUB
        stem = column // (2 * SUB)
        weight = jnp.zeros((B, O), float32)
        for k in range(STEMS):
            weight = jnp.where(stem == k, meta_ref[2 + k].astype(float32), weight)
        weight = jnp.where(position < valid, weight, 0.0)
        error = predicted - target_ref[...].reshape(B, O).astype(float32)
        root = jnp.sqrt(error * error + 1.0)
        misc_o[5:6, :O] += jnp.sum(weight * (root - 1.0), 0, keepdims=True)
        predicted_grad = (weight * error / root / samples).astype(bfloat)
        pg_s[rows, :] = predicted_grad
        end_grad = nt(predicted_grad, wh[...])
        misc_o[4:5, :] += jnp.sum(end_grad * ffn_out, 0, keepdims=True)
        ffn_grad = (scale_ffn * end_grad).astype(bfloat)
        fg_s[rows, :] = ffn_grad
        hidden_grad = (nt(ffn_grad, wd[...]) * slope).astype(bfloat)
        hg_s[rows, :] = hidden_grad
        mid_part, gain_grad = norm_back(unit, scale, gain_ffn, nt(hidden_grad, wu[...]))
        misc_o[2:3, :] += gain_grad
        mid_grad = end_grad + mid_part
        mid_o[...] = mid_grad
        misc_o[3:4, :] += jnp.sum(mid_grad * branch, 0, keepdims=True)
        branch_grad = (scale_attn * mid_grad).astype(bfloat)
        bg_s[rows, :] = branch_grad
        att_grad = nt(branch_grad, wop[...]).astype(bfloat)
        for h in range(H):
            lanes = slice(h * LANES, (h + 1) * LANES)
            one = att_grad[:, lanes].astype(float32)
            delta = jnp.sum(one * att[:, lanes].astype(float32), -1, keepdims=True)
            do_o[:, lanes] = with_column(one, delta, hd)

        outgoing = [
            pltpu.make_async_copy(do_o, do_out, sem.at[7]),
            pltpu.make_async_copy(mid_o, mid_out, sem.at[8]),
        ]
        for copy in outgoing:
            copy.start()
        spare_grad = tn(att_s[...], bg_s[...])
        for h in range(H):
            go_s[h * hd : (h + 1) * hd, :] = spare_grad[h * LANES : h * LANES + hd, :]
        gu_s[...] = tn(fin_s[...], hg_s[...])
        gd_s[...] = tn(act_s[...], fg_s[...])
        gh_s[...] = tn(low_s[...], pg_s[...])
        if z.direct:
            emit_blocks(
                z,
                meta_ref,
                keep_o,
                send_o,
                ((go_s, z.w, 1), (gu_s, z.w, 1), (gd_s, z.fw, 1), (gh_s, z.w, D // O)),
            )
        for copy in outgoing:
            copy.wait()

    if z.parts == 1:
        target_spec = pl.BlockSpec((z.segments, z.tokens_dev, O), lambda i: (0, 0, D // O))
    else:
        target_spec = whole(target.shape)
    in_specs = [smem(), smem(), anywhere(), anywhere(), target_spec]
    args = [meta, count, stream, att, target]
    scratch = [
        pltpu.VMEM((W, D), bfloat),
        pltpu.VMEM((T, W), bfloat),
        pltpu.VMEM((T, D), float32),
        pltpu.VMEM((T, W), bfloat),
        pltpu.VMEM((T, D), float32),
        pltpu.VMEM((T, F), bfloat),
        pltpu.VMEM((T, F), bfloat),
        pltpu.VMEM((T, D), bfloat),
        pltpu.VMEM((T, D), bfloat),
        pltpu.VMEM((T, D), bfloat),
        pltpu.VMEM((T, O), bfloat),
        pltpu.VMEM((T, D), bfloat),
        pltpu.SemaphoreType.DMA((9,)),
    ]
    shapes = [((T, W), bfloat), ((T, D), float32), ((8, D), float32)]
    grads = [((D, D), float32), ((D, F), float32), ((F, D), float32), ((D, O), float32)]
    if z.direct:
        args += list(weights)
        in_specs += [anywhere()] * 2
        scratch += [pltpu.VMEM(s, d) for s, d in grads] + [
            pltpu.VMEM((z.n, z.second_rows, D), bfloat),
            pltpu.VMEM((z.n, 16, D), bfloat),
            pltpu.VMEM((D, D), bfloat),
            pltpu.VMEM((D, F), bfloat),
            pltpu.VMEM((F, D), bfloat),
            pltpu.VMEM((D, O), bfloat),
        ]
        shapes += block_shapes(z, z.second_grads)
    else:
        for array in weights[3:]:
            args.append(array)
            in_specs.append(whole(array.shape))
        shapes += grads
    return pl.pallas_call(
        kernel,
        grid=(1,),
        out_shape=[jax.ShapeDtypeStruct(s, d) for s, d in shapes],
        in_specs=in_specs,
        out_specs=[anywhere(), anywhere()] + [whole(s) for s, d in shapes[2:]],
        scratch_shapes=scratch,
        compiler_params=pltpu.CompilerParams(vmem_limit_bytes=VMEM_LIMIT),
        cost_estimate=pl.CostEstimate(flops=20_000_000_000, bytes_accessed=20_000_000, transcendentals=4_000_000),
        name="middle",
    )(*args)


def head_back(z, q_ref, k_ref, v_ref, do_ref, put_query):
    T, hd = z.tokens, z.hd
    QB = 256 if z.keys <= 1024 else 128
    for b in range(T // QB):
        rows = slice(b * QB, (b + 1) * QB)
        q, do = q_ref[rows, :], do_ref[rows, :]
        probs = jnp.exp(nt(q, k_ref[...]))
        score_grad = (probs * nt(do, v_ref[...])).astype(bfloat)
        low = probs.astype(bfloat)
        put_query(rows, mm(score_grad, k_ref[...]).astype(bfloat))
        dk, dv = tn(q, score_grad), tn(do, low)
        if b == 0:
            dk_sum, dv_sum = dk, dv
        else:
            dk_sum, dv_sum = dk_sum + dk, dv_sum + dv
    return dk_sum[:hd, :].astype(bfloat), dv_sum[:hd, :].astype(bfloat)


def attend_back(z, q, k, v, do, heads):
    T, K, W, D = z.tokens, z.keys, z.wide, z.D
    hd = z.hd

    def kernel(q_ref, k_ref, v_ref, do_ref, dq_o, dkv_o):
        def put_query(rows, value):
            dq_o[rows, :] = value

        dkv_o[0], dkv_o[1] = head_back(z, q_ref, k_ref, v_ref, do_ref, put_query)

    def lanes(rows):
        return pl.BlockSpec((rows, LANES), lambda h: (0, h))

    return pl.pallas_call(
        kernel,
        grid=(heads,),
        out_shape=[
            jax.ShapeDtypeStruct((T, heads * LANES), bfloat),
            jax.ShapeDtypeStruct((2, heads * hd, K), bfloat),
        ],
        in_specs=[lanes(T), lanes(K), lanes(K), lanes(T)],
        out_specs=[lanes(T), pl.BlockSpec((2, hd, K), lambda h: (0, h, 0))],
        compiler_params=pltpu.CompilerParams(vmem_limit_bytes=VMEM_LIMIT),
        cost_estimate=pl.CostEstimate(
            flops=heads * 4_000_000_000, bytes_accessed=12_000_000, transcendentals=heads * 1_000_000
        ),
        name="attend_back",
    )(q, k, v, do)


def back(z, done, meta, q, k, v, do, dq, dkv, x, spectral, halo, stream, slope, normed, sn, mid, misc, weights):
    D, T, K, W, B, O = z.D, z.tokens, z.keys, z.wide, z.block, z.out
    frame, taps, hd = z.frame, z.taps, z.hd
    half = frame // 2
    steps = H - done
    extra = 2 if z.parts > 1 else 0
    n_weights = 1 if z.direct else 3
    n_out = 2 if z.direct else 4

    def kernel(meta_ref, q_ref, k_ref, v_ref, do_ref, misc_ref, *refs):
        refs = list(refs)
        before_after = refs[:extra]
        remote = refs[extra : extra + 9]
        refs = refs[extra + 9 :]
        weight_refs, refs = refs[:n_weights], refs[n_weights:]
        outs, refs = refs[:n_out], refs[n_out:]
        (dq_s, dkv_s, x_ref, sp_ref, stream_ref, slope_ref, normed_ref, sn_ref, mid_ref) = refs[:9]
        refs = refs[9:]
        cg_s, dn_s, dqc_s, dkvt_s, sem = refs[:5]
        refs = refs[5:]
        if z.direct:
            gc_s, gq_s, gkv_s, misc_s, place_s, blob_s, wq, wkv = refs
        else:
            gc_s, gq_s, gkv_s, misc_s = outs
            wq, wkv, gains_ref = weight_refs
        i = pl.program_id(0)
        old = done * LANES
        homes = [dq_s.at[:, :old], dkv_s.at[:, : done * hd]] + [
            x_ref, sp_ref, stream_ref, slope_ref, normed_ref, sn_ref, mid_ref
        ]
        copies = [
            pltpu.make_async_copy(a, b, sem.at[c])
            for c, (a, b) in enumerate(zip(remote, homes))
            if c != 3
        ]
        copies += spectral_copies(z, remote[3], sp_ref, sem, 10)
        if z.direct:
            copies.append(
                pltpu.make_async_copy(weight_refs[0].at[:, z.cw : z.first_rows], blob_s, sem.at[9])
            )

        @pl.when(i == 0)
        def _():
            for copy in copies:
                copy.start()

        lanes = pl.ds(pl.multiple_of((i + done) * LANES, LANES), LANES)

        def put_query(rows, value):
            dq_s[rows, lanes] = value

        dk, dv = head_back(z, q_ref, k_ref, v_ref, do_ref, put_query)
        here = pl.ds(pl.multiple_of((i + done) * hd, 16), hd)
        dkv_s[0, here, :] = dk
        dkv_s[1, here, :] = dv

        @pl.when(i == steps - 1)
        def _():
            for copy in copies:
                copy.wait()
            if z.direct:
                w = z.w
                total = jnp.zeros((16, D), float32)
                for j in range(z.n):
                    here = slice(j * w, (j + 1) * w)
                    wq[here, :] = blob_s[j, 0:w, :]
                    wkv[here, :D] = blob_s[j, w : 2 * w, :]
                    wkv[here, D:] = blob_s[j, 2 * w : 3 * w, :]
                    total = total + blob_s[j, 3 * w :, :].astype(float32)
            else:
                total = gains_ref[...]
            gain_query = total[0:1, :]
            misc_s[...] = misc_ref[...]
            dqc_s[...] = nt(dq_s[...], spread_matrix(D, hd)).astype(bfloat)
            dkvt_s[:, :D] = dkv_s[0].T
            dkvt_s[:, D:] = dkv_s[1].T
            gkv_s[...] = tn(sn_ref[...], dkvt_s[...])
            gq_s[...] = tn(normed_ref[...], dqc_s[...])

            for c in range(K // T):
                cg_s[...] = nt(dkvt_s[c * T : (c + 1) * T, :], wkv[...])
                for i in range(T // B):
                    rows = slice(i * B, (i + 1) * B)
                    unit, _ = norm_parts(sp_ref[c * T + i * B : c * T + (i + 1) * B, :].astype(float32))
                    misc_s[1:2, :] += jnp.sum(cg_s[rows, :] * unit, 0, keepdims=True)
            dn_s[...] = nt(dqc_s[...], wq[...])
            for i in range(T // B):
                rows = slice(i * B, (i + 1) * B)
                unit, scale = norm_parts(stream_ref[rows, :])
                part, gain_grad = norm_back(unit, scale, gain_query, dn_s[rows, :])
                misc_s[0:1, :] += gain_grad
                conv_grad = (mid_ref[rows, :] + part) * slope_ref[rows, :]
                cg_s[rows, :] = conv_grad.astype(bfloat).astype(float32)
            conv_grad = cg_s[...]
            gc_s[half : half + frame, :] = tn(x_ref[...], conv_grad.astype(bfloat))
            row = iota((T, D), 0)
            later = jnp.where(row == T - 1, 0.0, pltpu.roll(conv_grad, T - 1, 0)).astype(bfloat)
            gc_s[:half, :] = tn(x_ref[:, half:], later)
            sooner = jnp.where(row == 0, 0.0, pltpu.roll(conv_grad, 1, 0)).astype(bfloat)
            gc_s[half + frame :, :] = tn(x_ref[:, :half], sooner)
            if z.parts > 1:
                first = iota((16, D), 0) == 0
                top = jnp.where(first, conv_grad[0:16, :], 0.0).astype(bfloat)
                gc_s[:half, :] += tn(before_after[0][...], top)
                tail = jnp.where(first, pltpu.roll(conv_grad[T - 16 :, :], 1, 0), 0.0)
                gc_s[half + frame :, :] += tn(before_after[1][...], tail.astype(bfloat))
            if z.direct:
                for j in range(z.n):
                    row, lane = iota((D, LANES), 0), iota((D, LANES), 1)
                    hit = jnp.logical_and(row == lane + j * z.w, lane < z.w)
                    chosen = lax.dot_general(
                        misc_s[...], jnp.where(hit, 1.0, 0.0), (((1,), (0,)), ((), ())),
                        precision=lax.Precision.HIGHEST, preferred_element_type=float32,
                    )
                    low_rows = jnp.where(iota((8, LANES), 0) == 5, misc_s[:, :LANES], chosen)
                    place_s[j * 16 : (j + 1) * 16, :] = jnp.zeros((16, D), float32)
                    place_s[j * 16 : j * 16 + 8, :LANES] = low_rows
                emit_blocks(
                    z, meta_ref, outs[0], outs[1],
                    ((gc_s, z.cw, 1), (gq_s, z.w, 1), (gkv_s, z.w, 1), (place_s, 16, 1)),
                )

    def lanes_of(rows):
        return pl.BlockSpec((rows, LANES), lambda i: (0, i + done))

    args = [meta, q, k, v, do, misc]
    in_specs = [smem(), lanes_of(T), lanes_of(K), lanes_of(K), lanes_of(T), whole(misc.shape)]
    if z.parts > 1:
        args += list(halo)
        in_specs += [whole((16, D))] * 2
    remote = (dq, dkv, x, spectral, stream, slope, normed, sn, mid)
    args += list(remote)
    in_specs += [anywhere()] * 9
    scratch = [pltpu.VMEM((T, W), bfloat), pltpu.VMEM((2, D, K), bfloat)]
    homes = (x.shape, (K, D)) + tuple(a.shape for a in remote[4:])
    scratch += [pltpu.VMEM(s, a.dtype) for s, a in zip(homes, remote[2:])]
    scratch += [
        pltpu.VMEM((T, D), float32),
        pltpu.VMEM((T, D), float32),
        pltpu.VMEM((T, D), bfloat),
        pltpu.VMEM((K, 2 * D), bfloat),
        pltpu.SemaphoreType.DMA((10 + z.segments,)),
    ]
    grads = [((taps, D), float32), ((D, D), float32), ((D, 2 * D), float32), ((8, D), float32)]
    if z.direct:
        args.append(weights[0])
        in_specs.append(anywhere())
        scratch += [pltpu.VMEM(s, d) for s, d in grads] + [
            pltpu.VMEM((z.n * 16, D), float32),
            pltpu.VMEM((z.n, z.first_rows - z.cw, D), bfloat),
            pltpu.VMEM((D, D), bfloat),
            pltpu.VMEM((D, 2 * D), bfloat),
        ]
        shapes = block_shapes(z, z.first_grads)
    else:
        for array in (weights[1], weights[2], weights[7]):
            args.append(array)
            in_specs.append(whole(array.shape))
        shapes = grads
    return pl.pallas_call(
        kernel,
        grid=(steps,),
        out_shape=[jax.ShapeDtypeStruct(s, d) for s, d in shapes],
        in_specs=in_specs,
        out_specs=[whole(s) for s, d in shapes],
        scratch_shapes=scratch,
        compiler_params=pltpu.CompilerParams(vmem_limit_bytes=VMEM_LIMIT),
        cost_estimate=pl.CostEstimate(flops=30_000_000_000, bytes_accessed=20_000_000, transcendentals=8_000_000),
        name="back",
    )(*args)


def pairs(count, mask):
    return [(i, i ^ mask) for i in range(count)]


def tree_sum(values):
    while len(values) > 1:
        values = [values[i] + values[i + 1] for i in range(0, len(values), 2)]
    return values[0]


def over_core(z, keep, send):
    there = lax.ppermute(send, "tm", pairs(z.n, 1))
    sums = [keep[m] + there[m].astype(float32) for m in range(z.n // 2)]
    return sums[:1] + [value.astype(bfloat) for value in sums[1:]]


def over_plane(z, blocks):
    mine = blocks[:1]
    for m in range(1, z.n // 2):
        mine.append(lax.ppermute(blocks[m], "tm", pairs(z.n, 2 * m)).astype(float32))
    return tree_sum(mine)


def over_planes(z, mine):
    parts = [mine[0]]
    for m in range(1, z.planes):
        there = lax.ppermute(mine[m].astype(bfloat), "seg", pairs(z.planes, m))
        parts.append(there.astype(float32))
    low = tree_sum(parts).astype(bfloat)
    return [low] + [lax.ppermute(low, "seg", pairs(z.planes, m)) for m in range(1, z.planes)]


def adam_update(master, first, second, grad, factor, rate):
    clipped = grad * factor
    first_new = beta_first * first + (1.0 - beta_first) * clipped
    second_new = beta_second * second + (1.0 - beta_second) * clipped * clipped
    moment_hat = first_new / (1.0 - beta_first**STEP)
    square_hat = second_new / (1.0 - beta_second**STEP)
    master_new = master - rate * (
        moment_hat / (jnp.sqrt(square_hat) + adam_epsilon) + weight_decay * master
    )
    return (master_new, first_new, second_new)


RATES = (
    learn_rate, learn_rate, learn_rate, fast_rate, learn_rate, learn_rate, learn_rate, fast_rate,
)


def gather_quarters(z, meta_ref, refs, out_ref):
    quarter = refs[0].shape[0]
    for m, ref in enumerate(refs):
        start = pl.multiple_of((meta_ref[8] ^ m) * quarter, 16)
        out_ref[pl.ds(start, quarter), :] = ref[...].astype(float32)


def square_sums(z, meta, first, second):
    D = z.D

    def kernel(meta_ref, *refs):
        planes = z.planes
        a_o, b_o, sq_o = refs[2 * planes :]
        gather_quarters(z, meta_ref, refs[:planes], a_o)
        gather_quarters(z, meta_ref, refs[planes : 2 * planes], b_o)
        loss_row = z.cw + 3 * z.w + 5
        total = jnp.zeros((8, D), float32)
        for ref, skip in ((a_o, loss_row), (b_o, -1)):
            for r in range(0, ref.shape[0], 8):
                here = ref[r : r + 8, :]
                if r <= skip < r + 8:
                    here = jnp.where(iota((8, D), 0) == skip - r, 0.0, here)
                total = total + here * here
        sq_o[0:8, :] = total[:, :LANES] + total[:, LANES : 2 * LANES] + total[:, 2 * LANES :]
        loss = a_o[loss_row - 5 : loss_row + 3, :LANES]
        sq_o[8:16, :] = jnp.where(iota((8, LANES), 0) == 5, loss * (1.0 / z.n), 0.0)

    vmem = pl.BlockSpec(memory_space=pltpu.VMEM)
    shapes = [(z.first_grads, D), (z.second_grads, D), (16, LANES)]
    return pl.pallas_call(
        kernel,
        out_shape=[jax.ShapeDtypeStruct(s, float32) for s in shapes],
        in_specs=[smem()] + [vmem] * (2 * z.planes),
        out_specs=[vmem] * 3,
        compiler_params=pltpu.CompilerParams(vmem_limit_bytes=16 * 1024 * 1024),
        name="square_sums",
    )(meta, *first, *second)


def update(z, squares, first_sum, second_sum, masters, firsts, seconds):
    D, O, w, cw = z.D, z.out, z.w, z.cw
    given = len(squares)

    def kernel(*refs):
        sq_refs = refs[:given]
        a_ref, b_ref = refs[given : given + 2]
        ins = refs[given + 2 : given + 26]
        loss_o, norm_o = refs[given + 26 : given + 28]
        outs = refs[given + 28 :]
        sums = tree_sum([ref[...] for ref in sq_refs])
        norm = jnp.sqrt(jnp.sum(sums[0:8, :], keepdims=True))
        loss_o[...] = jnp.sum(sums[8:16, :], keepdims=True)
        norm_o[...] = norm
        factor = jnp.minimum(1.0, clip_limit / (norm + 1e-06))
        places = {
            0: [(a_ref, 0, cw, 0)],
            1: [(a_ref, cw, w, 0)],
            2: [(a_ref, cw + w + c * w, w, c * D) for c in range(2)],
            3: [(b_ref, 0, w, 0)],
            4: [(b_ref, w + c * w, w, c * D) for c in range(z.F // D)],
            5: [(b_ref, w + z.uw, z.fw, 0)],
        }

        def step(index, here, grad):
            values = adam_update(
                ins[index][here], ins[8 + index][here], ins[16 + index][here], grad, factor, RATES[index]
            )
            for kind, value in enumerate(values):
                outs[8 * kind + index][here] = value

        for index, pieces in places.items():
            for ref, start, count, lane in pieces:
                step(index, (slice(0, count), slice(lane, lane + D)), ref[start : start + count, :])
        start = w + z.uw + z.fw
        for g in range(D // O):
            here = (slice(g * z.hw, (g + 1) * z.hw), slice(0, O))
            step(6, here, b_ref[start : start + z.hw, g * O : (g + 1) * O])
        gains = a_ref[cw + 3 * w : cw + 3 * w + 8, :][:5, :w]
        step(7, (slice(0, 5), slice(0, w)), gains)

    vmem = pl.BlockSpec(memory_space=pltpu.VMEM)
    outs = [jax.ShapeDtypeStruct((1, 1), float32)] * 2
    outs += [jax.ShapeDtypeStruct(m.shape, float32) for m in masters] * 3
    return pl.pallas_call(
        kernel,
        out_shape=outs,
        in_specs=[vmem] * (given + 26),
        out_specs=[vmem] * 26,
        compiler_params=pltpu.CompilerParams(vmem_limit_bytes=20 * 1024 * 1024),
        name="update",
    )(*squares, first_sum, second_sum, *masters, *firsts, *seconds)


def on_device(*arguments):
    feats, spectral, target, valid_samples, stem_weights = arguments[:5]
    masters, firsts, seconds = arguments[5:13], arguments[13:21], arguments[21:29]
    n = lax.axis_size("tm")
    planes = lax.axis_size("seg")
    z = Sizes(n, planes, feats, spectral, target, masters[0], masters[4])
    S, T, D = z.segments, z.tokens, z.D
    place = lax.axis_index("tm")
    portion, member = place // S, place % S

    if z.direct:
        blobs = pack_weights(z, jnp.reshape(place, (1,)).astype(jnp.int32), masters)
        weights = [lax.all_gather(blob, "tm", axis=0) for blob in blobs]
    else:
        weights = [lax.all_gather(a.astype(bfloat), "tm", axis=0, tiled=True) for a in masters[:7]]
        gains = lax.all_gather(masters[7].astype(bfloat), "tm", axis=1, tiled=True)
        weights.append(jnp.pad(gains.astype(float32), ((0, 3), (0, 0))))
    groups = None if z.parts == 1 else [[p * S + i for i in range(S)] for p in range(z.parts)]

    packed = pack_tokens(z, jnp.transpose(feats, (0, 2, 1)), spectral, target)
    moved = lax.all_to_all(packed, "tm", 0, 0, axis_index_groups=groups, tiled=True)
    rows = z.tokens_dev
    spectral_all, target, halo = moved, moved, None
    if z.parts > 1:
        target = moved[:, :rows, D:]
        spectral_all = lax.all_gather(
            moved[:, :rows, :D].reshape(T, D), "tm", axis=0, tiled=True,
            axis_index_groups=[[p * S + i for p in range(z.parts)] for i in range(S)],
        )
        last = moved[S - 1, rows:, 4 * rows - 2 :].T.reshape(1, -1)
        lead = moved[0, rows:, :2].T.reshape(1, -1)
        halo = (
            lax.ppermute(jnp.pad(last, ((0, 15), (0, 0))), "tm", [(i, i + S) for i in range(n - S)]),
            lax.ppermute(jnp.pad(lead, ((0, 15), (0, 0))), "tm", [(i + S, i) for i in range(n - S)]),
        )
    local_count = jnp.sum(valid_samples)[None]
    if z.direct:
        counts = [local_count] + [lax.ppermute(local_count, "seg", pairs(planes, m)) for m in range(1, planes)]
        sample_count = tree_sum(counts).astype(float32)
    else:
        sample_count = lax.psum(local_count, "seg").astype(float32)
    meta = jnp.concatenate(
        [
            jnp.stack([portion * T, lax.dynamic_index_in_dim(valid_samples, member, keepdims=False)]),
            lax.dynamic_index_in_dim(stem_weights, member, keepdims=False),
            jnp.stack([place // 2, place % 2, lax.axis_index("seg")]),
        ]
    ).astype(jnp.int32)

    x, stream, slope, normed, sn, q, k, v, att = front(z, moved, spectral_all, halo, weights)
    second = middle(z, meta, sample_count, stream, att, target, weights)
    do, mid, misc = second[:3]
    done = 2
    dq, dkv = attend_back(z, q, k, v, do, done)
    if z.direct:
        second_blocks = over_core(z, second[3], second[4])
        dq, *second_blocks = lax.optimization_barrier((dq, *second_blocks))
    first = back(
        z, done, meta, q, k, v, do, dq, dkv, x, spectral_all, halo, stream, slope, normed, sn, mid, misc, weights
    )

    if z.direct:
        second_mine = over_plane(z, second_blocks)
        send, second_mine = lax.optimization_barrier((first[1], second_mine))
        first_blocks = over_core(z, first[0], send)
        second_parts = over_planes(z, second_mine)
        first_parts = over_planes(z, over_plane(z, first_blocks))
        first_sum, second_sum, both = square_sums(z, meta, first_parts, second_parts)
        both = both + lax.ppermute(both, "tm", pairs(n, 1))
        squares = [both] + [lax.ppermute(both, "tm", pairs(n, 2 * m)) for m in range(1, n // 2)]
        result = update(z, squares, first_sum, second_sum, masters, firsts, seconds)
        return (result[0].reshape(()), sample_count.reshape(()), result[1].reshape(()), *result[2:])

    grads = (first[0], first[1], first[2], second[3], second[4], second[5], second[6])
    shards = [lax.psum_scatter(g, "tm", scatter_dimension=0, tiled=True) for g in grads]
    shards.append(lax.psum_scatter(first[3][:5], "tm", scatter_dimension=1, tiled=True))
    reduced = lax.psum(tuple(shards), "seg")
    loss_sum = lax.psum(jnp.sum(first[3][5]), ("seg", "tm"))
    squares = lax.psum(sum(jnp.sum(shard * shard) for shard in reduced), "tm")
    grad_norm = jnp.sqrt(squares)
    factor = jnp.minimum(1.0, clip_limit / (grad_norm + 1e-06))
    updated = [
        adam_update(m, f, s, g, factor, r)
        for m, f, s, g, r in zip(masters, firsts, seconds, reduced, RATES)
    ]
    return (
        loss_sum, sample_count.reshape(()), grad_norm,
        *[u[0] for u in updated], *[u[1] for u in updated], *[u[2] for u in updated],
    )


def solution(mesh):
    rows, columns = P("tm", None), P(None, "tm")
    leaves = (rows,) * 7 + (columns,)
    tokens = P("seg", "tm", None)
    return jax.shard_map(
        on_device,
        mesh=mesh,
        in_specs=(tokens, tokens, tokens, P("seg"), P("seg", None)) + leaves * 3,
        out_specs=(P(), P(), P()) + leaves * 3,
        check_vma=False,
    )
```

```python
import functools
import jax
import jax.numpy as jnp
from jax import lax
from jax.experimental import pallas as pl
from jax.experimental.pallas import tpu as pltpu
from jax.sharding import PartitionSpec as P

H = 8
STEMS = 4
SUB = 16
STEP = 10
LANES = 128

clip_limit = 0.001
beta_first = 0.9
beta_second = 0.999
learn_rate = 0.03
fast_rate = 0.5
weight_decay = 0.05
adam_epsilon = 1e-08
norm_epsilon = 1e-05

bfloat = jnp.bfloat16
float32 = jnp.float32
VMEM_LIMIT = 60 * 1024 * 1024


def mm(left, right):
    return lax.dot_general(left, right, (((1,), (0,)), ((), ())), preferred_element_type=float32)


def nt(left, right):
    return lax.dot_general(left, right, (((1,), (1,)), ((), ())), preferred_element_type=float32)


def tn(left, right):
    return lax.dot_general(left, right, (((0,), (0,)), ((), ())), preferred_element_type=float32)


def iota(shape, dim):
    return lax.broadcasted_iota(jnp.int32, shape, dim)


def norm_parts(values):
    centred = values - jnp.mean(values, -1, keepdims=True)
    scale = lax.rsqrt(jnp.mean(centred * centred, -1, keepdims=True) + norm_epsilon)
    return centred * scale, scale


def norm_back(unit, scale, gain, upstream):
    inner = upstream * gain
    value_grad = scale * (
        inner
        - jnp.mean(inner, -1, keepdims=True)
        - unit * jnp.mean(inner * unit, -1, keepdims=True)
    )
    return value_grad, jnp.sum(upstream * unit, 0, keepdims=True)


def gelu_both(values):
    upper = 0.5 * (1.0 + lax.erf(values * 0.7071067811865476))
    density = jnp.exp(-0.5 * values * values) * 0.3989422804014327
    return values * upper, upper + values * density


def spread_matrix(width, head_size):
    shape = (width, width // head_size * LANES)
    lane = iota(shape, 1)
    inside = lane % LANES
    source = (lane // LANES) * head_size + inside
    hit = jnp.logical_and(iota(shape, 0) == source, inside < head_size)
    return jnp.where(hit, 1.0, 0.0).astype(bfloat)


def with_column(block, column, head_size):
    lane = iota(block.shape, 1)
    high = column.astype(bfloat).astype(float32)
    rest = column - high
    middle = rest.astype(bfloat).astype(float32)
    low = rest - middle
    pieces = jnp.where(lane == head_size, high, jnp.where(lane == head_size + 1, middle, low))
    spare = jnp.logical_and(lane >= head_size, lane < head_size + 3)
    return jnp.where(spare, pieces, block.astype(float32)).astype(bfloat)


class Sizes:
    def __init__(self, n, planes, feats, spectral, target, conv_weight, up_weight):
        self.n = n
        self.planes = planes
        self.segments = feats.shape[0]
        self.parts = n // self.segments
        self.channels = feats.shape[2]
        self.tokens_dev = spectral.shape[1]
        self.D = spectral.shape[2]
        self.taps = conv_weight.shape[0] * n
        self.frame = self.taps // 2
        self.F = up_weight.shape[1]
        self.out = target.shape[2]
        self.tokens = self.segments * self.tokens_dev
        self.keys = self.tokens * self.parts
        self.hd = self.D // H
        self.wide = H * LANES
        self.w = self.D // n
        self.cw = self.taps // n
        self.uw = self.w * (self.F // self.D)
        self.fw = self.F // n
        self.hw = self.w * self.out // self.D
        self.first_rows = self.cw + 3 * self.w + 16
        self.second_rows = self.w + self.uw + self.fw + self.hw
        step = 16 * planes
        self.first_grads = -(-self.first_rows // step) * step
        self.second_grads = -(-self.second_rows // step) * step
        self.direct = self.parts == 1 and self.w % 16 == 0 and self.hw % 16 == 0 and self.hw > 0
        self.block = 256
        self.query_block = 1024 if self.keys <= 1024 else 256


def smem():
    return pl.BlockSpec(memory_space=pltpu.SMEM)


def anywhere():
    return pl.BlockSpec(memory_space=pl.ANY)


def whole(shape):
    return pl.BlockSpec(shape, lambda i: (0,) * len(shape))


def pack_weights(z, tm_place, masters):
    D, w, O, cw = z.D, z.w, z.out, z.cw

    def kernel(place_ref, conv_r, query_r, keyval_r, out_r, up_r, down_r, head_r, gains_r, first_o, second_o):
        first_o[:cw, :] = conv_r[...].astype(bfloat)
        first_o[cw : cw + w, :] = query_r[...].astype(bfloat)
        first_o[cw + w : cw + 2 * w, :] = keyval_r[:, :D].astype(bfloat)
        first_o[cw + 2 * w : cw + 3 * w, :] = keyval_r[:, D:].astype(bfloat)
        start = place_ref[0] * w
        shift = jnp.where(iota((w, D), 1) == iota((w, D), 0) + start, 1.0, 0.0).astype(bfloat)
        placed = mm(gains_r[...].astype(bfloat), shift)
        padded = jnp.concatenate([placed, jnp.zeros((16 - placed.shape[0], D), float32)], 0)
        first_o[cw + 3 * w :, :] = padded.astype(bfloat)
        second_o[:w, :] = out_r[...].astype(bfloat)
        for c in range(z.F // D):
            second_o[w + c * w : 2 * w + c * w, :] = up_r[:, c * D : (c + 1) * D].astype(bfloat)
        row = w + z.uw
        second_o[row : row + z.fw, :] = down_r[...].astype(bfloat)
        row += z.fw
        for g in range(D // O):
            here = head_r[g * z.hw : (g + 1) * z.hw, :]
            second_o[row : row + z.hw, g * O : (g + 1) * O] = here.astype(bfloat)

    vmem = pl.BlockSpec(memory_space=pltpu.VMEM)
    return pl.pallas_call(
        kernel,
        out_shape=[
            jax.ShapeDtypeStruct((z.first_rows, D), bfloat),
            jax.ShapeDtypeStruct((z.second_rows, D), bfloat),
        ],
        in_specs=[smem()] + [vmem] * 8,
        out_specs=[vmem] * 2,
        name="pack_weights",
    )(tm_place, *masters)


def pack_tokens(z, feats, spectral, target):
    rows, D, C = z.tokens_dev, z.D, z.channels

    def kernel(f_ref, s_ref, t_ref, o_ref, buffer, in_sem, out_sem):
        arriving, leaving = [], []
        for i in range(z.segments):
            arriving.append(
                [
                    pltpu.make_async_copy(f_ref.at[i], buffer.at[i, rows:, :], in_sem.at[i, 0]),
                    pltpu.make_async_copy(s_ref.at[i], buffer.at[i, :rows, :D], in_sem.at[i, 1]),
                    pltpu.make_async_copy(t_ref.at[i], buffer.at[i, :rows, D:], in_sem.at[i, 2]),
                ]
            )
            leaving.append(pltpu.make_async_copy(buffer.at[i], o_ref.at[i], out_sem.at[i]))
            for copy in arriving[i]:
                copy.start()
        for i in range(z.segments):
            for copy in arriving[i]:
                copy.wait()
            leaving[i].start()
        for copy in leaving:
            copy.wait()

    shape = (z.segments, rows + C, 4 * rows)
    return pl.pallas_call(
        kernel,
        out_shape=jax.ShapeDtypeStruct(shape, bfloat),
        in_specs=[anywhere()] * 3,
        out_specs=anywhere(),
        scratch_shapes=[
            pltpu.VMEM(shape, bfloat),
            pltpu.SemaphoreType.DMA((z.segments, 3)),
            pltpu.SemaphoreType.DMA((z.segments,)),
        ],
        compiler_params=pltpu.CompilerParams(vmem_limit_bytes=VMEM_LIMIT),
        name="pack_tokens",
    )(feats, spectral, target)


def spectral_copies(z, source, home, sem, first):
    if z.parts > 1:
        return [pltpu.make_async_copy(source, home, sem.at[first])]
    rows = z.tokens_dev
    return [
        pltpu.make_async_copy(source.at[i, :rows, : z.D], home.at[i * rows : (i + 1) * rows, :], sem.at[first + i])
        for i in range(z.segments)
    ]


def share_copies(z, meta_ref, shares, home, rows, sem, first):
    place = meta_ref[6] * 2 + meta_ref[7]
    return [
        pltpu.make_async_copy(share.at[rows], home.at[place ^ x], sem.at[first + x])
        for x, share in enumerate(shares)
    ]


def front(z, meta, moved, spectral, halo, weights):
    D, T, K, W, B = z.D, z.tokens, z.keys, z.wide, z.block
    frame, taps, hd = z.frame, z.taps, z.hd
    half = frame // 2
    QB = z.query_block
    count = z.tokens_dev
    CB = 2 * LANES
    extra = 2 if z.parts > 1 else 0
    n_weights = z.n if z.direct else 4

    def kernel(meta_ref, *refs):
        refs = list(refs)
        frames_ref, sp_ref = refs[:2]
        before_after = refs[2 : 2 + extra]
        weight_refs = refs[2 + extra : 2 + extra + n_weights]
        refs = refs[2 + extra + n_weights :]
        (x_o, stream_o, slope_o, normed_o, sn_o, q_o, k_o, v_o, att_o) = refs[:9]
        (frames_s, sp_s, x_s, stream_s, slope_s, normed_s, sn_s) = refs[9:16]
        (conv_s, wq_s, wk_s, wv_s, q_s, k_s, v_s, in_sem, out_sem) = refs[16:25]
        refs = refs[25:]
        h = pl.program_id(0)
        outgoing = [
            pltpu.make_async_copy(src, dst, out_sem.at[i])
            for i, (src, dst) in enumerate(
                ((x_s, x_o), (stream_s, stream_o), (slope_s, slope_o), (normed_s, normed_o), (sn_s, sn_o))
            )
        ]

        @pl.when(h == 0)
        def _():
            frames_copy = pltpu.make_async_copy(frames_ref.at[:, count:, :], frames_s, in_sem.at[0])
            spectral_in = spectral_copies(z, sp_ref, sp_s, in_sem, 1)
            if z.direct:
                blob_s, wc, wqkv = refs
                blob_in = share_copies(z, meta_ref, weight_refs, blob_s, slice(0, z.first_rows), in_sem, 1 + z.segments)
                for copy in blob_in:
                    copy.start()
            for copy in spectral_in:
                copy.start()
            frames_copy.start()
            if z.direct:
                for copy in blob_in:
                    copy.wait()
                w, cw = z.w, z.cw
                total = jnp.zeros((16, D), float32)
                for j in range(z.n):
                    wc[j * cw : (j + 1) * cw, :] = blob_s[j, 0:cw, :]
                    for c in range(3):
                        first = cw + c * w
                        wqkv[j * w : (j + 1) * w, c * D : (c + 1) * D] = blob_s[j, first : first + w, :]
                    total = total + blob_s[j, cw + 3 * w : cw + 3 * w + 16, :].astype(float32)
                gain_query, gain_keys = total[0:1, :], total[1:2, :]
                parts_w = [wqkv[:, c * D : (c + 1) * D] for c in range(3)]
            else:
                wc, wq, wkv, gains_ref = weight_refs
                gain_query, gain_keys = gains_ref[0:1, :], gains_ref[1:2, :]
                parts_w = [wq[...], wkv[:, :D], wkv[:, D:]]
            spread = spread_matrix(D, hd)
            for target_s, part in zip((wq_s, wk_s, wv_s), parts_w):
                target_s[...] = mm(part, spread).astype(bfloat)
            for copy in spectral_in:
                copy.wait()
            for i in range(K // B):
                rows = slice(i * B, (i + 1) * B)
                unit, _ = norm_parts(sp_s[rows, :].astype(float32))
                sn_s[rows, :] = (unit * gain_keys).astype(bfloat)
            outgoing[4].start()
            inside = iota((K, CB), 1) % LANES
            spare = jnp.logical_and(inside >= hd, inside < hd + 3)
            for home, part in ((k_s, wk_s), (v_s, wv_s)):
                for c in range(0, W, CB):
                    product = mm(sn_s[...], part[:, c : c + CB])
                    home[:, c : c + CB] = jnp.where(spare, -1.0, product).astype(bfloat)
            frames_copy.wait()
            shape = (4 * count, 4 * count)
            row, column = iota(shape, 0), iota(shape, 1)
            order = jnp.where(column == (row % count) * 4 + row // count, 1.0, 0.0).astype(bfloat)
            for i in range(z.segments):
                taps_rows = nt(order, frames_s[i])
                x_s[i * count : (i + 1) * count, :] = jnp.concatenate(
                    [taps_rows[j * count : (j + 1) * count, :] for j in range(4)], 1
                ).astype(bfloat)
            outgoing[0].start()
            conv_s[...] = mm(x_s[...], wc[half : half + frame, :])
            row = iota((T, D), 0)
            older = pltpu.roll(mm(x_s[:, half:], wc[:half, :]), 1, 0)
            first_row, last_row = 0.0, 0.0
            if z.parts > 1:
                first_row = mm(before_after[0][...], wc[:half, :])[0:1, :]
                last_row = mm(before_after[1][...], wc[half + frame :, :])[0:1, :]
            conv_s[...] += jnp.where(row == 0, first_row, older)
            newer = pltpu.roll(mm(x_s[:, :half], wc[half + frame :, :]), T - 1, 0)
            conv_s[...] += jnp.where(row == T - 1, last_row, newer)

            for i in range(T // B):
                rows = slice(i * B, (i + 1) * B)
                stream, slope = gelu_both(conv_s[rows, :])
                stream_s[rows, :] = stream
                slope_s[rows, :] = slope
                unit, _ = norm_parts(stream)
                normed = (unit * gain_query).astype(bfloat)
                normed_s[rows, :] = normed
            for c in range(0, W, CB):
                q_s[:, c : c + CB] = mm(normed_s[...], wq_s[:, c : c + CB]).astype(bfloat)
            for copy in outgoing[1:4]:
                copy.start()

        lanes = pl.ds(pl.multiple_of(h * LANES, LANES), LANES)
        k_o[...] = k_s[:, lanes]
        v_o[...] = v_s[:, lanes]
        for b in range(T // QB):
            rows = slice(b * QB, (b + 1) * QB)
            q = q_s[rows, lanes]

            def finish(grown, top, rows=rows, q=q):
                mass = jnp.sum(grown, 0, keepdims=True)
                probs = (grown * (1.0 / mass)).astype(bfloat)
                total = top + jnp.log(mass)
                result = tn(v_o[...], probs)
                high = total.astype(bfloat).astype(float32)
                rest = total - high
                mid = rest.astype(bfloat).astype(float32)
                sub = iota((LANES, QB), 0)
                spare = jnp.where(sub == hd, high, jnp.where(sub == hd + 1, mid, rest - mid))
                spare = jnp.where(sub < hd + 3, spare, 0.0)
                both = jnp.where(sub < hd, result, spare).T
                att_o[rows, :] = both.astype(bfloat)
                lane = iota((QB, LANES), 1)
                q_o[rows, :] = jnp.where(lane < hd, q.astype(float32), both).astype(bfloat)
                return mass

            mass = finish(jnp.exp(nt(k_o[...], q)), 0.0)
            safe = jnp.logical_and(jnp.min(mass) > 1e-20, jnp.max(mass) < 1e30)

            @pl.when(jnp.logical_not(safe))
            def _(q=q, finish=finish):
                scores = nt(k_o[...], q)
                top = jnp.max(scores, 0, keepdims=True)
                finish(jnp.exp(scores - top), top)

        @pl.when(h == H - 1)
        def _():
            for copy in outgoing:
                copy.wait()

    def lanes_of(rows):
        return pl.BlockSpec((rows, LANES), lambda h: (0, h))

    in_specs = [smem(), anywhere(), anywhere()]
    args = [meta, moved, moved if z.parts == 1 else spectral]
    if z.parts > 1:
        args += list(halo)
        in_specs += [whole((16, D))] * 2
    scratch = [
        pltpu.VMEM((z.segments, z.channels, 4 * count), bfloat),
        pltpu.VMEM((K, D), bfloat),
        pltpu.VMEM((T, frame), bfloat),
        pltpu.VMEM((T, D), float32),
        pltpu.VMEM((T, D), float32),
        pltpu.VMEM((T, D), bfloat),
        pltpu.VMEM((K, D), bfloat),
        pltpu.VMEM((T, D), float32),
        pltpu.VMEM((D, W), bfloat),
        pltpu.VMEM((D, W), bfloat),
        pltpu.VMEM((D, W), bfloat),
        pltpu.VMEM((T, W), bfloat),
        pltpu.VMEM((K, W), bfloat),
        pltpu.VMEM((K, W), bfloat),
        pltpu.SemaphoreType.DMA((1 + z.segments + z.n,)),
        pltpu.SemaphoreType.DMA((5,)),
    ]
    if z.direct:
        args += weights[0]
        in_specs += [anywhere()] * z.n
        scratch += [
            pltpu.VMEM((z.n, z.first_rows, D), bfloat),
            pltpu.VMEM((taps, D), bfloat),
            pltpu.VMEM((D, 3 * D), bfloat),
        ]
    else:
        for array in (weights[0], weights[1], weights[2], weights[7]):
            args.append(array)
            in_specs.append(whole(array.shape))
    shapes = [
        ((T, frame), bfloat),
        ((T, D), float32),
        ((T, D), float32),
        ((T, D), bfloat),
        ((K, D), bfloat),
        ((T, W), bfloat),
        ((K, W), bfloat),
        ((K, W), bfloat),
        ((T, W), bfloat),
    ]
    return pl.pallas_call(
        kernel,
        grid=(H,),
        out_shape=[jax.ShapeDtypeStruct(s, d) for s, d in shapes],
        in_specs=in_specs,
        out_specs=[anywhere()] * 5 + [lanes_of(T), lanes_of(K), lanes_of(K), lanes_of(T)],
        scratch_shapes=scratch,
        compiler_params=pltpu.CompilerParams(vmem_limit_bytes=VMEM_LIMIT),
        cost_estimate=pl.CostEstimate(flops=20_000_000_000, bytes_accessed=20_000_000, transcendentals=10_000_000),
        name="front",
    )(*args)


def emit_blocks(z, meta_ref, keep_o, send_o, sources):
    chip, core, plane = meta_ref[6], meta_ref[7], meta_ref[8]
    quarter = keep_o.shape[2]

    def write(out, m, row, here, lanes):
        first = 0
        while first < here.shape[0]:
            part, inside = divmod(row + first, quarter)
            size = min(here.shape[0] - first, quarter - inside)
            out[m, part ^ plane, inside : inside + size, lanes] = here[first : first + size].astype(out.dtype)
            first += size

    for m in range(z.n // 2):
        owner = (chip ^ m) * 2
        for out, place in ((keep_o, owner + core), (send_o, owner + 1 - core)):
            row = 0
            for ref, rows, pieces in sources:
                width = ref.shape[-1]
                if width >= z.D:
                    start = pl.multiple_of(place * rows, 16)
                    for lane in range(0, width, z.D):
                        write(out, m, row, ref[pl.ds(start, rows), lane : lane + z.D], slice(0, z.D))
                        row += rows
                else:
                    size = rows // pieces
                    for g in range(pieces):
                        start = pl.multiple_of(place * rows + g * size, 16)
                        write(out, m, row, ref[pl.ds(start, size), :], slice(g * width, (g + 1) * width))
                    row += size
            if row < quarter * z.planes:
                rest = quarter * z.planes - row
                write(out, m, row, jnp.zeros((rest, z.D), float32), slice(0, z.D))


def block_shapes(z, rows):
    shape = (z.n // 2, z.planes, rows // z.planes, z.D)
    return [(shape, float32), (shape, bfloat)]


def middle(z, meta, count, stream, att, target, weights):
    D, T, W, F, O = z.D, z.tokens, z.wide, z.F, z.out
    B = T
    hd = z.hd

    def kernel(meta_ref, count_ref, stream_ref, att_ref, target_ref, *refs):
        refs = list(refs)
        if z.direct:
            first_refs, second_refs = refs[: z.n], refs[z.n : 2 * z.n]
            refs = refs[2 * z.n :]
            do_out, mid_out, misc_o, keep_o, send_o = refs[:5]
            refs = refs[5:]
        else:
            wo, wu, wd, wh, gains_ref = refs[:5]
            do_out, mid_out, misc_o, go_s, gu_s, gd_s, gh_s = refs[5:12]
            refs = refs[12:]
        wop, att_s, stream_s, do_o, mid_o, act_s, hg_s, fin_s, fg_s, low_s, pg_s, bg_s, sem = refs[:13]
        refs = refs[13:]
        if z.direct:
            go_s, gu_s, gd_s, gh_s, blob_s, gain_s, wo, wu, wd, wh = refs

        att_copy = pltpu.make_async_copy(att_ref, att_s, sem.at[0])
        stream_copy = pltpu.make_async_copy(stream_ref, stream_s, sem.at[1])
        if z.direct:
            w, uw, fw, hw = z.w, z.uw, z.fw, z.hw
            ends = (0, w, w + uw, w + uw + fw, z.second_rows)
            pieces = [
                share_copies(z, meta_ref, second_refs, blob_s.at[:, p:q], slice(p, q), sem, 9 + c * z.n)
                for c, (p, q) in enumerate(zip(ends[:-1], ends[1:]))
            ]
            last = slice(z.first_rows - 16, z.first_rows)
            gain_in = share_copies(z, meta_ref, first_refs, gain_s, last, sem, 9 + 4 * z.n)
            for copy in pieces[0] + gain_in:
                copy.start()
        att_copy.start()
        stream_copy.start()
        if z.direct:
            for piece in pieces[1:]:
                for copy in piece:
                    copy.start()
            for copy in pieces[0] + gain_in:
                copy.wait()
            total = jnp.zeros((16, D), float32)
            for j in range(z.n):
                wo[j * w : (j + 1) * w, :] = blob_s[j, 0:w, :]
                total = total + gain_s[j].astype(float32)
        else:
            total = gains_ref[...]
        wop[...] = tn(spread_matrix(D, hd), wo[...]).astype(bfloat)
        misc_o[...] = jnp.zeros_like(misc_o)
        gain_ffn, scale_attn, scale_ffn = total[2:3, :], total[3:4, :], total[4:5, :]
        base, valid = meta_ref[0], meta_ref[1]
        samples = count_ref[0]
        rows = slice(0, B)
        att_copy.wait()
        att = att_s
        branch = mm(att[...], wop[...])
        stream_copy.wait()
        stream_mid = stream_s[...] + scale_attn * branch
        unit, scale = norm_parts(stream_mid)
        ffn_in = (unit * gain_ffn).astype(bfloat)
        fin_s[rows, :] = ffn_in
        if z.direct:
            for copy in pieces[1]:
                copy.wait()
            for j in range(z.n):
                for c in range(F // D):
                    first = w + c * w
                    wu[j * w : (j + 1) * w, c * D : (c + 1) * D] = blob_s[j, first : first + w, :]
        hidden = mm(ffn_in, wu[...])
        active, slope = gelu_both(hidden)
        active = active.astype(bfloat)
        act_s[rows, :] = active
        if z.direct:
            for copy in pieces[2] + pieces[3]:
                copy.wait()
            for j in range(z.n):
                wd[j * fw : (j + 1) * fw, :] = blob_s[j, w + uw : w + uw + fw, :]
                for g in range(D // O):
                    start = j * w + g * hw
                    wh[start : start + hw, :] = blob_s[j, w + uw + fw :, g * O : (g + 1) * O]
        ffn_out = mm(active, wd[...])
        stream_low = (stream_mid + scale_ffn * ffn_out).astype(bfloat)
        low_s[rows, :] = stream_low
        predicted = mm(stream_low, wh[...])
        column = iota((B, O), 1)
        position = (base + iota((B, O), 0)) * SUB + column % SUB
        stem = column // (2 * SUB)
        weight = jnp.zeros((B, O), float32)
        for k in range(STEMS):
            weight = jnp.where(stem == k, meta_ref[2 + k].astype(float32), weight)
        weight = jnp.where(position < valid, weight, 0.0)
        error = predicted - target_ref[...].reshape(B, O).astype(float32)
        root = jnp.sqrt(error * error + 1.0)
        misc_o[5:6, :O] += jnp.sum(weight * (root - 1.0), 0, keepdims=True)
        predicted_grad = (weight * error / root / samples).astype(bfloat)
        pg_s[rows, :] = predicted_grad
        end_grad = nt(predicted_grad, wh[...])
        misc_o[4:5, :] += jnp.sum(end_grad * ffn_out, 0, keepdims=True)
        ffn_grad = (scale_ffn * end_grad).astype(bfloat)
        fg_s[rows, :] = ffn_grad
        hidden_grad = (nt(ffn_grad, wd[...]) * slope).astype(bfloat)
        hg_s[rows, :] = hidden_grad
        mid_part, gain_grad = norm_back(unit, scale, gain_ffn, nt(hidden_grad, wu[...]))
        misc_o[2:3, :] += gain_grad
        mid_grad = end_grad + mid_part
        mid_o[...] = mid_grad
        misc_o[3:4, :] += jnp.sum(mid_grad * branch, 0, keepdims=True)
        branch_grad = (scale_attn * mid_grad).astype(bfloat)
        bg_s[rows, :] = branch_grad
        att_grad = nt(branch_grad, wop[...]).astype(bfloat)
        for h in range(H):
            lanes = slice(h * LANES, (h + 1) * LANES)
            one = att_grad[:, lanes].astype(float32)
            delta = jnp.sum(one * att[:, lanes].astype(float32), -1, keepdims=True)
            do_o[:, lanes] = with_column(one, delta, hd)

        outgoing = [
            pltpu.make_async_copy(do_o, do_out, sem.at[7]),
            pltpu.make_async_copy(mid_o, mid_out, sem.at[8]),
        ]
        for copy in outgoing:
            copy.start()
        spare_grad = tn(att_s[...], bg_s[...])
        for h in range(H):
            go_s[h * hd : (h + 1) * hd, :] = spare_grad[h * LANES : h * LANES + hd, :]
        gu_s[...] = tn(fin_s[...], hg_s[...])
        gd_s[...] = tn(act_s[...], fg_s[...])
        gh_s[...] = tn(low_s[...], pg_s[...])
        if z.direct:
            emit_blocks(
                z,
                meta_ref,
                keep_o,
                send_o,
                ((go_s, z.w, 1), (gu_s, z.w, 1), (gd_s, z.fw, 1), (gh_s, z.w, D // O)),
            )
        for copy in outgoing:
            copy.wait()

    if z.parts == 1:
        target_spec = pl.BlockSpec((z.segments, z.tokens_dev, O), lambda i: (0, 0, D // O))
    else:
        target_spec = whole(target.shape)
    in_specs = [smem(), smem(), anywhere(), anywhere(), target_spec]
    args = [meta, count, stream, att, target]
    scratch = [
        pltpu.VMEM((W, D), bfloat),
        pltpu.VMEM((T, W), bfloat),
        pltpu.VMEM((T, D), float32),
        pltpu.VMEM((T, W), bfloat),
        pltpu.VMEM((T, D), float32),
        pltpu.VMEM((T, F), bfloat),
        pltpu.VMEM((T, F), bfloat),
        pltpu.VMEM((T, D), bfloat),
        pltpu.VMEM((T, D), bfloat),
        pltpu.VMEM((T, D), bfloat),
        pltpu.VMEM((T, O), bfloat),
        pltpu.VMEM((T, D), bfloat),
        pltpu.SemaphoreType.DMA((9 + 5 * z.n,)),
    ]
    shapes = [((T, W), bfloat), ((T, D), float32), ((8, D), float32)]
    grads = [((D, D), float32), ((D, F), float32), ((F, D), float32), ((D, O), float32)]
    if z.direct:
        args += weights[0] + weights[1]
        in_specs += [anywhere()] * (2 * z.n)
        scratch += [pltpu.VMEM(s, d) for s, d in grads] + [
            pltpu.VMEM((z.n, z.second_rows, D), bfloat),
            pltpu.VMEM((z.n, 16, D), bfloat),
            pltpu.VMEM((D, D), bfloat),
            pltpu.VMEM((D, F), bfloat),
            pltpu.VMEM((F, D), bfloat),
            pltpu.VMEM((D, O), bfloat),
        ]
        shapes += block_shapes(z, z.second_grads)
    else:
        for array in weights[3:]:
            args.append(array)
            in_specs.append(whole(array.shape))
        shapes += grads
    return pl.pallas_call(
        kernel,
        grid=(1,),
        out_shape=[jax.ShapeDtypeStruct(s, d) for s, d in shapes],
        in_specs=in_specs,
        out_specs=[anywhere(), anywhere()] + [whole(s) for s, d in shapes[2:]],
        scratch_shapes=scratch,
        compiler_params=pltpu.CompilerParams(vmem_limit_bytes=VMEM_LIMIT),
        cost_estimate=pl.CostEstimate(flops=20_000_000_000, bytes_accessed=20_000_000, transcendentals=4_000_000),
        name="middle",
    )(*args)


def head_back(z, q_ref, k_ref, v_ref, do_ref, put_query):
    T, hd = z.tokens, z.hd
    QB = 256 if z.keys <= 1024 else 128
    for b in range(T // QB):
        rows = slice(b * QB, (b + 1) * QB)
        q, do = q_ref[rows, :], do_ref[rows, :]
        probs = jnp.exp(nt(q, k_ref[...]))
        score_grad = (probs * nt(do, v_ref[...])).astype(bfloat)
        low = probs.astype(bfloat)
        put_query(rows, mm(score_grad, k_ref[...]).astype(bfloat))
        dk, dv = tn(q, score_grad), tn(do, low)
        if b == 0:
            dk_sum, dv_sum = dk, dv
        else:
            dk_sum, dv_sum = dk_sum + dk, dv_sum + dv
    return dk_sum[:hd, :].astype(bfloat), dv_sum[:hd, :].astype(bfloat)


def attend_back(z, q, k, v, do, heads):
    T, K, W, D = z.tokens, z.keys, z.wide, z.D
    hd = z.hd

    def kernel(q_ref, k_ref, v_ref, do_ref, dq_o, dkv_o):
        def put_query(rows, value):
            dq_o[rows, :] = value

        dkv_o[0], dkv_o[1] = head_back(z, q_ref, k_ref, v_ref, do_ref, put_query)

    def lanes(rows):
        return pl.BlockSpec((rows, LANES), lambda h: (0, h))

    return pl.pallas_call(
        kernel,
        grid=(heads,),
        out_shape=[
            jax.ShapeDtypeStruct((T, heads * LANES), bfloat),
            jax.ShapeDtypeStruct((2, heads * hd, K), bfloat),
        ],
        in_specs=[lanes(T), lanes(K), lanes(K), lanes(T)],
        out_specs=[lanes(T), pl.BlockSpec((2, hd, K), lambda h: (0, h, 0))],
        compiler_params=pltpu.CompilerParams(vmem_limit_bytes=VMEM_LIMIT),
        cost_estimate=pl.CostEstimate(
            flops=heads * 4_000_000_000, bytes_accessed=12_000_000, transcendentals=heads * 1_000_000
        ),
        name="attend_back",
    )(q, k, v, do)


def back(z, done, meta, q, k, v, do, dq, dkv, x, spectral, halo, stream, slope, normed, sn, mid, misc, weights):
    D, T, K, W, B, O = z.D, z.tokens, z.keys, z.wide, z.block, z.out
    frame, taps, hd = z.frame, z.taps, z.hd
    half = frame // 2
    steps = H - done
    extra = 2 if z.parts > 1 else 0
    n_weights = z.n if z.direct else 3
    n_out = 2 if z.direct else 4

    def kernel(meta_ref, q_ref, k_ref, v_ref, do_ref, misc_ref, *refs):
        refs = list(refs)
        before_after = refs[:extra]
        remote = refs[extra : extra + 9]
        refs = refs[extra + 9 :]
        weight_refs, refs = refs[:n_weights], refs[n_weights:]
        outs, refs = refs[:n_out], refs[n_out:]
        (dq_s, dkv_s, x_ref, sp_ref, stream_ref, slope_ref, normed_ref, sn_ref, mid_ref) = refs[:9]
        refs = refs[9:]
        cg_s, dn_s, dqc_s, dkvt_s, sem = refs[:5]
        refs = refs[5:]
        if z.direct:
            gc_s, gq_s, gkv_s, misc_s, place_s, blob_s, wq, wkv = refs
        else:
            gc_s, gq_s, gkv_s, misc_s = outs
            wq, wkv, gains_ref = weight_refs
        i = pl.program_id(0)
        old = done * LANES
        homes = [dq_s.at[:, :old], dkv_s.at[:, : done * hd]] + [
            x_ref, sp_ref, stream_ref, slope_ref, normed_ref, sn_ref, mid_ref
        ]
        copies = [
            pltpu.make_async_copy(a, b, sem.at[c])
            for c, (a, b) in enumerate(zip(remote, homes))
            if c != 3
        ]
        copies += spectral_copies(z, remote[3], sp_ref, sem, 10)
        if z.direct:
            copies += share_copies(
                z, meta_ref, weight_refs, blob_s, slice(z.cw, z.first_rows), sem, 10 + z.segments
            )

        @pl.when(i == 0)
        def _():
            for copy in copies:
                copy.start()

        lanes = pl.ds(pl.multiple_of((i + done) * LANES, LANES), LANES)

        def put_query(rows, value):
            dq_s[rows, lanes] = value

        dk, dv = head_back(z, q_ref, k_ref, v_ref, do_ref, put_query)
        here = pl.ds(pl.multiple_of((i + done) * hd, 16), hd)
        dkv_s[0, here, :] = dk
        dkv_s[1, here, :] = dv

        @pl.when(i == steps - 1)
        def _():
            for copy in copies:
                copy.wait()
            if z.direct:
                w = z.w
                total = jnp.zeros((16, D), float32)
                for j in range(z.n):
                    here = slice(j * w, (j + 1) * w)
                    wq[here, :] = blob_s[j, 0:w, :]
                    wkv[here, :D] = blob_s[j, w : 2 * w, :]
                    wkv[here, D:] = blob_s[j, 2 * w : 3 * w, :]
                    total = total + blob_s[j, 3 * w :, :].astype(float32)
            else:
                total = gains_ref[...]
            gain_query = total[0:1, :]
            misc_s[...] = misc_ref[...]
            dqc_s[...] = nt(dq_s[...], spread_matrix(D, hd)).astype(bfloat)
            dkvt_s[:, :D] = dkv_s[0].T
            dkvt_s[:, D:] = dkv_s[1].T
            gkv_s[...] = tn(sn_ref[...], dkvt_s[...])
            gq_s[...] = tn(normed_ref[...], dqc_s[...])

            for c in range(K // T):
                cg_s[...] = nt(dkvt_s[c * T : (c + 1) * T, :], wkv[...])
                for i in range(T // B):
                    rows = slice(i * B, (i + 1) * B)
                    unit, _ = norm_parts(sp_ref[c * T + i * B : c * T + (i + 1) * B, :].astype(float32))
                    misc_s[1:2, :] += jnp.sum(cg_s[rows, :] * unit, 0, keepdims=True)
            dn_s[...] = nt(dqc_s[...], wq[...])
            for i in range(T // B):
                rows = slice(i * B, (i + 1) * B)
                unit, scale = norm_parts(stream_ref[rows, :])
                part, gain_grad = norm_back(unit, scale, gain_query, dn_s[rows, :])
                misc_s[0:1, :] += gain_grad
                conv_grad = (mid_ref[rows, :] + part) * slope_ref[rows, :]
                cg_s[rows, :] = conv_grad.astype(bfloat).astype(float32)
            conv_grad = cg_s[...]
            gc_s[half : half + frame, :] = tn(x_ref[...], conv_grad.astype(bfloat))
            row = iota((T, D), 0)
            later = jnp.where(row == T - 1, 0.0, pltpu.roll(conv_grad, T - 1, 0)).astype(bfloat)
            gc_s[:half, :] = tn(x_ref[:, half:], later)
            sooner = jnp.where(row == 0, 0.0, pltpu.roll(conv_grad, 1, 0)).astype(bfloat)
            gc_s[half + frame :, :] = tn(x_ref[:, :half], sooner)
            if z.parts > 1:
                first = iota((16, D), 0) == 0
                top = jnp.where(first, conv_grad[0:16, :], 0.0).astype(bfloat)
                gc_s[:half, :] += tn(before_after[0][...], top)
                tail = jnp.where(first, pltpu.roll(conv_grad[T - 16 :, :], 1, 0), 0.0)
                gc_s[half + frame :, :] += tn(before_after[1][...], tail.astype(bfloat))
            if z.direct:
                for j in range(z.n):
                    row, lane = iota((D, LANES), 0), iota((D, LANES), 1)
                    hit = jnp.logical_and(row == lane + j * z.w, lane < z.w)
                    chosen = lax.dot_general(
                        misc_s[...], jnp.where(hit, 1.0, 0.0), (((1,), (0,)), ((), ())),
                        precision=lax.Precision.HIGHEST, preferred_element_type=float32,
                    )
                    low_rows = jnp.where(iota((8, LANES), 0) == 5, misc_s[:, :LANES], chosen)
                    place_s[j * 16 : (j + 1) * 16, :] = jnp.zeros((16, D), float32)
                    place_s[j * 16 : j * 16 + 8, :LANES] = low_rows
                emit_blocks(
                    z, meta_ref, outs[0], outs[1],
                    ((gc_s, z.cw, 1), (gq_s, z.w, 1), (gkv_s, z.w, 1), (place_s, 16, 1)),
                )

    def lanes_of(rows):
        return pl.BlockSpec((rows, LANES), lambda i: (0, i + done))

    args = [meta, q, k, v, do, misc]
    in_specs = [smem(), lanes_of(T), lanes_of(K), lanes_of(K), lanes_of(T), whole(misc.shape)]
    if z.parts > 1:
        args += list(halo)
        in_specs += [whole((16, D))] * 2
    remote = (dq, dkv, x, spectral, stream, slope, normed, sn, mid)
    args += list(remote)
    in_specs += [anywhere()] * 9
    scratch = [pltpu.VMEM((T, W), bfloat), pltpu.VMEM((2, D, K), bfloat)]
    homes = (x.shape, (K, D)) + tuple(a.shape for a in remote[4:])
    scratch += [pltpu.VMEM(s, a.dtype) for s, a in zip(homes, remote[2:])]
    scratch += [
        pltpu.VMEM((T, D), float32),
        pltpu.VMEM((T, D), float32),
        pltpu.VMEM((T, D), bfloat),
        pltpu.VMEM((K, 2 * D), bfloat),
        pltpu.SemaphoreType.DMA((10 + z.segments + z.n,)),
    ]
    grads = [((taps, D), float32), ((D, D), float32), ((D, 2 * D), float32), ((8, D), float32)]
    if z.direct:
        args += weights[0]
        in_specs += [anywhere()] * z.n
        scratch += [pltpu.VMEM(s, d) for s, d in grads] + [
            pltpu.VMEM((z.n * 16, D), float32),
            pltpu.VMEM((z.n, z.first_rows - z.cw, D), bfloat),
            pltpu.VMEM((D, D), bfloat),
            pltpu.VMEM((D, 2 * D), bfloat),
        ]
        shapes = block_shapes(z, z.first_grads)
    else:
        for array in (weights[1], weights[2], weights[7]):
            args.append(array)
            in_specs.append(whole(array.shape))
        shapes = grads
    return pl.pallas_call(
        kernel,
        grid=(steps,),
        out_shape=[jax.ShapeDtypeStruct(s, d) for s, d in shapes],
        in_specs=in_specs,
        out_specs=[whole(s) for s, d in shapes],
        scratch_shapes=scratch,
        compiler_params=pltpu.CompilerParams(vmem_limit_bytes=VMEM_LIMIT),
        cost_estimate=pl.CostEstimate(flops=30_000_000_000, bytes_accessed=20_000_000, transcendentals=8_000_000),
        name="back",
    )(*args)


def pairs(count, mask):
    return [(i, i ^ mask) for i in range(count)]


def tree_sum(values):
    while len(values) > 1:
        values = [values[i] + values[i + 1] for i in range(0, len(values), 2)]
    return values[0]


def from_chips(z, own):
    return [own] + [lax.ppermute(own, "tm", pairs(z.n, 2 * m)) for m in range(1, z.n // 2)]


def with_core(z, same):
    other = [lax.ppermute(share, "tm", pairs(z.n, 1)) for share in same]
    return [share for pair in zip(same, other) for share in pair]


def over_core(z, keep, send):
    there = lax.ppermute(send, "tm", pairs(z.n, 1))
    sums = [keep[m] + there[m].astype(float32) for m in range(z.n // 2)]
    return sums[:1] + [value.astype(bfloat) for value in sums[1:]]


def over_plane(z, blocks):
    mine = blocks[:1]
    for m in range(1, z.n // 2):
        mine.append(lax.ppermute(blocks[m], "tm", pairs(z.n, 2 * m)).astype(float32))
    return tree_sum(mine)


def over_planes(z, mine):
    parts = [mine[0]]
    for m in range(1, z.planes):
        there = lax.ppermute(mine[m].astype(bfloat), "seg", pairs(z.planes, m))
        parts.append(there.astype(float32))
    low = tree_sum(parts).astype(bfloat)
    return [low] + [lax.ppermute(low, "seg", pairs(z.planes, m)) for m in range(1, z.planes)]


def adam_update(master, first, second, grad, factor, rate):
    clipped = grad * factor
    first_new = beta_first * first + (1.0 - beta_first) * clipped
    second_new = beta_second * second + (1.0 - beta_second) * clipped * clipped
    moment_hat = first_new / (1.0 - beta_first**STEP)
    square_hat = second_new / (1.0 - beta_second**STEP)
    master_new = master - rate * (
        moment_hat / (jnp.sqrt(square_hat) + adam_epsilon) + weight_decay * master
    )
    return (master_new, first_new, second_new)


RATES = (
    learn_rate, learn_rate, learn_rate, fast_rate, learn_rate, learn_rate, learn_rate, fast_rate,
)


def gather_quarters(z, meta_ref, refs, out_ref):
    quarter = refs[0].shape[0]
    for m, ref in enumerate(refs):
        start = pl.multiple_of((meta_ref[8] ^ m) * quarter, 16)
        out_ref[pl.ds(start, quarter), :] = ref[...].astype(float32)


def square_sums(z, meta, first, second):
    D = z.D

    def kernel(meta_ref, *refs):
        planes = z.planes
        a_o, b_o, sq_o = refs[2 * planes :]
        gather_quarters(z, meta_ref, refs[:planes], a_o)
        gather_quarters(z, meta_ref, refs[planes : 2 * planes], b_o)
        loss_row = z.cw + 3 * z.w + 5
        total = jnp.zeros((8, D), float32)
        for ref, skip in ((a_o, loss_row), (b_o, -1)):
            for r in range(0, ref.shape[0], 8):
                here = ref[r : r + 8, :]
                if r <= skip < r + 8:
                    here = jnp.where(iota((8, D), 0) == skip - r, 0.0, here)
                total = total + here * here
        sq_o[0:8, :] = total[:, :LANES] + total[:, LANES : 2 * LANES] + total[:, 2 * LANES :]
        loss = a_o[loss_row - 5 : loss_row + 3, :LANES]
        sq_o[8:16, :] = jnp.where(iota((8, LANES), 0) == 5, loss * (1.0 / z.n), 0.0)

    vmem = pl.BlockSpec(memory_space=pltpu.VMEM)
    shapes = [(z.first_grads, D), (z.second_grads, D), (16, LANES)]
    return pl.pallas_call(
        kernel,
        out_shape=[jax.ShapeDtypeStruct(s, float32) for s in shapes],
        in_specs=[smem()] + [vmem] * (2 * z.planes),
        out_specs=[vmem] * 3,
        compiler_params=pltpu.CompilerParams(vmem_limit_bytes=16 * 1024 * 1024),
        name="square_sums",
    )(meta, *first, *second)


def update(z, squares, first_sum, second_sum, masters, firsts, seconds):
    D, O, w, cw = z.D, z.out, z.w, z.cw
    given = len(squares)

    def kernel(*refs):
        sq_refs = refs[:given]
        a_ref, b_ref = refs[given : given + 2]
        ins = refs[given + 2 : given + 26]
        loss_o, norm_o = refs[given + 26 : given + 28]
        outs = refs[given + 28 :]
        sums = tree_sum([ref[...] for ref in sq_refs])
        norm = jnp.sqrt(jnp.sum(sums[0:8, :], keepdims=True))
        loss_o[...] = jnp.sum(sums[8:16, :], keepdims=True)
        norm_o[...] = norm
        factor = jnp.minimum(1.0, clip_limit / (norm + 1e-06))
        places = {
            0: [(a_ref, 0, cw, 0)],
            1: [(a_ref, cw, w, 0)],
            2: [(a_ref, cw + w + c * w, w, c * D) for c in range(2)],
            3: [(b_ref, 0, w, 0)],
            4: [(b_ref, w + c * w, w, c * D) for c in range(z.F // D)],
            5: [(b_ref, w + z.uw, z.fw, 0)],
        }

        def step(index, here, grad):
            values = adam_update(
                ins[index][here], ins[8 + index][here], ins[16 + index][here], grad, factor, RATES[index]
            )
            for kind, value in enumerate(values):
                outs[8 * kind + index][here] = value

        for index, pieces in places.items():
            for ref, start, count, lane in pieces:
                step(index, (slice(0, count), slice(lane, lane + D)), ref[start : start + count, :])
        start = w + z.uw + z.fw
        for g in range(D // O):
            here = (slice(g * z.hw, (g + 1) * z.hw), slice(0, O))
            step(6, here, b_ref[start : start + z.hw, g * O : (g + 1) * O])
        gains = a_ref[cw + 3 * w : cw + 3 * w + 8, :][:5, :w]
        step(7, (slice(0, 5), slice(0, w)), gains)

    vmem = pl.BlockSpec(memory_space=pltpu.VMEM)
    outs = [jax.ShapeDtypeStruct((1, 1), float32)] * 2
    outs += [jax.ShapeDtypeStruct(m.shape, float32) for m in masters] * 3
    return pl.pallas_call(
        kernel,
        out_shape=outs,
        in_specs=[vmem] * (given + 26),
        out_specs=[vmem] * 26,
        compiler_params=pltpu.CompilerParams(vmem_limit_bytes=20 * 1024 * 1024),
        name="update",
    )(*squares, first_sum, second_sum, *masters, *firsts, *seconds)


def on_device(*arguments):
    feats, spectral, target, valid_samples, stem_weights = arguments[:5]
    masters, firsts, seconds = arguments[5:13], arguments[13:21], arguments[21:29]
    n = lax.axis_size("tm")
    planes = lax.axis_size("seg")
    z = Sizes(n, planes, feats, spectral, target, masters[0], masters[4])
    S, T, D = z.segments, z.tokens, z.D
    place = lax.axis_index("tm")
    portion, member = place // S, place % S

    if z.direct:
        blobs = pack_weights(z, jnp.reshape(place, (1,)).astype(jnp.int32), masters)
        same_first = from_chips(z, blobs[0])
    else:
        weights = [lax.all_gather(a.astype(bfloat), "tm", axis=0, tiled=True) for a in masters[:7]]
        gains = lax.all_gather(masters[7].astype(bfloat), "tm", axis=1, tiled=True)
        weights.append(jnp.pad(gains.astype(float32), ((0, 3), (0, 0))))
    groups = None if z.parts == 1 else [[p * S + i for i in range(S)] for p in range(z.parts)]

    packed = pack_tokens(z, jnp.transpose(feats, (0, 2, 1)), spectral, target)
    if z.direct:
        packed, *same_first = lax.optimization_barrier((packed, *same_first))
    moved = lax.all_to_all(packed, "tm", 0, 0, axis_index_groups=groups, tiled=True)
    if z.direct:
        weights = [with_core(z, same_first)]
        blob, valid_samples, _ = lax.optimization_barrier((blobs[1], valid_samples, weights[0][1]))
        same_second = from_chips(z, blob)
    rows = z.tokens_dev
    spectral_all, target, halo = moved, moved, None
    if z.parts > 1:
        target = moved[:, :rows, D:]
        spectral_all = lax.all_gather(
            moved[:, :rows, :D].reshape(T, D), "tm", axis=0, tiled=True,
            axis_index_groups=[[p * S + i for p in range(z.parts)] for i in range(S)],
        )
        last = moved[S - 1, rows:, 4 * rows - 2 :].T.reshape(1, -1)
        lead = moved[0, rows:, :2].T.reshape(1, -1)
        halo = (
            lax.ppermute(jnp.pad(last, ((0, 15), (0, 0))), "tm", [(i, i + S) for i in range(n - S)]),
            lax.ppermute(jnp.pad(lead, ((0, 15), (0, 0))), "tm", [(i + S, i) for i in range(n - S)]),
        )
    local_count = jnp.sum(valid_samples)[None]
    if z.direct:
        counts = [local_count] + [lax.ppermute(local_count, "seg", pairs(planes, m)) for m in range(1, planes)]
        sample_count = tree_sum(counts).astype(float32)
    else:
        sample_count = lax.psum(local_count, "seg").astype(float32)
    meta = jnp.concatenate(
        [
            jnp.stack([portion * T, lax.dynamic_index_in_dim(valid_samples, member, keepdims=False)]),
            lax.dynamic_index_in_dim(stem_weights, member, keepdims=False),
            jnp.stack([place // 2, place % 2, lax.axis_index("seg")]),
        ]
    ).astype(jnp.int32)
    meta, sample_count = lax.optimization_barrier((meta, sample_count))

    x, stream, slope, normed, sn, q, k, v, att = front(z, meta, moved, spectral_all, halo, weights)
    if z.direct:
        att, *same_second = lax.optimization_barrier((att, *same_second))
        weights.append(with_core(z, same_second))
    second = middle(z, meta, sample_count, stream, att, target, weights)
    do, mid, misc = second[:3]
    done = 2
    dq, dkv = attend_back(z, q, k, v, do, done)
    if z.direct:
        second_blocks = over_core(z, second[3], second[4])
        dq, *second_blocks = lax.optimization_barrier((dq, *second_blocks))
    first = back(
        z, done, meta, q, k, v, do, dq, dkv, x, spectral_all, halo, stream, slope, normed, sn, mid, misc, weights
    )

    if z.direct:
        second_mine = over_plane(z, second_blocks)
        send, second_mine = lax.optimization_barrier((first[1], second_mine))
        first_blocks = over_core(z, first[0], send)
        second_parts = over_planes(z, second_mine)
        first_parts = over_planes(z, over_plane(z, first_blocks))
        first_sum, second_sum, both = square_sums(z, meta, first_parts, second_parts)
        both = both + lax.ppermute(both, "tm", pairs(n, 1))
        squares = [both] + [lax.ppermute(both, "tm", pairs(n, 2 * m)) for m in range(1, n // 2)]
        result = update(z, squares, first_sum, second_sum, masters, firsts, seconds)
        return (result[0].reshape(()), sample_count.reshape(()), result[1].reshape(()), *result[2:])

    grads = (first[0], first[1], first[2], second[3], second[4], second[5], second[6])
    shards = [lax.psum_scatter(g, "tm", scatter_dimension=0, tiled=True) for g in grads]
    shards.append(lax.psum_scatter(first[3][:5], "tm", scatter_dimension=1, tiled=True))
    reduced = lax.psum(tuple(shards), "seg")
    loss_sum = lax.psum(jnp.sum(first[3][5]), ("seg", "tm"))
    squares = lax.psum(sum(jnp.sum(shard * shard) for shard in reduced), "tm")
    grad_norm = jnp.sqrt(squares)
    factor = jnp.minimum(1.0, clip_limit / (grad_norm + 1e-06))
    updated = [
        adam_update(m, f, s, g, factor, r)
        for m, f, s, g, r in zip(masters, firsts, seconds, reduced, RATES)
    ]
    return (
        loss_sum, sample_count.reshape(()), grad_norm,
        *[u[0] for u in updated], *[u[1] for u in updated], *[u[2] for u in updated],
    )


def solution(mesh):
    rows, columns = P("tm", None), P(None, "tm")
    leaves = (rows,) * 7 + (columns,)
    tokens = P("seg", "tm", None)
    return jax.shard_map(
        on_device,
        mesh=mesh,
        in_specs=(tokens, tokens, tokens, P("seg"), P("seg", None)) + leaves * 3,
        out_specs=(P(), P(), P()) + leaves * 3,
        check_vma=False,
    )
```

```python
import functools
import jax
import jax.numpy as jnp
from jax import lax
from jax.experimental import pallas as pl
from jax.experimental.pallas import tpu as pltpu
from jax.sharding import PartitionSpec as P

H = 8
STEMS = 4
SUB = 16
STEP = 10
LANES = 128

clip_limit = 0.001
beta_first = 0.9
beta_second = 0.999
learn_rate = 0.03
fast_rate = 0.5
weight_decay = 0.05
adam_epsilon = 1e-08
norm_epsilon = 1e-05

bfloat = jnp.bfloat16
float32 = jnp.float32
VMEM_LIMIT = 60 * 1024 * 1024


def mm(left, right):
    return lax.dot_general(left, right, (((1,), (0,)), ((), ())), preferred_element_type=float32)


def nt(left, right):
    return lax.dot_general(left, right, (((1,), (1,)), ((), ())), preferred_element_type=float32)


def tn(left, right):
    return lax.dot_general(left, right, (((0,), (0,)), ((), ())), preferred_element_type=float32)


def iota(shape, dim):
    return lax.broadcasted_iota(jnp.int32, shape, dim)


def norm_parts(values):
    centred = values - jnp.mean(values, -1, keepdims=True)
    scale = lax.rsqrt(jnp.mean(centred * centred, -1, keepdims=True) + norm_epsilon)
    return centred * scale, scale


def norm_back(unit, scale, gain, upstream):
    inner = upstream * gain
    value_grad = scale * (
        inner
        - jnp.mean(inner, -1, keepdims=True)
        - unit * jnp.mean(inner * unit, -1, keepdims=True)
    )
    return value_grad, jnp.sum(upstream * unit, 0, keepdims=True)


def gelu_both(values):
    upper = 0.5 * (1.0 + lax.erf(values * 0.7071067811865476))
    density = jnp.exp(-0.5 * values * values) * 0.3989422804014327
    return values * upper, upper + values * density


def spread_matrix(width, head_size):
    shape = (width, width // head_size * LANES)
    lane = iota(shape, 1)
    inside = lane % LANES
    source = (lane // LANES) * head_size + inside
    hit = jnp.logical_and(iota(shape, 0) == source, inside < head_size)
    return jnp.where(hit, 1.0, 0.0).astype(bfloat)


def with_column(block, column, head_size):
    lane = iota(block.shape, 1)
    high = column.astype(bfloat).astype(float32)
    rest = column - high
    middle = rest.astype(bfloat).astype(float32)
    low = rest - middle
    pieces = jnp.where(lane == head_size, high, jnp.where(lane == head_size + 1, middle, low))
    spare = jnp.logical_and(lane >= head_size, lane < head_size + 3)
    return jnp.where(spare, pieces, block.astype(float32)).astype(bfloat)


class Sizes:
    def __init__(self, n, planes, feats, spectral, target, conv_weight, up_weight):
        self.n = n
        self.planes = planes
        self.segments = feats.shape[0]
        self.parts = n // self.segments
        self.channels = feats.shape[2]
        self.tokens_dev = spectral.shape[1]
        self.D = spectral.shape[2]
        self.taps = conv_weight.shape[0] * n
        self.frame = self.taps // 2
        self.F = up_weight.shape[1]
        self.out = target.shape[2]
        self.tokens = self.segments * self.tokens_dev
        self.keys = self.tokens * self.parts
        self.hd = self.D // H
        self.wide = H * LANES
        self.w = self.D // n
        self.cw = self.taps // n
        self.uw = self.w * (self.F // self.D)
        self.fw = self.F // n
        self.hw = self.w * self.out // self.D
        self.first_rows = self.cw + 3 * self.w + 16
        self.second_rows = self.w + self.uw + self.fw + self.hw
        step = 16 * planes
        self.first_grads = -(-self.first_rows // step) * step
        self.second_grads = -(-self.second_rows // step) * step
        self.direct = self.parts == 1 and self.w % 16 == 0 and self.hw % 16 == 0 and self.hw > 0
        self.block = 256
        self.middle_block = 256
        self.query_block = 1024 if self.keys <= 1024 else 256


def smem():
    return pl.BlockSpec(memory_space=pltpu.SMEM)


def anywhere():
    return pl.BlockSpec(memory_space=pl.ANY)


def whole(shape):
    return pl.BlockSpec(shape, lambda i: (0,) * len(shape))


def pack_weights(z, tm_place, masters):
    D, w, O, cw = z.D, z.w, z.out, z.cw

    def kernel(place_ref, conv_r, query_r, keyval_r, out_r, up_r, down_r, head_r, gains_r, first_o, second_o):
        first_o[:cw, :] = conv_r[...].astype(bfloat)
        first_o[cw : cw + w, :] = query_r[...].astype(bfloat)
        first_o[cw + w : cw + 2 * w, :] = keyval_r[:, :D].astype(bfloat)
        first_o[cw + 2 * w : cw + 3 * w, :] = keyval_r[:, D:].astype(bfloat)
        start = place_ref[0] * w
        shift = jnp.where(iota((w, D), 1) == iota((w, D), 0) + start, 1.0, 0.0).astype(bfloat)
        placed = mm(gains_r[...].astype(bfloat), shift)
        padded = jnp.concatenate([placed, jnp.zeros((16 - placed.shape[0], D), float32)], 0)
        first_o[cw + 3 * w :, :] = padded.astype(bfloat)
        second_o[:w, :] = out_r[...].astype(bfloat)
        for c in range(z.F // D):
            second_o[w + c * w : 2 * w + c * w, :] = up_r[:, c * D : (c + 1) * D].astype(bfloat)
        row = w + z.uw
        second_o[row : row + z.fw, :] = down_r[...].astype(bfloat)
        row += z.fw
        for g in range(D // O):
            here = head_r[g * z.hw : (g + 1) * z.hw, :]
            second_o[row : row + z.hw, g * O : (g + 1) * O] = here.astype(bfloat)

    vmem = pl.BlockSpec(memory_space=pltpu.VMEM)
    return pl.pallas_call(
        kernel,
        out_shape=[
            jax.ShapeDtypeStruct((z.first_rows, D), bfloat),
            jax.ShapeDtypeStruct((z.second_rows, D), bfloat),
        ],
        in_specs=[smem()] + [vmem] * 8,
        out_specs=[vmem] * 2,
        name="pack_weights",
    )(tm_place, *masters)


def pack_tokens(z, feats, spectral, target):
    rows, D, C = z.tokens_dev, z.D, z.channels

    def kernel(f_ref, s_ref, t_ref, o_ref, buffer, in_sem, out_sem):
        arriving, leaving = [], []
        for i in range(z.segments):
            arriving.append(
                [
                    pltpu.make_async_copy(f_ref.at[i], buffer.at[i, rows:, :], in_sem.at[i, 0]),
                    pltpu.make_async_copy(s_ref.at[i], buffer.at[i, :rows, :D], in_sem.at[i, 1]),
                    pltpu.make_async_copy(t_ref.at[i], buffer.at[i, :rows, D:], in_sem.at[i, 2]),
                ]
            )
            leaving.append(pltpu.make_async_copy(buffer.at[i], o_ref.at[i], out_sem.at[i]))
            for copy in arriving[i]:
                copy.start()
        for i in range(z.segments):
            for copy in arriving[i]:
                copy.wait()
            leaving[i].start()
        for copy in leaving:
            copy.wait()

    shape = (z.segments, rows + C, 4 * rows)
    return pl.pallas_call(
        kernel,
        out_shape=jax.ShapeDtypeStruct(shape, bfloat),
        in_specs=[anywhere()] * 3,
        out_specs=anywhere(),
        scratch_shapes=[
            pltpu.VMEM(shape, bfloat),
            pltpu.SemaphoreType.DMA((z.segments, 3)),
            pltpu.SemaphoreType.DMA((z.segments,)),
        ],
        compiler_params=pltpu.CompilerParams(vmem_limit_bytes=VMEM_LIMIT),
        name="pack_tokens",
    )(feats, spectral, target)


def spectral_copies(z, source, home, sem, first):
    if z.parts > 1:
        return [pltpu.make_async_copy(source, home, sem.at[first])]
    rows = z.tokens_dev
    return [
        pltpu.make_async_copy(source.at[i, :rows, : z.D], home.at[i * rows : (i + 1) * rows, :], sem.at[first + i])
        for i in range(z.segments)
    ]


def share_copies(z, meta_ref, shares, home, rows, sem, first):
    place = meta_ref[6] * 2 + meta_ref[7]
    return [
        pltpu.make_async_copy(share.at[rows], home.at[place ^ x], sem.at[first + x])
        for x, share in enumerate(shares)
    ]


def front(z, meta, moved, spectral, halo, weights):
    D, T, K, W, B = z.D, z.tokens, z.keys, z.wide, z.block
    frame, taps, hd = z.frame, z.taps, z.hd
    half = frame // 2
    QB = z.query_block
    count = z.tokens_dev
    CB = 2 * LANES
    extra = 2 if z.parts > 1 else 0
    n_weights = z.n if z.direct else 4

    def kernel(meta_ref, *refs):
        refs = list(refs)
        frames_ref, sp_ref = refs[:2]
        before_after = refs[2 : 2 + extra]
        weight_refs = refs[2 + extra : 2 + extra + n_weights]
        refs = refs[2 + extra + n_weights :]
        (x_o, stream_o, slope_o, normed_o, sn_o, q_o, k_o, v_o, att_o) = refs[:9]
        (frames_s, sp_s, x_s, stream_s, slope_s, normed_s, sn_s) = refs[9:16]
        (conv_s, wq_s, wk_s, wv_s, q_s, k_s, v_s, in_sem, out_sem) = refs[16:25]
        refs = refs[25:]
        h = pl.program_id(0)
        outgoing = [
            pltpu.make_async_copy(src, dst, out_sem.at[i])
            for i, (src, dst) in enumerate(
                ((x_s, x_o), (stream_s, stream_o), (slope_s, slope_o), (normed_s, normed_o), (sn_s, sn_o))
            )
        ]

        @pl.when(h == 0)
        def _():
            frames_copy = pltpu.make_async_copy(frames_ref.at[:, count:, :], frames_s, in_sem.at[0])
            spectral_in = spectral_copies(z, sp_ref, sp_s, in_sem, 1)
            if z.direct:
                blob_s, wc, wqkv = refs
                blob_in = share_copies(z, meta_ref, weight_refs, blob_s, slice(0, z.first_rows), in_sem, 1 + z.segments)
                for copy in blob_in:
                    copy.start()
            for copy in spectral_in:
                copy.start()
            frames_copy.start()
            if z.direct:
                for copy in blob_in:
                    copy.wait()
                w, cw = z.w, z.cw
                total = jnp.zeros((16, D), float32)
                for j in range(z.n):
                    wc[j * cw : (j + 1) * cw, :] = blob_s[j, 0:cw, :]
                    for c in range(3):
                        first = cw + c * w
                        wqkv[j * w : (j + 1) * w, c * D : (c + 1) * D] = blob_s[j, first : first + w, :]
                    total = total + blob_s[j, cw + 3 * w : cw + 3 * w + 16, :].astype(float32)
                gain_query, gain_keys = total[0:1, :], total[1:2, :]
                parts_w = [wqkv[:, c * D : (c + 1) * D] for c in range(3)]
            else:
                wc, wq, wkv, gains_ref = weight_refs
                gain_query, gain_keys = gains_ref[0:1, :], gains_ref[1:2, :]
                parts_w = [wq[...], wkv[:, :D], wkv[:, D:]]
            spread = spread_matrix(D, hd)
            for target_s, part in zip((wq_s, wk_s, wv_s), parts_w):
                target_s[...] = mm(part, spread).astype(bfloat)
            for copy in spectral_in:
                copy.wait()

            def key_block(i, carry):
                rows = pl.ds(pl.multiple_of(i * B, B), B)
                unit, _ = norm_parts(sp_s[rows, :].astype(float32))
                sn_s[rows, :] = (unit * gain_keys).astype(bfloat)
                return carry

            lax.fori_loop(0, K // B, key_block, 0)
            outgoing[4].start()
            inside = iota((K, CB), 1) % LANES
            spare = jnp.logical_and(inside >= hd, inside < hd + 3)
            for home, part in ((k_s, wk_s), (v_s, wv_s)):
                for c in range(0, W, CB):
                    product = mm(sn_s[...], part[:, c : c + CB])
                    home[:, c : c + CB] = jnp.where(spare, -1.0, product).astype(bfloat)
            frames_copy.wait()
            shape = (4 * count, 4 * count)
            row, column = iota(shape, 0), iota(shape, 1)
            order = jnp.where(column == (row % count) * 4 + row // count, 1.0, 0.0).astype(bfloat)
            for i in range(z.segments):
                taps_rows = nt(order, frames_s[i])
                x_s[i * count : (i + 1) * count, :] = jnp.concatenate(
                    [taps_rows[j * count : (j + 1) * count, :] for j in range(4)], 1
                ).astype(bfloat)
            outgoing[0].start()
            conv_s[...] = mm(x_s[...], wc[half : half + frame, :])
            row = iota((T, D), 0)
            older = pltpu.roll(mm(x_s[:, half:], wc[:half, :]), 1, 0)
            first_row, last_row = 0.0, 0.0
            if z.parts > 1:
                first_row = mm(before_after[0][...], wc[:half, :])[0:1, :]
                last_row = mm(before_after[1][...], wc[half + frame :, :])[0:1, :]
            conv_s[...] += jnp.where(row == 0, first_row, older)
            newer = pltpu.roll(mm(x_s[:, :half], wc[half + frame :, :]), T - 1, 0)
            conv_s[...] += jnp.where(row == T - 1, last_row, newer)

            def token_block(i, carry):
                rows = pl.ds(pl.multiple_of(i * B, B), B)
                stream, slope = gelu_both(conv_s[rows, :])
                stream_s[rows, :] = stream
                slope_s[rows, :] = slope
                unit, _ = norm_parts(stream)
                normed = (unit * gain_query).astype(bfloat)
                normed_s[rows, :] = normed
                return carry

            lax.fori_loop(0, T // B, token_block, 0)
            for c in range(0, W, CB):
                q_s[:, c : c + CB] = mm(normed_s[...], wq_s[:, c : c + CB]).astype(bfloat)
            for copy in outgoing[1:4]:
                copy.start()

        lanes = pl.ds(pl.multiple_of(h * LANES, LANES), LANES)
        k_o[...] = k_s[:, lanes]
        v_o[...] = v_s[:, lanes]
        def finish(rows, count, grown, top):
            q = q_s[rows, lanes]
            mass = jnp.sum(grown, 0, keepdims=True)
            probs = (grown * (1.0 / mass)).astype(bfloat)
            total = top + jnp.log(mass)
            result = tn(v_o[...], probs)
            high = total.astype(bfloat).astype(float32)
            rest = total - high
            mid = rest.astype(bfloat).astype(float32)
            sub = iota((LANES, count), 0)
            spare = jnp.where(sub == hd, high, jnp.where(sub == hd + 1, mid, rest - mid))
            spare = jnp.where(sub < hd + 3, spare, 0.0)
            both = jnp.where(sub < hd, result, spare).T
            att_o[rows, :] = both.astype(bfloat)
            lane = iota((count, LANES), 1)
            q_o[rows, :] = jnp.where(lane < hd, q.astype(float32), both).astype(bfloat)
            return mass

        least, most = jnp.inf, 0.0
        for b in range(T // QB):
            rows = slice(b * QB, (b + 1) * QB)
            mass = finish(rows, QB, jnp.exp(nt(k_o[...], q_s[rows, lanes])), 0.0)
            least = jnp.minimum(least, jnp.min(mass))
            most = jnp.maximum(most, jnp.max(mass))
        safe = jnp.logical_and(least > 1e-20, most < 1e30)

        @pl.when(jnp.logical_not(safe))
        def _():
            def again(i, carry):
                rows = pl.ds(pl.multiple_of(i * LANES, LANES), LANES)
                scores = nt(k_o[...], q_s[rows, lanes])
                top = jnp.max(scores, 0, keepdims=True)
                finish(rows, LANES, jnp.exp(scores - top), top)
                return carry

            lax.fori_loop(0, T // LANES, again, 0)

        @pl.when(h == H - 1)
        def _():
            for copy in outgoing:
                copy.wait()

    def lanes_of(rows):
        return pl.BlockSpec((rows, LANES), lambda h: (0, h))

    in_specs = [smem(), anywhere(), anywhere()]
    args = [meta, moved, moved if z.parts == 1 else spectral]
    if z.parts > 1:
        args += list(halo)
        in_specs += [whole((16, D))] * 2
    scratch = [
        pltpu.VMEM((z.segments, z.channels, 4 * count), bfloat),
        pltpu.VMEM((K, D), bfloat),
        pltpu.VMEM((T, frame), bfloat),
        pltpu.VMEM((T, D), float32),
        pltpu.VMEM((T, D), float32),
        pltpu.VMEM((T, D), bfloat),
        pltpu.VMEM((K, D), bfloat),
        pltpu.VMEM((T, D), float32),
        pltpu.VMEM((D, W), bfloat),
        pltpu.VMEM((D, W), bfloat),
        pltpu.VMEM((D, W), bfloat),
        pltpu.VMEM((T, W), bfloat),
        pltpu.VMEM((K, W), bfloat),
        pltpu.VMEM((K, W), bfloat),
        pltpu.SemaphoreType.DMA((1 + z.segments + z.n,)),
        pltpu.SemaphoreType.DMA((5,)),
    ]
    if z.direct:
        args += weights[0]
        in_specs += [anywhere()] * z.n
        scratch += [
            pltpu.VMEM((z.n, z.first_rows, D), bfloat),
            pltpu.VMEM((taps, D), bfloat),
            pltpu.VMEM((D, 3 * D), bfloat),
        ]
    else:
        for array in (weights[0], weights[1], weights[2], weights[7]):
            args.append(array)
            in_specs.append(whole(array.shape))
    shapes = [
        ((T, frame), bfloat),
        ((T, D), float32),
        ((T, D), float32),
        ((T, D), bfloat),
        ((K, D), bfloat),
        ((T, W), bfloat),
        ((K, W), bfloat),
        ((K, W), bfloat),
        ((T, W), bfloat),
    ]
    return pl.pallas_call(
        kernel,
        grid=(H,),
        out_shape=[jax.ShapeDtypeStruct(s, d) for s, d in shapes],
        in_specs=in_specs,
        out_specs=[anywhere()] * 5 + [lanes_of(T), lanes_of(K), lanes_of(K), lanes_of(T)],
        scratch_shapes=scratch,
        compiler_params=pltpu.CompilerParams(vmem_limit_bytes=VMEM_LIMIT),
        cost_estimate=pl.CostEstimate(flops=20_000_000_000, bytes_accessed=20_000_000, transcendentals=10_000_000),
        name="front",
    )(*args)


def emit_blocks(z, meta_ref, keep_o, send_o, sources):
    chip, core, plane = meta_ref[6], meta_ref[7], meta_ref[8]
    quarter = keep_o.shape[2]

    def write(out, m, row, here, lanes):
        first = 0
        while first < here.shape[0]:
            part, inside = divmod(row + first, quarter)
            size = min(here.shape[0] - first, quarter - inside)
            out[m, part ^ plane, inside : inside + size, lanes] = here[first : first + size].astype(out.dtype)
            first += size

    for m in range(z.n // 2):
        owner = (chip ^ m) * 2
        for out, place in ((keep_o, owner + core), (send_o, owner + 1 - core)):
            row = 0
            for ref, rows, pieces in sources:
                width = ref.shape[-1]
                if width >= z.D:
                    start = pl.multiple_of(place * rows, 16)
                    for lane in range(0, width, z.D):
                        write(out, m, row, ref[pl.ds(start, rows), lane : lane + z.D], slice(0, z.D))
                        row += rows
                else:
                    size = rows // pieces
                    for g in range(pieces):
                        start = pl.multiple_of(place * rows + g * size, 16)
                        write(out, m, row, ref[pl.ds(start, size), :], slice(g * width, (g + 1) * width))
                    row += size
            if row < quarter * z.planes:
                rest = quarter * z.planes - row
                write(out, m, row, jnp.zeros((rest, z.D), float32), slice(0, z.D))


def block_shapes(z, rows):
    shape = (z.n // 2, z.planes, rows // z.planes, z.D)
    return [(shape, float32), (shape, bfloat)]


def middle(z, meta, count, stream, att, target, weights):
    D, T, W, F, O = z.D, z.tokens, z.wide, z.F, z.out
    B = z.middle_block
    hd = z.hd

    def kernel(meta_ref, count_ref, stream_ref, att_ref, target_ref, *refs):
        refs = list(refs)
        if z.direct:
            first_refs, second_refs = refs[: z.n], refs[z.n : 2 * z.n]
            refs = refs[2 * z.n :]
            do_out, mid_out, misc_o, keep_o, send_o = refs[:5]
            refs = refs[5:]
        else:
            wo, wu, wd, wh, gains_ref = refs[:5]
            do_out, mid_out, misc_o, go_s, gu_s, gd_s, gh_s = refs[5:12]
            refs = refs[12:]
        wop, att_s, stream_s, do_o, mid_o, act_s, hg_s, fin_s, fg_s, low_s, pg_s, bg_s, sem = refs[:13]
        refs = refs[13:]
        if z.direct:
            go_s, gu_s, gd_s, gh_s, blob_s, gain_s, wo, wu, wd, wh = refs

        att_copy = pltpu.make_async_copy(att_ref, att_s, sem.at[0])
        stream_copy = pltpu.make_async_copy(stream_ref, stream_s, sem.at[1])
        if z.direct:
            w, uw, fw, hw = z.w, z.uw, z.fw, z.hw
            ends = (0, w, w + uw, w + uw + fw, z.second_rows)
            pieces = [
                share_copies(z, meta_ref, second_refs, blob_s.at[:, p:q], slice(p, q), sem, 9 + c * z.n)
                for c, (p, q) in enumerate(zip(ends[:-1], ends[1:]))
            ]
            last = slice(z.first_rows - 16, z.first_rows)
            gain_in = share_copies(z, meta_ref, first_refs, gain_s, last, sem, 9 + 4 * z.n)
            for copy in pieces[0] + gain_in:
                copy.start()
        att_copy.start()
        stream_copy.start()
        if z.direct:
            for piece in pieces[1:]:
                for copy in piece:
                    copy.start()
            for copy in pieces[0] + gain_in:
                copy.wait()
            total = jnp.zeros((16, D), float32)
            for j in range(z.n):
                wo[j * w : (j + 1) * w, :] = blob_s[j, 0:w, :]
                total = total + gain_s[j].astype(float32)
        else:
            total = gains_ref[...]
        wop[...] = tn(spread_matrix(D, hd), wo[...]).astype(bfloat)
        misc_o[...] = jnp.zeros_like(misc_o)
        gain_ffn, scale_attn, scale_ffn = total[2:3, :], total[3:4, :], total[4:5, :]
        base, valid = meta_ref[0], meta_ref[1]
        samples = count_ref[0]
        att_copy.wait()
        stream_copy.wait()
        if z.direct:
            for copy in pieces[1]:
                copy.wait()
            for j in range(z.n):
                for c in range(F // D):
                    first = w + c * w
                    wu[j * w : (j + 1) * w, c * D : (c + 1) * D] = blob_s[j, first : first + w, :]
        if z.direct:
            for copy in pieces[2] + pieces[3]:
                copy.wait()
            for j in range(z.n):
                wd[j * fw : (j + 1) * fw, :] = blob_s[j, w + uw : w + uw + fw, :]
                for g in range(D // O):
                    start = j * w + g * hw
                    wh[start : start + hw, :] = blob_s[j, w + uw + fw :, g * O : (g + 1) * O]
        chunks = B // z.tokens_dev

        def block(i, carry):
            rows = pl.ds(pl.multiple_of(i * B, B), B)
            branch = mm(att_s[rows, :], wop[...])
            stream_mid = stream_s[rows, :] + scale_attn * branch
            unit, scale = norm_parts(stream_mid)
            ffn_in = (unit * gain_ffn).astype(bfloat)
            fin_s[rows, :] = ffn_in
            hidden = mm(ffn_in, wu[...])
            active, slope = gelu_both(hidden)
            active = active.astype(bfloat)
            act_s[rows, :] = active
            ffn_out = mm(active, wd[...])
            stream_low = (stream_mid + scale_ffn * ffn_out).astype(bfloat)
            low_s[rows, :] = stream_low
            predicted = mm(stream_low, wh[...])
            column = iota((B, O), 1)
            position = (base + i * B + iota((B, O), 0)) * SUB + column % SUB
            stem = column // (2 * SUB)
            weight = jnp.zeros((B, O), float32)
            for k in range(STEMS):
                weight = jnp.where(stem == k, meta_ref[2 + k].astype(float32), weight)
            weight = jnp.where(position < valid, weight, 0.0)
            error = predicted - target_ref[pl.ds(i * chunks, chunks)].reshape(B, O).astype(float32)
            root = jnp.sqrt(error * error + 1.0)
            misc_o[5:6, :O] += jnp.sum(weight * (root - 1.0), 0, keepdims=True)
            predicted_grad = (weight * error / root / samples).astype(bfloat)
            pg_s[rows, :] = predicted_grad
            end_grad = nt(predicted_grad, wh[...])
            misc_o[4:5, :] += jnp.sum(end_grad * ffn_out, 0, keepdims=True)
            ffn_grad = (scale_ffn * end_grad).astype(bfloat)
            fg_s[rows, :] = ffn_grad
            hidden_grad = (nt(ffn_grad, wd[...]) * slope).astype(bfloat)
            hg_s[rows, :] = hidden_grad
            mid_part, gain_grad = norm_back(unit, scale, gain_ffn, nt(hidden_grad, wu[...]))
            misc_o[2:3, :] += gain_grad
            mid_grad = end_grad + mid_part
            mid_o[rows, :] = mid_grad
            misc_o[3:4, :] += jnp.sum(mid_grad * branch, 0, keepdims=True)
            branch_grad = (scale_attn * mid_grad).astype(bfloat)
            bg_s[rows, :] = branch_grad
            att_grad = nt(branch_grad, wop[...]).astype(bfloat)
            for h in range(H):
                lanes = slice(h * LANES, (h + 1) * LANES)
                one = att_grad[:, lanes].astype(float32)
                delta = jnp.sum(one * att_s[rows, lanes].astype(float32), -1, keepdims=True)
                do_o[rows, lanes] = with_column(one, delta, hd)
            return carry

        lax.fori_loop(0, T // B, block, 0)
        outgoing = [
            pltpu.make_async_copy(do_o, do_out, sem.at[7]),
            pltpu.make_async_copy(mid_o, mid_out, sem.at[8]),
        ]
        for copy in outgoing:
            copy.start()
        spare_grad = tn(att_s[...], bg_s[...])
        for h in range(H):
            go_s[h * hd : (h + 1) * hd, :] = spare_grad[h * LANES : h * LANES + hd, :]
        gu_s[...] = tn(fin_s[...], hg_s[...])
        gd_s[...] = tn(act_s[...], fg_s[...])
        gh_s[...] = tn(low_s[...], pg_s[...])
        if z.direct:
            emit_blocks(
                z,
                meta_ref,
                keep_o,
                send_o,
                ((go_s, z.w, 1), (gu_s, z.w, 1), (gd_s, z.fw, 1), (gh_s, z.w, D // O)),
            )
        for copy in outgoing:
            copy.wait()

    if z.parts == 1:
        target_spec = pl.BlockSpec((z.segments, z.tokens_dev, O), lambda i: (0, 0, D // O))
    else:
        target_spec = whole(target.shape)
    in_specs = [smem(), smem(), anywhere(), anywhere(), target_spec]
    args = [meta, count, stream, att, target]
    scratch = [
        pltpu.VMEM((W, D), bfloat),
        pltpu.VMEM((T, W), bfloat),
        pltpu.VMEM((T, D), float32),
        pltpu.VMEM((T, W), bfloat),
        pltpu.VMEM((T, D), float32),
        pltpu.VMEM((T, F), bfloat),
        pltpu.VMEM((T, F), bfloat),
        pltpu.VMEM((T, D), bfloat),
        pltpu.VMEM((T, D), bfloat),
        pltpu.VMEM((T, D), bfloat),
        pltpu.VMEM((T, O), bfloat),
        pltpu.VMEM((T, D), bfloat),
        pltpu.SemaphoreType.DMA((9 + 5 * z.n,)),
    ]
    shapes = [((T, W), bfloat), ((T, D), float32), ((8, D), float32)]
    grads = [((D, D), float32), ((D, F), float32), ((F, D), float32), ((D, O), float32)]
    if z.direct:
        args += weights[0] + weights[1]
        in_specs += [anywhere()] * (2 * z.n)
        scratch += [pltpu.VMEM(s, d) for s, d in grads] + [
            pltpu.VMEM((z.n, z.second_rows, D), bfloat),
            pltpu.VMEM((z.n, 16, D), bfloat),
            pltpu.VMEM((D, D), bfloat),
            pltpu.VMEM((D, F), bfloat),
            pltpu.VMEM((F, D), bfloat),
            pltpu.VMEM((D, O), bfloat),
        ]
        shapes += block_shapes(z, z.second_grads)
    else:
        for array in weights[3:]:
            args.append(array)
            in_specs.append(whole(array.shape))
        shapes += grads
    return pl.pallas_call(
        kernel,
        grid=(1,),
        out_shape=[jax.ShapeDtypeStruct(s, d) for s, d in shapes],
        in_specs=in_specs,
        out_specs=[anywhere(), anywhere()] + [whole(s) for s, d in shapes[2:]],
        scratch_shapes=scratch,
        compiler_params=pltpu.CompilerParams(vmem_limit_bytes=VMEM_LIMIT),
        cost_estimate=pl.CostEstimate(flops=20_000_000_000, bytes_accessed=20_000_000, transcendentals=4_000_000),
        name="middle",
    )(*args)


def head_back(z, q_ref, k_ref, v_ref, do_ref, put_query, dk_s, dv_s):
    T, hd = z.tokens, z.hd
    QB = 256 if z.keys <= 1024 else 128
    dk_s[...] = jnp.zeros_like(dk_s)
    dv_s[...] = jnp.zeros_like(dv_s)

    def block(i, carry):
        for b in range(2):
            rows = pl.ds(pl.multiple_of((i * 2 + b) * QB, QB), QB)
            q, do = q_ref[rows, :], do_ref[rows, :]
            probs = jnp.exp(nt(q, k_ref[...]))
            score_grad = (probs * nt(do, v_ref[...])).astype(bfloat)
            low = probs.astype(bfloat)
            put_query(rows, mm(score_grad, k_ref[...]).astype(bfloat))
            dk_s[...] += tn(q, score_grad)[:hd, :]
            dv_s[...] += tn(do, low)[:hd, :]
        return carry

    lax.fori_loop(0, T // (2 * QB), block, 0)
    return dk_s[...].astype(bfloat), dv_s[...].astype(bfloat)


def attend_back(z, q, k, v, do, heads):
    T, K, W, D = z.tokens, z.keys, z.wide, z.D
    hd = z.hd

    def kernel(q_ref, k_ref, v_ref, do_ref, dq_o, dkv_o, dk_s, dv_s):
        def put_query(rows, value):
            dq_o[rows, :] = value

        dkv_o[0], dkv_o[1] = head_back(z, q_ref, k_ref, v_ref, do_ref, put_query, dk_s, dv_s)

    def lanes(rows):
        return pl.BlockSpec((rows, LANES), lambda h: (0, h))

    return pl.pallas_call(
        kernel,
        grid=(heads,),
        out_shape=[
            jax.ShapeDtypeStruct((T, heads * LANES), bfloat),
            jax.ShapeDtypeStruct((2, heads * hd, K), bfloat),
        ],
        in_specs=[lanes(T), lanes(K), lanes(K), lanes(T)],
        out_specs=[lanes(T), pl.BlockSpec((2, hd, K), lambda h: (0, h, 0))],
        scratch_shapes=[pltpu.VMEM((hd, K), float32)] * 2,
        compiler_params=pltpu.CompilerParams(vmem_limit_bytes=VMEM_LIMIT),
        cost_estimate=pl.CostEstimate(
            flops=heads * 4_000_000_000, bytes_accessed=12_000_000, transcendentals=heads * 1_000_000
        ),
        name="attend_back",
    )(q, k, v, do)


def back(z, done, meta, q, k, v, do, dq, dkv, x, spectral, halo, stream, slope, normed, sn, mid, misc, weights):
    D, T, K, W, B, O = z.D, z.tokens, z.keys, z.wide, z.block, z.out
    frame, taps, hd = z.frame, z.taps, z.hd
    half = frame // 2
    steps = H - done
    extra = 2 if z.parts > 1 else 0
    n_weights = z.n if z.direct else 3
    n_out = 2 if z.direct else 4

    def kernel(meta_ref, q_ref, k_ref, v_ref, do_ref, misc_ref, *refs):
        refs = list(refs)
        before_after = refs[:extra]
        remote = refs[extra : extra + 9]
        refs = refs[extra + 9 :]
        weight_refs, refs = refs[:n_weights], refs[n_weights:]
        outs, refs = refs[:n_out], refs[n_out:]
        (dq_s, dkv_s, x_ref, sp_ref, stream_ref, slope_ref, normed_ref, sn_ref, mid_ref) = refs[:9]
        refs = refs[9:]
        cg_s, dn_s, dqc_s, dkvt_s, dk_s, dv_s, sem = refs[:7]
        refs = refs[7:]
        if z.direct:
            gc_s, gq_s, gkv_s, misc_s, place_s, blob_s, wq, wkv = refs
        else:
            gc_s, gq_s, gkv_s, misc_s = outs
            wq, wkv, gains_ref = weight_refs
        i = pl.program_id(0)
        old = done * LANES
        homes = [dq_s.at[:, :old], dkv_s.at[:, : done * hd]] + [
            x_ref, sp_ref, stream_ref, slope_ref, normed_ref, sn_ref, mid_ref
        ]
        copies = [
            pltpu.make_async_copy(a, b, sem.at[c])
            for c, (a, b) in enumerate(zip(remote, homes))
            if c != 3
        ]
        copies += spectral_copies(z, remote[3], sp_ref, sem, 10)
        if z.direct:
            copies += share_copies(
                z, meta_ref, weight_refs, blob_s, slice(z.cw, z.first_rows), sem, 10 + z.segments
            )

        @pl.when(i == 0)
        def _():
            for copy in copies:
                copy.start()

        lanes = pl.ds(pl.multiple_of((i + done) * LANES, LANES), LANES)

        def put_query(rows, value):
            dq_s[rows, lanes] = value

        dk, dv = head_back(z, q_ref, k_ref, v_ref, do_ref, put_query, dk_s, dv_s)
        here = pl.ds(pl.multiple_of((i + done) * hd, 16), hd)
        dkv_s[0, here, :] = dk
        dkv_s[1, here, :] = dv

        @pl.when(i == steps - 1)
        def _():
            for copy in copies:
                copy.wait()
            if z.direct:
                w = z.w
                total = jnp.zeros((16, D), float32)
                for j in range(z.n):
                    here = slice(j * w, (j + 1) * w)
                    wq[here, :] = blob_s[j, 0:w, :]
                    wkv[here, :D] = blob_s[j, w : 2 * w, :]
                    wkv[here, D:] = blob_s[j, 2 * w : 3 * w, :]
                    total = total + blob_s[j, 3 * w :, :].astype(float32)
            else:
                total = gains_ref[...]
            gain_query = total[0:1, :]
            misc_s[...] = misc_ref[...]
            dqc_s[...] = nt(dq_s[...], spread_matrix(D, hd)).astype(bfloat)
            dkvt_s[:, :D] = dkv_s[0].T
            dkvt_s[:, D:] = dkv_s[1].T
            gkv_s[...] = tn(sn_ref[...], dkvt_s[...])
            gq_s[...] = tn(normed_ref[...], dqc_s[...])

            for c in range(K // T):
                cg_s[...] = nt(dkvt_s[c * T : (c + 1) * T, :], wkv[...])

                def key_block(i, carry):
                    rows = pl.ds(pl.multiple_of(i * B, B), B)
                    source = pl.ds(pl.multiple_of(c * T + i * B, B), B)
                    unit, _ = norm_parts(sp_ref[source, :].astype(float32))
                    misc_s[1:2, :] += jnp.sum(cg_s[rows, :] * unit, 0, keepdims=True)
                    return carry

                lax.fori_loop(0, T // B, key_block, 0)
            dn_s[...] = nt(dqc_s[...], wq[...])

            def token_block(i, carry):
                rows = pl.ds(pl.multiple_of(i * B, B), B)
                unit, scale = norm_parts(stream_ref[rows, :])
                part, gain_grad = norm_back(unit, scale, gain_query, dn_s[rows, :])
                misc_s[0:1, :] += gain_grad
                conv_grad = (mid_ref[rows, :] + part) * slope_ref[rows, :]
                cg_s[rows, :] = conv_grad.astype(bfloat).astype(float32)
                return carry

            lax.fori_loop(0, T // B, token_block, 0)
            conv_grad = cg_s[...]
            gc_s[half : half + frame, :] = tn(x_ref[...], conv_grad.astype(bfloat))
            row = iota((T, D), 0)
            later = jnp.where(row == T - 1, 0.0, pltpu.roll(conv_grad, T - 1, 0)).astype(bfloat)
            gc_s[:half, :] = tn(x_ref[:, half:], later)
            sooner = jnp.where(row == 0, 0.0, pltpu.roll(conv_grad, 1, 0)).astype(bfloat)
            gc_s[half + frame :, :] = tn(x_ref[:, :half], sooner)
            if z.parts > 1:
                first = iota((16, D), 0) == 0
                top = jnp.where(first, conv_grad[0:16, :], 0.0).astype(bfloat)
                gc_s[:half, :] += tn(before_after[0][...], top)
                tail = jnp.where(first, pltpu.roll(conv_grad[T - 16 :, :], 1, 0), 0.0)
                gc_s[half + frame :, :] += tn(before_after[1][...], tail.astype(bfloat))
            if z.direct:
                for j in range(z.n):
                    row, lane = iota((D, LANES), 0), iota((D, LANES), 1)
                    hit = jnp.logical_and(row == lane + j * z.w, lane < z.w)
                    chosen = lax.dot_general(
                        misc_s[...], jnp.where(hit, 1.0, 0.0), (((1,), (0,)), ((), ())),
                        precision=lax.Precision.HIGHEST, preferred_element_type=float32,
                    )
                    low_rows = jnp.where(iota((8, LANES), 0) == 5, misc_s[:, :LANES], chosen)
                    place_s[j * 16 : (j + 1) * 16, :] = jnp.zeros((16, D), float32)
                    place_s[j * 16 : j * 16 + 8, :LANES] = low_rows
                emit_blocks(
                    z, meta_ref, outs[0], outs[1],
                    ((gc_s, z.cw, 1), (gq_s, z.w, 1), (gkv_s, z.w, 1), (place_s, 16, 1)),
                )

    def lanes_of(rows):
        return pl.BlockSpec((rows, LANES), lambda i: (0, i + done))

    args = [meta, q, k, v, do, misc]
    in_specs = [smem(), lanes_of(T), lanes_of(K), lanes_of(K), lanes_of(T), whole(misc.shape)]
    if z.parts > 1:
        args += list(halo)
        in_specs += [whole((16, D))] * 2
    remote = (dq, dkv, x, spectral, stream, slope, normed, sn, mid)
    args += list(remote)
    in_specs += [anywhere()] * 9
    scratch = [pltpu.VMEM((T, W), bfloat), pltpu.VMEM((2, D, K), bfloat)]
    homes = (x.shape, (K, D)) + tuple(a.shape for a in remote[4:])
    scratch += [pltpu.VMEM(s, a.dtype) for s, a in zip(homes, remote[2:])]
    scratch += [
        pltpu.VMEM((T, D), float32),
        pltpu.VMEM((T, D), float32),
        pltpu.VMEM((T, D), bfloat),
        pltpu.VMEM((K, 2 * D), bfloat),
        pltpu.VMEM((hd, K), float32),
        pltpu.VMEM((hd, K), float32),
        pltpu.SemaphoreType.DMA((10 + z.segments + z.n,)),
    ]
    grads = [((taps, D), float32), ((D, D), float32), ((D, 2 * D), float32), ((8, D), float32)]
    if z.direct:
        args += weights[0]
        in_specs += [anywhere()] * z.n
        scratch += [pltpu.VMEM(s, d) for s, d in grads] + [
            pltpu.VMEM((z.n * 16, D), float32),
            pltpu.VMEM((z.n, z.first_rows - z.cw, D), bfloat),
            pltpu.VMEM((D, D), bfloat),
            pltpu.VMEM((D, 2 * D), bfloat),
        ]
        shapes = block_shapes(z, z.first_grads)
    else:
        for array in (weights[1], weights[2], weights[7]):
            args.append(array)
            in_specs.append(whole(array.shape))
        shapes = grads
    return pl.pallas_call(
        kernel,
        grid=(steps,),
        out_shape=[jax.ShapeDtypeStruct(s, d) for s, d in shapes],
        in_specs=in_specs,
        out_specs=[whole(s) for s, d in shapes],
        scratch_shapes=scratch,
        compiler_params=pltpu.CompilerParams(vmem_limit_bytes=VMEM_LIMIT),
        cost_estimate=pl.CostEstimate(flops=30_000_000_000, bytes_accessed=20_000_000, transcendentals=8_000_000),
        name="back",
    )(*args)


def pairs(count, mask):
    return [(i, i ^ mask) for i in range(count)]


def tree_sum(values):
    while len(values) > 1:
        values = [values[i] + values[i + 1] for i in range(0, len(values), 2)]
    return values[0]


def from_chips(z, own):
    return [own] + [lax.ppermute(own, "tm", pairs(z.n, 2 * m)) for m in range(1, z.n // 2)]


def with_core(z, same):
    other = [lax.ppermute(share, "tm", pairs(z.n, 1)) for share in same]
    return [share for pair in zip(same, other) for share in pair]


def over_core(z, keep, send):
    there = lax.ppermute(send, "tm", pairs(z.n, 1))
    sums = [keep[m] + there[m].astype(float32) for m in range(z.n // 2)]
    return sums[:1] + [value.astype(bfloat) for value in sums[1:]]


def over_plane(z, blocks):
    mine = blocks[:1]
    for m in range(1, z.n // 2):
        mine.append(lax.ppermute(blocks[m], "tm", pairs(z.n, 2 * m)).astype(float32))
    return tree_sum(mine)


def over_planes(z, mine):
    parts = [mine[0]]
    for m in range(1, z.planes):
        there = lax.ppermute(mine[m].astype(bfloat), "seg", pairs(z.planes, m))
        parts.append(there.astype(float32))
    low = tree_sum(parts).astype(bfloat)
    return [low] + [lax.ppermute(low, "seg", pairs(z.planes, m)) for m in range(1, z.planes)]


def adam_update(master, first, second, grad, factor, rate):
    clipped = grad * factor
    first_new = beta_first * first + (1.0 - beta_first) * clipped
    second_new = beta_second * second + (1.0 - beta_second) * clipped * clipped
    moment_hat = first_new / (1.0 - beta_first**STEP)
    square_hat = second_new / (1.0 - beta_second**STEP)
    master_new = master - rate * (
        moment_hat / (jnp.sqrt(square_hat) + adam_epsilon) + weight_decay * master
    )
    return (master_new, first_new, second_new)


RATES = (
    learn_rate, learn_rate, learn_rate, fast_rate, learn_rate, learn_rate, learn_rate, fast_rate,
)


def gather_quarters(z, meta_ref, refs, out_ref):
    quarter = refs[0].shape[0]
    for m, ref in enumerate(refs):
        start = pl.multiple_of((meta_ref[8] ^ m) * quarter, 16)
        out_ref[pl.ds(start, quarter), :] = ref[...].astype(float32)


def square_sums(z, meta, first, second):
    D = z.D

    def kernel(meta_ref, *refs):
        planes = z.planes
        a_o, b_o, sq_o = refs[2 * planes :]
        gather_quarters(z, meta_ref, refs[:planes], a_o)
        gather_quarters(z, meta_ref, refs[planes : 2 * planes], b_o)
        loss_row = z.cw + 3 * z.w + 5
        total = jnp.zeros((8, D), float32)
        for ref, skip in ((a_o, loss_row), (b_o, -1)):
            for r in range(0, ref.shape[0], 8):
                here = ref[r : r + 8, :]
                if r <= skip < r + 8:
                    here = jnp.where(iota((8, D), 0) == skip - r, 0.0, here)
                total = total + here * here
        sq_o[0:8, :] = total[:, :LANES] + total[:, LANES : 2 * LANES] + total[:, 2 * LANES :]
        loss = a_o[loss_row - 5 : loss_row + 3, :LANES]
        sq_o[8:16, :] = jnp.where(iota((8, LANES), 0) == 5, loss * (1.0 / z.n), 0.0)

    vmem = pl.BlockSpec(memory_space=pltpu.VMEM)
    shapes = [(z.first_grads, D), (z.second_grads, D), (16, LANES)]
    return pl.pallas_call(
        kernel,
        out_shape=[jax.ShapeDtypeStruct(s, float32) for s in shapes],
        in_specs=[smem()] + [vmem] * (2 * z.planes),
        out_specs=[vmem] * 3,
        compiler_params=pltpu.CompilerParams(vmem_limit_bytes=16 * 1024 * 1024),
        name="square_sums",
    )(meta, *first, *second)


def update(z, squares, first_sum, second_sum, masters, firsts, seconds):
    D, O, w, cw = z.D, z.out, z.w, z.cw
    given = len(squares)

    def kernel(*refs):
        sq_refs = refs[:given]
        a_ref, b_ref = refs[given : given + 2]
        ins = refs[given + 2 : given + 26]
        loss_o, norm_o = refs[given + 26 : given + 28]
        outs = refs[given + 28 :]
        sums = tree_sum([ref[...] for ref in sq_refs])
        norm = jnp.sqrt(jnp.sum(sums[0:8, :], keepdims=True))
        loss_o[...] = jnp.sum(sums[8:16, :], keepdims=True)
        norm_o[...] = norm
        factor = jnp.minimum(1.0, clip_limit / (norm + 1e-06))
        places = {
            0: [(a_ref, 0, cw, 0)],
            1: [(a_ref, cw, w, 0)],
            2: [(a_ref, cw + w + c * w, w, c * D) for c in range(2)],
            3: [(b_ref, 0, w, 0)],
            4: [(b_ref, w + c * w, w, c * D) for c in range(z.F // D)],
            5: [(b_ref, w + z.uw, z.fw, 0)],
        }

        def step(index, here, grad):
            values = adam_update(
                ins[index][here], ins[8 + index][here], ins[16 + index][here], grad, factor, RATES[index]
            )
            for kind, value in enumerate(values):
                outs[8 * kind + index][here] = value

        def block(index, ref, start, lane):
            def body(i, carry):
                here = pl.ds(pl.multiple_of(i * 16, 16), 16)
                step(index, (here, slice(lane, lane + D)), ref[pl.ds(pl.multiple_of(start + i * 16, 16), 16), :])
                return carry

            return body

        for index, pieces in places.items():
            for ref, start, count, lane in pieces:
                lax.fori_loop(0, count // 16, block(index, ref, start, lane), 0)
        start = w + z.uw + z.fw
        for g in range(D // O):
            here = (slice(g * z.hw, (g + 1) * z.hw), slice(0, O))
            step(6, here, b_ref[start : start + z.hw, g * O : (g + 1) * O])
        gains = a_ref[cw + 3 * w : cw + 3 * w + 8, :][:5, :w]
        step(7, (slice(0, 5), slice(0, w)), gains)

    vmem = pl.BlockSpec(memory_space=pltpu.VMEM)
    outs = [jax.ShapeDtypeStruct((1, 1), float32)] * 2
    outs += [jax.ShapeDtypeStruct(m.shape, float32) for m in masters] * 3
    return pl.pallas_call(
        kernel,
        out_shape=outs,
        in_specs=[vmem] * (given + 26),
        out_specs=[vmem] * 26,
        compiler_params=pltpu.CompilerParams(vmem_limit_bytes=20 * 1024 * 1024),
        name="update",
    )(*squares, first_sum, second_sum, *masters, *firsts, *seconds)


def on_device(*arguments):
    feats, spectral, target, valid_samples, stem_weights = arguments[:5]
    masters, firsts, seconds = arguments[5:13], arguments[13:21], arguments[21:29]
    n = lax.axis_size("tm")
    planes = lax.axis_size("seg")
    z = Sizes(n, planes, feats, spectral, target, masters[0], masters[4])
    S, T, D = z.segments, z.tokens, z.D
    place = lax.axis_index("tm")
    portion, member = place // S, place % S

    if z.direct:
        blobs = pack_weights(z, jnp.reshape(place, (1,)).astype(jnp.int32), masters)
        same_first = from_chips(z, blobs[0])
    else:
        weights = [lax.all_gather(a.astype(bfloat), "tm", axis=0, tiled=True) for a in masters[:7]]
        gains = lax.all_gather(masters[7].astype(bfloat), "tm", axis=1, tiled=True)
        weights.append(jnp.pad(gains.astype(float32), ((0, 3), (0, 0))))
    groups = None if z.parts == 1 else [[p * S + i for i in range(S)] for p in range(z.parts)]

    packed = pack_tokens(z, jnp.transpose(feats, (0, 2, 1)), spectral, target)
    if z.direct:
        packed, *same_first = lax.optimization_barrier((packed, *same_first))
    moved = lax.all_to_all(packed, "tm", 0, 0, axis_index_groups=groups, tiled=True)
    if z.direct:
        weights = [with_core(z, same_first)]
        blob, valid_samples, _ = lax.optimization_barrier((blobs[1], valid_samples, weights[0][1]))
        same_second = from_chips(z, blob)
    rows = z.tokens_dev
    spectral_all, target, halo = moved, moved, None
    if z.parts > 1:
        target = moved[:, :rows, D:]
        spectral_all = lax.all_gather(
            moved[:, :rows, :D].reshape(T, D), "tm", axis=0, tiled=True,
            axis_index_groups=[[p * S + i for p in range(z.parts)] for i in range(S)],
        )
        last = moved[S - 1, rows:, 4 * rows - 2 :].T.reshape(1, -1)
        lead = moved[0, rows:, :2].T.reshape(1, -1)
        halo = (
            lax.ppermute(jnp.pad(last, ((0, 15), (0, 0))), "tm", [(i, i + S) for i in range(n - S)]),
            lax.ppermute(jnp.pad(lead, ((0, 15), (0, 0))), "tm", [(i + S, i) for i in range(n - S)]),
        )
    local_count = jnp.sum(valid_samples)[None]
    if z.direct:
        counts = [local_count] + [lax.ppermute(local_count, "seg", pairs(planes, m)) for m in range(1, planes)]
        sample_count = tree_sum(counts).astype(float32)
    else:
        sample_count = lax.psum(local_count, "seg").astype(float32)
    meta = jnp.concatenate(
        [
            jnp.stack([portion * T, lax.dynamic_index_in_dim(valid_samples, member, keepdims=False)]),
            lax.dynamic_index_in_dim(stem_weights, member, keepdims=False),
            jnp.stack([place // 2, place % 2, lax.axis_index("seg")]),
        ]
    ).astype(jnp.int32)
    meta, sample_count = lax.optimization_barrier((meta, sample_count))

    x, stream, slope, normed, sn, q, k, v, att = front(z, meta, moved, spectral_all, halo, weights)
    if z.direct:
        att, *same_second = lax.optimization_barrier((att, *same_second))
        weights.append(with_core(z, same_second))
    second = middle(z, meta, sample_count, stream, att, target, weights)
    do, mid, misc = second[:3]
    done = 2
    dq, dkv = attend_back(z, q, k, v, do, done)
    if z.direct:
        second_blocks = over_core(z, second[3], second[4])
        dq, *second_blocks = lax.optimization_barrier((dq, *second_blocks))
    first = back(
        z, done, meta, q, k, v, do, dq, dkv, x, spectral_all, halo, stream, slope, normed, sn, mid, misc, weights
    )

    if z.direct:
        second_mine = over_plane(z, second_blocks)
        send, second_mine = lax.optimization_barrier((first[1], second_mine))
        first_blocks = over_core(z, first[0], send)
        second_parts = over_planes(z, second_mine)
        first_parts = over_planes(z, over_plane(z, first_blocks))
        first_sum, second_sum, both = square_sums(z, meta, first_parts, second_parts)
        both = both + lax.ppermute(both, "tm", pairs(n, 1))
        squares = [both] + [lax.ppermute(both, "tm", pairs(n, 2 * m)) for m in range(1, n // 2)]
        result = update(z, squares, first_sum, second_sum, masters, firsts, seconds)
        return (result[0].reshape(()), sample_count.reshape(()), result[1].reshape(()), *result[2:])

    grads = (first[0], first[1], first[2], second[3], second[4], second[5], second[6])
    shards = [lax.psum_scatter(g, "tm", scatter_dimension=0, tiled=True) for g in grads]
    shards.append(lax.psum_scatter(first[3][:5], "tm", scatter_dimension=1, tiled=True))
    reduced = lax.psum(tuple(shards), "seg")
    loss_sum = lax.psum(jnp.sum(first[3][5]), ("seg", "tm"))
    squares = lax.psum(sum(jnp.sum(shard * shard) for shard in reduced), "tm")
    grad_norm = jnp.sqrt(squares)
    factor = jnp.minimum(1.0, clip_limit / (grad_norm + 1e-06))
    updated = [
        adam_update(m, f, s, g, factor, r)
        for m, f, s, g, r in zip(masters, firsts, seconds, reduced, RATES)
    ]
    return (
        loss_sum, sample_count.reshape(()), grad_norm,
        *[u[0] for u in updated], *[u[1] for u in updated], *[u[2] for u in updated],
    )


def solution(mesh):
    rows, columns = P("tm", None), P(None, "tm")
    leaves = (rows,) * 7 + (columns,)
    tokens = P("seg", "tm", None)
    return jax.shard_map(
        on_device,
        mesh=mesh,
        in_specs=(tokens, tokens, tokens, P("seg"), P("seg", None)) + leaves * 3,
        out_specs=(P(), P(), P()) + leaves * 3,
        check_vma=False,
    )
```

```python
import functools
import jax
import jax.numpy as jnp
from jax import lax
from jax.experimental import pallas as pl
from jax.experimental.pallas import tpu as pltpu
from jax.sharding import PartitionSpec as P

H = 8
STEMS = 4
SUB = 16
STEP = 10
LANES = 128

clip_limit = 0.001
beta_first = 0.9
beta_second = 0.999
learn_rate = 0.03
fast_rate = 0.5
weight_decay = 0.05
adam_epsilon = 1e-08
norm_epsilon = 1e-05

bfloat = jnp.bfloat16
float32 = jnp.float32
VMEM_LIMIT = 60 * 1024 * 1024


def mm(left, right):
    return lax.dot_general(left, right, (((1,), (0,)), ((), ())), preferred_element_type=float32)


def nt(left, right):
    return lax.dot_general(left, right, (((1,), (1,)), ((), ())), preferred_element_type=float32)


def tn(left, right):
    return lax.dot_general(left, right, (((0,), (0,)), ((), ())), preferred_element_type=float32)


def iota(shape, dim):
    return lax.broadcasted_iota(jnp.int32, shape, dim)


def norm_parts(values):
    centred = values - jnp.mean(values, -1, keepdims=True)
    scale = lax.rsqrt(jnp.mean(centred * centred, -1, keepdims=True) + norm_epsilon)
    return centred * scale, scale


def norm_back(unit, scale, gain, upstream):
    inner = upstream * gain
    value_grad = scale * (
        inner
        - jnp.mean(inner, -1, keepdims=True)
        - unit * jnp.mean(inner * unit, -1, keepdims=True)
    )
    return value_grad, jnp.sum(upstream * unit, 0, keepdims=True)


def gelu_both(values):
    upper = 0.5 * (1.0 + lax.erf(values * 0.7071067811865476))
    density = jnp.exp(-0.5 * values * values) * 0.3989422804014327
    return values * upper, upper + values * density


def spread_matrix(width, head_size):
    shape = (width, width // head_size * LANES)
    lane = iota(shape, 1)
    inside = lane % LANES
    source = (lane // LANES) * head_size + inside
    hit = jnp.logical_and(iota(shape, 0) == source, inside < head_size)
    return jnp.where(hit, 1.0, 0.0).astype(bfloat)


def with_column(block, column, head_size):
    lane = iota(block.shape, 1)
    high = column.astype(bfloat).astype(float32)
    rest = column - high
    middle = rest.astype(bfloat).astype(float32)
    low = rest - middle
    pieces = jnp.where(lane == head_size, high, jnp.where(lane == head_size + 1, middle, low))
    spare = jnp.logical_and(lane >= head_size, lane < head_size + 3)
    return jnp.where(spare, pieces, block.astype(float32)).astype(bfloat)


class Sizes:
    def __init__(self, n, planes, feats, spectral, target, conv_weight, up_weight):
        self.n = n
        self.planes = planes
        self.segments = feats.shape[0]
        self.parts = n // self.segments
        self.channels = feats.shape[2]
        self.tokens_dev = spectral.shape[1]
        self.D = spectral.shape[2]
        self.taps = conv_weight.shape[0] * n
        self.frame = self.taps // 2
        self.F = up_weight.shape[1]
        self.out = target.shape[2]
        self.tokens = self.segments * self.tokens_dev
        self.keys = self.tokens * self.parts
        self.hd = self.D // H
        self.wide = H * LANES
        self.w = self.D // n
        self.cw = self.taps // n
        self.uw = self.w * (self.F // self.D)
        self.fw = self.F // n
        self.hw = self.w * self.out // self.D
        self.first_rows = self.cw + 3 * self.w + 16
        self.second_rows = self.w + self.uw + self.fw + self.hw
        step = 16 * planes
        self.first_grads = -(-self.first_rows // step) * step
        self.second_grads = -(-self.second_rows // step) * step
        self.direct = self.parts == 1 and self.w % 16 == 0 and self.hw % 16 == 0 and self.hw > 0
        self.block = 256
        self.middle_block = 512
        self.query_block = 1024 if self.keys <= 1024 else 256


def smem():
    return pl.BlockSpec(memory_space=pltpu.SMEM)


def anywhere():
    return pl.BlockSpec(memory_space=pl.ANY)


def whole(shape):
    return pl.BlockSpec(shape, lambda i: (0,) * len(shape))


def pack_weights(z, tm_place, masters):
    D, w, O, cw = z.D, z.w, z.out, z.cw

    def kernel(place_ref, conv_r, query_r, keyval_r, out_r, up_r, down_r, head_r, gains_r, first_o, second_o):
        first_o[:cw, :] = conv_r[...].astype(bfloat)
        first_o[cw : cw + w, :] = query_r[...].astype(bfloat)
        first_o[cw + w : cw + 2 * w, :] = keyval_r[:, :D].astype(bfloat)
        first_o[cw + 2 * w : cw + 3 * w, :] = keyval_r[:, D:].astype(bfloat)
        start = place_ref[0] * w
        shift = jnp.where(iota((w, D), 1) == iota((w, D), 0) + start, 1.0, 0.0).astype(bfloat)
        placed = mm(gains_r[...].astype(bfloat), shift)
        padded = jnp.concatenate([placed, jnp.zeros((16 - placed.shape[0], D), float32)], 0)
        first_o[cw + 3 * w :, :] = padded.astype(bfloat)
        second_o[:w, :] = out_r[...].astype(bfloat)
        for c in range(z.F // D):
            second_o[w + c * w : 2 * w + c * w, :] = up_r[:, c * D : (c + 1) * D].astype(bfloat)
        row = w + z.uw
        second_o[row : row + z.fw, :] = down_r[...].astype(bfloat)
        row += z.fw
        for g in range(D // O):
            here = head_r[g * z.hw : (g + 1) * z.hw, :]
            second_o[row : row + z.hw, g * O : (g + 1) * O] = here.astype(bfloat)

    vmem = pl.BlockSpec(memory_space=pltpu.VMEM)
    return pl.pallas_call(
        kernel,
        out_shape=[
            jax.ShapeDtypeStruct((z.first_rows, D), bfloat),
            jax.ShapeDtypeStruct((z.second_rows, D), bfloat),
        ],
        in_specs=[smem()] + [vmem] * 8,
        out_specs=[vmem] * 2,
        name="pack_weights",
    )(tm_place, *masters)


def pack_tokens(z, feats, spectral, target):
    rows, D, C = z.tokens_dev, z.D, z.channels

    def kernel(f_ref, s_ref, t_ref, o_ref, buffer, in_sem, out_sem):
        arriving, leaving = [], []
        for i in range(z.segments):
            arriving.append(
                [
                    pltpu.make_async_copy(f_ref.at[i], buffer.at[i, rows:, :], in_sem.at[i, 0]),
                    pltpu.make_async_copy(s_ref.at[i], buffer.at[i, :rows, :D], in_sem.at[i, 1]),
                    pltpu.make_async_copy(t_ref.at[i], buffer.at[i, :rows, D:], in_sem.at[i, 2]),
                ]
            )
            leaving.append(pltpu.make_async_copy(buffer.at[i], o_ref.at[i], out_sem.at[i]))
            for copy in arriving[i]:
                copy.start()
        for i in range(z.segments):
            for copy in arriving[i]:
                copy.wait()
            leaving[i].start()
        for copy in leaving:
            copy.wait()

    shape = (z.segments, rows + C, 4 * rows)
    return pl.pallas_call(
        kernel,
        out_shape=jax.ShapeDtypeStruct(shape, bfloat),
        in_specs=[anywhere()] * 3,
        out_specs=anywhere(),
        scratch_shapes=[
            pltpu.VMEM(shape, bfloat),
            pltpu.SemaphoreType.DMA((z.segments, 3)),
            pltpu.SemaphoreType.DMA((z.segments,)),
        ],
        compiler_params=pltpu.CompilerParams(vmem_limit_bytes=VMEM_LIMIT),
        name="pack_tokens",
    )(feats, spectral, target)


def spectral_copies(z, source, home, sem, first):
    if z.parts > 1:
        return [pltpu.make_async_copy(source, home, sem.at[first])]
    rows = z.tokens_dev
    return [
        pltpu.make_async_copy(source.at[i, :rows, : z.D], home.at[i * rows : (i + 1) * rows, :], sem.at[first + i])
        for i in range(z.segments)
    ]


def share_copies(z, meta_ref, shares, home, rows, sem, first):
    place = meta_ref[6] * 2 + meta_ref[7]
    return [
        pltpu.make_async_copy(share.at[rows], home.at[place ^ x], sem.at[first + x])
        for x, share in enumerate(shares)
    ]


def front(z, meta, moved, spectral, halo, weights):
    D, T, K, W, B = z.D, z.tokens, z.keys, z.wide, z.block
    frame, taps, hd = z.frame, z.taps, z.hd
    half = frame // 2
    QB = z.query_block
    count = z.tokens_dev
    CB = 2 * LANES
    extra = 2 if z.parts > 1 else 0
    n_weights = z.n if z.direct else 4

    def kernel(meta_ref, *refs):
        refs = list(refs)
        frames_ref, sp_ref = refs[:2]
        before_after = refs[2 : 2 + extra]
        weight_refs = refs[2 + extra : 2 + extra + n_weights]
        refs = refs[2 + extra + n_weights :]
        (x_o, stream_o, slope_o, normed_o, sn_o, q_o, k_o, v_o, att_o) = refs[:9]
        (frames_s, sp_s, x_s, stream_s, slope_s, normed_s, sn_s) = refs[9:16]
        (conv_s, wq_s, wk_s, wv_s, q_s, k_s, v_s, in_sem, out_sem) = refs[16:25]
        refs = refs[25:]
        h = pl.program_id(0)
        outgoing = [
            pltpu.make_async_copy(src, dst, out_sem.at[i])
            for i, (src, dst) in enumerate(
                ((x_s, x_o), (stream_s, stream_o), (slope_s, slope_o), (normed_s, normed_o), (sn_s, sn_o))
            )
        ]

        @pl.when(h == 0)
        def _():
            frames_copy = pltpu.make_async_copy(frames_ref.at[:, count:, :], frames_s, in_sem.at[0])
            spectral_in = spectral_copies(z, sp_ref, sp_s, in_sem, 1)
            if z.direct:
                blob_s, wc, wqkv = refs
                blob_in = share_copies(z, meta_ref, weight_refs, blob_s, slice(0, z.first_rows), in_sem, 1 + z.segments)
                for copy in blob_in:
                    copy.start()
            for copy in spectral_in:
                copy.start()
            frames_copy.start()
            if z.direct:
                for copy in blob_in:
                    copy.wait()
                w, cw = z.w, z.cw
                total = jnp.zeros((16, D), float32)
                for j in range(z.n):
                    wc[j * cw : (j + 1) * cw, :] = blob_s[j, 0:cw, :]
                    for c in range(3):
                        first = cw + c * w
                        wqkv[j * w : (j + 1) * w, c * D : (c + 1) * D] = blob_s[j, first : first + w, :]
                    total = total + blob_s[j, cw + 3 * w : cw + 3 * w + 16, :].astype(float32)
                gain_query, gain_keys = total[0:1, :], total[1:2, :]
                parts_w = [wqkv[:, c * D : (c + 1) * D] for c in range(3)]
            else:
                wc, wq, wkv, gains_ref = weight_refs
                gain_query, gain_keys = gains_ref[0:1, :], gains_ref[1:2, :]
                parts_w = [wq[...], wkv[:, :D], wkv[:, D:]]
            spread = spread_matrix(D, hd)
            for target_s, part in zip((wq_s, wk_s, wv_s), parts_w):
                target_s[...] = mm(part, spread).astype(bfloat)
            for copy in spectral_in:
                copy.wait()

            def key_block(i, carry):
                rows = pl.ds(pl.multiple_of(i * B, B), B)
                unit, _ = norm_parts(sp_s[rows, :].astype(float32))
                sn_s[rows, :] = (unit * gain_keys).astype(bfloat)
                return carry

            lax.fori_loop(0, K // B, key_block, 0)
            outgoing[4].start()
            inside = iota((K, CB), 1) % LANES
            spare = jnp.logical_and(inside >= hd, inside < hd + 3)
            for home, part in ((k_s, wk_s), (v_s, wv_s)):
                for c in range(0, W, CB):
                    product = mm(sn_s[...], part[:, c : c + CB])
                    home[:, c : c + CB] = jnp.where(spare, -1.0, product).astype(bfloat)
            frames_copy.wait()
            shape = (4 * count, 4 * count)
            row, column = iota(shape, 0), iota(shape, 1)
            order = jnp.where(column == (row % count) * 4 + row // count, 1.0, 0.0).astype(bfloat)
            for i in range(z.segments):
                taps_rows = nt(order, frames_s[i])
                x_s[i * count : (i + 1) * count, :] = jnp.concatenate(
                    [taps_rows[j * count : (j + 1) * count, :] for j in range(4)], 1
                ).astype(bfloat)
            outgoing[0].start()
            conv_s[...] = mm(x_s[...], wc[half : half + frame, :])
            row = iota((T, D), 0)
            older = pltpu.roll(mm(x_s[:, half:], wc[:half, :]), 1, 0)
            first_row, last_row = 0.0, 0.0
            if z.parts > 1:
                first_row = mm(before_after[0][...], wc[:half, :])[0:1, :]
                last_row = mm(before_after[1][...], wc[half + frame :, :])[0:1, :]
            conv_s[...] += jnp.where(row == 0, first_row, older)
            newer = pltpu.roll(mm(x_s[:, :half], wc[half + frame :, :]), T - 1, 0)
            conv_s[...] += jnp.where(row == T - 1, last_row, newer)

            def token_block(i, carry):
                rows = pl.ds(pl.multiple_of(i * B, B), B)
                stream, slope = gelu_both(conv_s[rows, :])
                stream_s[rows, :] = stream
                slope_s[rows, :] = slope
                unit, _ = norm_parts(stream)
                normed = (unit * gain_query).astype(bfloat)
                normed_s[rows, :] = normed
                return carry

            lax.fori_loop(0, T // B, token_block, 0)
            for c in range(0, W, CB):
                q_s[:, c : c + CB] = mm(normed_s[...], wq_s[:, c : c + CB]).astype(bfloat)
            for copy in outgoing[1:4]:
                copy.start()

        lanes = pl.ds(pl.multiple_of(h * LANES, LANES), LANES)
        k_o[...] = k_s[:, lanes]
        v_o[...] = v_s[:, lanes]
        def finish(rows, count, grown, top):
            q = q_s[rows, lanes]
            mass = jnp.sum(grown, 0, keepdims=True)
            probs = (grown * (1.0 / mass)).astype(bfloat)
            total = top + jnp.log(mass)
            result = tn(v_o[...], probs)
            high = total.astype(bfloat).astype(float32)
            rest = total - high
            mid = rest.astype(bfloat).astype(float32)
            sub = iota((LANES, count), 0)
            spare = jnp.where(sub == hd, high, jnp.where(sub == hd + 1, mid, rest - mid))
            spare = jnp.where(sub < hd + 3, spare, 0.0)
            both = jnp.where(sub < hd, result, spare).T
            att_o[rows, :] = both.astype(bfloat)
            lane = iota((count, LANES), 1)
            q_o[rows, :] = jnp.where(lane < hd, q.astype(float32), both).astype(bfloat)
            return mass

        least, most = jnp.inf, 0.0
        for b in range(T // QB):
            rows = slice(b * QB, (b + 1) * QB)
            mass = finish(rows, QB, jnp.exp(nt(k_o[...], q_s[rows, lanes])), 0.0)
            least = jnp.minimum(least, jnp.min(mass))
            most = jnp.maximum(most, jnp.max(mass))
        safe = jnp.logical_and(least > 1e-20, most < 1e30)

        @pl.when(jnp.logical_not(safe))
        def _():
            def again(i, carry):
                rows = pl.ds(pl.multiple_of(i * LANES, LANES), LANES)
                scores = nt(k_o[...], q_s[rows, lanes])
                top = jnp.max(scores, 0, keepdims=True)
                finish(rows, LANES, jnp.exp(scores - top), top)
                return carry

            lax.fori_loop(0, T // LANES, again, 0)

        @pl.when(h == H - 1)
        def _():
            for copy in outgoing:
                copy.wait()

    def lanes_of(rows):
        return pl.BlockSpec((rows, LANES), lambda h: (0, h))

    in_specs = [smem(), anywhere(), anywhere()]
    args = [meta, moved, moved if z.parts == 1 else spectral]
    if z.parts > 1:
        args += list(halo)
        in_specs += [whole((16, D))] * 2
    scratch = [
        pltpu.VMEM((z.segments, z.channels, 4 * count), bfloat),
        pltpu.VMEM((K, D), bfloat),
        pltpu.VMEM((T, frame), bfloat),
        pltpu.VMEM((T, D), float32),
        pltpu.VMEM((T, D), float32),
        pltpu.VMEM((T, D), bfloat),
        pltpu.VMEM((K, D), bfloat),
        pltpu.VMEM((T, D), float32),
        pltpu.VMEM((D, W), bfloat),
        pltpu.VMEM((D, W), bfloat),
        pltpu.VMEM((D, W), bfloat),
        pltpu.VMEM((T, W), bfloat),
        pltpu.VMEM((K, W), bfloat),
        pltpu.VMEM((K, W), bfloat),
        pltpu.SemaphoreType.DMA((1 + z.segments + z.n,)),
        pltpu.SemaphoreType.DMA((5,)),
    ]
    if z.direct:
        args += weights[0]
        in_specs += [anywhere()] * z.n
        scratch += [
            pltpu.VMEM((z.n, z.first_rows, D), bfloat),
            pltpu.VMEM((taps, D), bfloat),
            pltpu.VMEM((D, 3 * D), bfloat),
        ]
    else:
        for array in (weights[0], weights[1], weights[2], weights[7]):
            args.append(array)
            in_specs.append(whole(array.shape))
    shapes = [
        ((T, frame), bfloat),
        ((T, D), float32),
        ((T, D), float32),
        ((T, D), bfloat),
        ((K, D), bfloat),
        ((T, W), bfloat),
        ((K, W), bfloat),
        ((K, W), bfloat),
        ((T, W), bfloat),
    ]
    return pl.pallas_call(
        kernel,
        grid=(H,),
        out_shape=[jax.ShapeDtypeStruct(s, d) for s, d in shapes],
        in_specs=in_specs,
        out_specs=[anywhere()] * 5 + [lanes_of(T), lanes_of(K), lanes_of(K), lanes_of(T)],
        scratch_shapes=scratch,
        compiler_params=pltpu.CompilerParams(vmem_limit_bytes=VMEM_LIMIT),
        cost_estimate=pl.CostEstimate(flops=20_000_000_000, bytes_accessed=20_000_000, transcendentals=10_000_000),
        name="front",
    )(*args)


def emit_blocks(z, meta_ref, keep_o, send_o, sources):
    chip, core, plane = meta_ref[6], meta_ref[7], meta_ref[8]
    quarter = keep_o.shape[2]

    def write(out, m, row, here, lanes):
        first = 0
        while first < here.shape[0]:
            part, inside = divmod(row + first, quarter)
            size = min(here.shape[0] - first, quarter - inside)
            out[m, part ^ plane, inside : inside + size, lanes] = here[first : first + size].astype(out.dtype)
            first += size

    for m in range(z.n // 2):
        owner = (chip ^ m) * 2
        for out, place in ((keep_o, owner + core), (send_o, owner + 1 - core)):
            row = 0
            for ref, rows, pieces in sources:
                width = ref.shape[-1]
                if width >= z.D:
                    start = pl.multiple_of(place * rows, 16)
                    for lane in range(0, width, z.D):
                        write(out, m, row, ref[pl.ds(start, rows), lane : lane + z.D], slice(0, z.D))
                        row += rows
                else:
                    size = rows // pieces
                    for g in range(pieces):
                        start = pl.multiple_of(place * rows + g * size, 16)
                        write(out, m, row, ref[pl.ds(start, size), :], slice(g * width, (g + 1) * width))
                    row += size
            if row < quarter * z.planes:
                rest = quarter * z.planes - row
                write(out, m, row, jnp.zeros((rest, z.D), float32), slice(0, z.D))


def block_shapes(z, rows):
    shape = (z.n // 2, z.planes, rows // z.planes, z.D)
    return [(shape, float32), (shape, bfloat)]


def middle(z, meta, count, stream, att, target, weights):
    D, T, W, F, O = z.D, z.tokens, z.wide, z.F, z.out
    B = z.middle_block
    hd = z.hd

    def kernel(meta_ref, count_ref, stream_ref, att_ref, target_ref, *refs):
        refs = list(refs)
        if z.direct:
            first_refs, second_refs = refs[: z.n], refs[z.n : 2 * z.n]
            refs = refs[2 * z.n :]
            do_out, mid_out, misc_o, keep_o, send_o = refs[:5]
            refs = refs[5:]
        else:
            wo, wu, wd, wh, gains_ref = refs[:5]
            do_out, mid_out, misc_o, go_s, gu_s, gd_s, gh_s = refs[5:12]
            refs = refs[12:]
        wop, att_s, stream_s, do_o, mid_o, act_s, hg_s, fin_s, fg_s, low_s, pg_s, bg_s, sem = refs[:13]
        refs = refs[13:]
        if z.direct:
            go_s, gu_s, gd_s, gh_s, blob_s, gain_s, wo, wu, wd, wh = refs

        att_copy = pltpu.make_async_copy(att_ref, att_s, sem.at[0])
        stream_copy = pltpu.make_async_copy(stream_ref, stream_s, sem.at[1])
        if z.direct:
            w, uw, fw, hw = z.w, z.uw, z.fw, z.hw
            ends = (0, w, w + uw, w + uw + fw, z.second_rows)
            pieces = [
                share_copies(z, meta_ref, second_refs, blob_s.at[:, p:q], slice(p, q), sem, 9 + c * z.n)
                for c, (p, q) in enumerate(zip(ends[:-1], ends[1:]))
            ]
            last = slice(z.first_rows - 16, z.first_rows)
            gain_in = share_copies(z, meta_ref, first_refs, gain_s, last, sem, 9 + 4 * z.n)
            for copy in pieces[0] + gain_in:
                copy.start()
        att_copy.start()
        stream_copy.start()
        if z.direct:
            for piece in pieces[1:]:
                for copy in piece:
                    copy.start()
            for copy in pieces[0] + gain_in:
                copy.wait()
            total = jnp.zeros((16, D), float32)
            for j in range(z.n):
                wo[j * w : (j + 1) * w, :] = blob_s[j, 0:w, :]
                total = total + gain_s[j].astype(float32)
        else:
            total = gains_ref[...]
        wop[...] = tn(spread_matrix(D, hd), wo[...]).astype(bfloat)
        misc_o[...] = jnp.zeros_like(misc_o)
        gain_ffn, scale_attn, scale_ffn = total[2:3, :], total[3:4, :], total[4:5, :]
        base, valid = meta_ref[0], meta_ref[1]
        samples = count_ref[0]
        att_copy.wait()
        stream_copy.wait()
        if z.direct:
            for copy in pieces[1]:
                copy.wait()
            for j in range(z.n):
                for c in range(F // D):
                    first = w + c * w
                    wu[j * w : (j + 1) * w, c * D : (c + 1) * D] = blob_s[j, first : first + w, :]
        if z.direct:
            for copy in pieces[2] + pieces[3]:
                copy.wait()
            for j in range(z.n):
                wd[j * fw : (j + 1) * fw, :] = blob_s[j, w + uw : w + uw + fw, :]
                for g in range(D // O):
                    start = j * w + g * hw
                    wh[start : start + hw, :] = blob_s[j, w + uw + fw :, g * O : (g + 1) * O]
        chunks = B // z.tokens_dev

        def block(i, carry):
            rows = pl.ds(pl.multiple_of(i * B, B), B)
            branch = mm(att_s[rows, :], wop[...])
            stream_mid = stream_s[rows, :] + scale_attn * branch
            unit, scale = norm_parts(stream_mid)
            ffn_in = (unit * gain_ffn).astype(bfloat)
            fin_s[rows, :] = ffn_in
            hidden = mm(ffn_in, wu[...])
            active, slope = gelu_both(hidden)
            active = active.astype(bfloat)
            act_s[rows, :] = active
            ffn_out = mm(active, wd[...])
            stream_low = (stream_mid + scale_ffn * ffn_out).astype(bfloat)
            low_s[rows, :] = stream_low
            predicted = mm(stream_low, wh[...])
            column = iota((B, O), 1)
            position = (base + i * B + iota((B, O), 0)) * SUB + column % SUB
            stem = column // (2 * SUB)
            weight = jnp.zeros((B, O), float32)
            for k in range(STEMS):
                weight = jnp.where(stem == k, meta_ref[2 + k].astype(float32), weight)
            weight = jnp.where(position < valid, weight, 0.0)
            error = predicted - target_ref[pl.ds(i * chunks, chunks)].reshape(B, O).astype(float32)
            root = jnp.sqrt(error * error + 1.0)
            misc_o[5:6, :O] += jnp.sum(weight * (root - 1.0), 0, keepdims=True)
            predicted_grad = (weight * error / root / samples).astype(bfloat)
            pg_s[rows, :] = predicted_grad
            end_grad = nt(predicted_grad, wh[...])
            misc_o[4:5, :] += jnp.sum(end_grad * ffn_out, 0, keepdims=True)
            ffn_grad = (scale_ffn * end_grad).astype(bfloat)
            fg_s[rows, :] = ffn_grad
            hidden_grad = (nt(ffn_grad, wd[...]) * slope).astype(bfloat)
            hg_s[rows, :] = hidden_grad
            mid_part, gain_grad = norm_back(unit, scale, gain_ffn, nt(hidden_grad, wu[...]))
            misc_o[2:3, :] += gain_grad
            mid_grad = end_grad + mid_part
            mid_o[rows, :] = mid_grad
            misc_o[3:4, :] += jnp.sum(mid_grad * branch, 0, keepdims=True)
            branch_grad = (scale_attn * mid_grad).astype(bfloat)
            bg_s[rows, :] = branch_grad
            att_grad = nt(branch_grad, wop[...]).astype(bfloat)
            for h in range(H):
                lanes = slice(h * LANES, (h + 1) * LANES)
                one = att_grad[:, lanes].astype(float32)
                delta = jnp.sum(one * att_s[rows, lanes].astype(float32), -1, keepdims=True)
                do_o[rows, lanes] = with_column(one, delta, hd)
            return carry

        lax.fori_loop(0, T // B, block, 0)
        outgoing = [
            pltpu.make_async_copy(do_o, do_out, sem.at[7]),
            pltpu.make_async_copy(mid_o, mid_out, sem.at[8]),
        ]
        for copy in outgoing:
            copy.start()
        spare_grad = tn(att_s[...], bg_s[...])
        for h in range(H):
            go_s[h * hd : (h + 1) * hd, :] = spare_grad[h * LANES : h * LANES + hd, :]

        def up_columns(c, carry):
            here = pl.ds(pl.multiple_of(c * D, LANES), D)
            gu_s[:, here] = tn(fin_s[...], hg_s[:, here])
            return carry

        lax.fori_loop(0, F // D, up_columns, 0)
        gd_s[...] = tn(act_s[...], fg_s[...])
        gh_s[...] = tn(low_s[...], pg_s[...])
        if z.direct:
            emit_blocks(
                z,
                meta_ref,
                keep_o,
                send_o,
                ((go_s, z.w, 1), (gu_s, z.w, 1), (gd_s, z.fw, 1), (gh_s, z.w, D // O)),
            )
        for copy in outgoing:
            copy.wait()

    if z.parts == 1:
        target_spec = pl.BlockSpec((z.segments, z.tokens_dev, O), lambda i: (0, 0, D // O))
    else:
        target_spec = whole(target.shape)
    in_specs = [smem(), smem(), anywhere(), anywhere(), target_spec]
    args = [meta, count, stream, att, target]
    scratch = [
        pltpu.VMEM((W, D), bfloat),
        pltpu.VMEM((T, W), bfloat),
        pltpu.VMEM((T, D), float32),
        pltpu.VMEM((T, W), bfloat),
        pltpu.VMEM((T, D), float32),
        pltpu.VMEM((T, F), bfloat),
        pltpu.VMEM((T, F), bfloat),
        pltpu.VMEM((T, D), bfloat),
        pltpu.VMEM((T, D), bfloat),
        pltpu.VMEM((T, D), bfloat),
        pltpu.VMEM((T, O), bfloat),
        pltpu.VMEM((T, D), bfloat),
        pltpu.SemaphoreType.DMA((9 + 5 * z.n,)),
    ]
    shapes = [((T, W), bfloat), ((T, D), float32), ((8, D), float32)]
    grads = [((D, D), float32), ((D, F), float32), ((F, D), float32), ((D, O), float32)]
    if z.direct:
        args += weights[0] + weights[1]
        in_specs += [anywhere()] * (2 * z.n)
        scratch += [pltpu.VMEM(s, d) for s, d in grads] + [
            pltpu.VMEM((z.n, z.second_rows, D), bfloat),
            pltpu.VMEM((z.n, 16, D), bfloat),
            pltpu.VMEM((D, D), bfloat),
            pltpu.VMEM((D, F), bfloat),
            pltpu.VMEM((F, D), bfloat),
            pltpu.VMEM((D, O), bfloat),
        ]
        shapes += block_shapes(z, z.second_grads)
    else:
        for array in weights[3:]:
            args.append(array)
            in_specs.append(whole(array.shape))
        shapes += grads
    return pl.pallas_call(
        kernel,
        grid=(1,),
        out_shape=[jax.ShapeDtypeStruct(s, d) for s, d in shapes],
        in_specs=in_specs,
        out_specs=[anywhere(), anywhere()] + [whole(s) for s, d in shapes[2:]],
        scratch_shapes=scratch,
        compiler_params=pltpu.CompilerParams(vmem_limit_bytes=VMEM_LIMIT),
        cost_estimate=pl.CostEstimate(flops=20_000_000_000, bytes_accessed=20_000_000, transcendentals=4_000_000),
        name="middle",
    )(*args)


def head_back(z, q_ref, k_ref, v_ref, do_ref, put_query, dk_s, dv_s):
    T, hd = z.tokens, z.hd
    QB = 256 if z.keys <= 1024 else 128
    dk_s[...] = jnp.zeros_like(dk_s)
    dv_s[...] = jnp.zeros_like(dv_s)

    def block(i, carry):
        for b in range(2):
            rows = pl.ds(pl.multiple_of((i * 2 + b) * QB, QB), QB)
            q, do = q_ref[rows, :], do_ref[rows, :]
            probs = jnp.exp(nt(q, k_ref[...]))
            score_grad = (probs * nt(do, v_ref[...])).astype(bfloat)
            low = probs.astype(bfloat)
            put_query(rows, mm(score_grad, k_ref[...]).astype(bfloat))
            dk_s[...] += tn(q, score_grad)[:hd, :]
            dv_s[...] += tn(do, low)[:hd, :]
        return carry

    lax.fori_loop(0, T // (2 * QB), block, 0)
    return dk_s[...].astype(bfloat), dv_s[...].astype(bfloat)


def attend_back(z, q, k, v, do, heads):
    T, K, W, D = z.tokens, z.keys, z.wide, z.D
    hd = z.hd

    def kernel(q_ref, k_ref, v_ref, do_ref, dq_o, dkv_o, dk_s, dv_s):
        def put_query(rows, value):
            dq_o[rows, :] = value

        dkv_o[0], dkv_o[1] = head_back(z, q_ref, k_ref, v_ref, do_ref, put_query, dk_s, dv_s)

    def lanes(rows):
        return pl.BlockSpec((rows, LANES), lambda h: (0, h))

    return pl.pallas_call(
        kernel,
        grid=(heads,),
        out_shape=[
            jax.ShapeDtypeStruct((T, heads * LANES), bfloat),
            jax.ShapeDtypeStruct((2, heads * hd, K), bfloat),
        ],
        in_specs=[lanes(T), lanes(K), lanes(K), lanes(T)],
        out_specs=[lanes(T), pl.BlockSpec((2, hd, K), lambda h: (0, h, 0))],
        scratch_shapes=[pltpu.VMEM((hd, K), float32)] * 2,
        compiler_params=pltpu.CompilerParams(vmem_limit_bytes=VMEM_LIMIT),
        cost_estimate=pl.CostEstimate(
            flops=heads * 4_000_000_000, bytes_accessed=12_000_000, transcendentals=heads * 1_000_000
        ),
        name="attend_back",
    )(q, k, v, do)


def back(z, done, meta, q, k, v, do, dq, dkv, x, spectral, halo, stream, slope, normed, sn, mid, misc, weights):
    D, T, K, W, B, O = z.D, z.tokens, z.keys, z.wide, z.block, z.out
    frame, taps, hd = z.frame, z.taps, z.hd
    half = frame // 2
    steps = H - done
    extra = 2 if z.parts > 1 else 0
    n_weights = z.n if z.direct else 3
    n_out = 2 if z.direct else 4

    def kernel(meta_ref, q_ref, k_ref, v_ref, do_ref, misc_ref, *refs):
        refs = list(refs)
        before_after = refs[:extra]
        remote = refs[extra : extra + 9]
        refs = refs[extra + 9 :]
        weight_refs, refs = refs[:n_weights], refs[n_weights:]
        outs, refs = refs[:n_out], refs[n_out:]
        (dq_s, dkv_s, x_ref, sp_ref, stream_ref, slope_ref, normed_ref, sn_ref, mid_ref) = refs[:9]
        refs = refs[9:]
        cg_s, dn_s, dqc_s, dkvt_s, dk_s, dv_s, sem = refs[:7]
        refs = refs[7:]
        if z.direct:
            gc_s, gq_s, gkv_s, misc_s, place_s, blob_s, wq, wkv = refs
        else:
            gc_s, gq_s, gkv_s, misc_s = outs
            wq, wkv, gains_ref = weight_refs
        i = pl.program_id(0)
        old = done * LANES
        homes = [dq_s.at[:, :old], dkv_s.at[:, : done * hd]] + [
            x_ref, sp_ref, stream_ref, slope_ref, normed_ref, sn_ref, mid_ref
        ]
        copies = [
            pltpu.make_async_copy(a, b, sem.at[c])
            for c, (a, b) in enumerate(zip(remote, homes))
            if c != 3
        ]
        copies += spectral_copies(z, remote[3], sp_ref, sem, 10)
        if z.direct:
            copies += share_copies(
                z, meta_ref, weight_refs, blob_s, slice(z.cw, z.first_rows), sem, 10 + z.segments
            )

        @pl.when(i == 0)
        def _():
            for copy in copies:
                copy.start()

        lanes = pl.ds(pl.multiple_of((i + done) * LANES, LANES), LANES)

        def put_query(rows, value):
            dq_s[rows, lanes] = value

        dk, dv = head_back(z, q_ref, k_ref, v_ref, do_ref, put_query, dk_s, dv_s)
        here = pl.ds(pl.multiple_of((i + done) * hd, 16), hd)
        dkv_s[0, here, :] = dk
        dkv_s[1, here, :] = dv

        @pl.when(i == steps - 1)
        def _():
            for copy in copies:
                copy.wait()
            if z.direct:
                w = z.w
                total = jnp.zeros((16, D), float32)
                for j in range(z.n):
                    here = slice(j * w, (j + 1) * w)
                    wq[here, :] = blob_s[j, 0:w, :]
                    wkv[here, :D] = blob_s[j, w : 2 * w, :]
                    wkv[here, D:] = blob_s[j, 2 * w : 3 * w, :]
                    total = total + blob_s[j, 3 * w :, :].astype(float32)
            else:
                total = gains_ref[...]
            gain_query = total[0:1, :]
            misc_s[...] = misc_ref[...]
            dqc_s[...] = nt(dq_s[...], spread_matrix(D, hd)).astype(bfloat)
            dkvt_s[:, :D] = dkv_s[0].T
            dkvt_s[:, D:] = dkv_s[1].T
            gkv_s[...] = tn(sn_ref[...], dkvt_s[...])
            gq_s[...] = tn(normed_ref[...], dqc_s[...])

            for c in range(K // T):
                cg_s[...] = nt(dkvt_s[c * T : (c + 1) * T, :], wkv[...])
                for i in range(T // B):
                    rows = slice(i * B, (i + 1) * B)
                    unit, _ = norm_parts(sp_ref[c * T + i * B : c * T + (i + 1) * B, :].astype(float32))
                    misc_s[1:2, :] += jnp.sum(cg_s[rows, :] * unit, 0, keepdims=True)
            dn_s[...] = nt(dqc_s[...], wq[...])
            for i in range(T // B):
                rows = slice(i * B, (i + 1) * B)
                unit, scale = norm_parts(stream_ref[rows, :])
                part, gain_grad = norm_back(unit, scale, gain_query, dn_s[rows, :])
                misc_s[0:1, :] += gain_grad
                conv_grad = (mid_ref[rows, :] + part) * slope_ref[rows, :]
                cg_s[rows, :] = conv_grad.astype(bfloat).astype(float32)
            conv_grad = cg_s[...]
            gc_s[half : half + frame, :] = tn(x_ref[...], conv_grad.astype(bfloat))
            row = iota((T, D), 0)
            later = jnp.where(row == T - 1, 0.0, pltpu.roll(conv_grad, T - 1, 0)).astype(bfloat)
            gc_s[:half, :] = tn(x_ref[:, half:], later)
            sooner = jnp.where(row == 0, 0.0, pltpu.roll(conv_grad, 1, 0)).astype(bfloat)
            gc_s[half + frame :, :] = tn(x_ref[:, :half], sooner)
            if z.parts > 1:
                first = iota((16, D), 0) == 0
                top = jnp.where(first, conv_grad[0:16, :], 0.0).astype(bfloat)
                gc_s[:half, :] += tn(before_after[0][...], top)
                tail = jnp.where(first, pltpu.roll(conv_grad[T - 16 :, :], 1, 0), 0.0)
                gc_s[half + frame :, :] += tn(before_after[1][...], tail.astype(bfloat))
            if z.direct:
                for j in range(z.n):
                    row, lane = iota((D, LANES), 0), iota((D, LANES), 1)
                    hit = jnp.logical_and(row == lane + j * z.w, lane < z.w)
                    chosen = lax.dot_general(
                        misc_s[...], jnp.where(hit, 1.0, 0.0), (((1,), (0,)), ((), ())),
                        precision=lax.Precision.HIGHEST, preferred_element_type=float32,
                    )
                    low_rows = jnp.where(iota((8, LANES), 0) == 5, misc_s[:, :LANES], chosen)
                    place_s[j * 16 : (j + 1) * 16, :] = jnp.zeros((16, D), float32)
                    place_s[j * 16 : j * 16 + 8, :LANES] = low_rows
                emit_blocks(
                    z, meta_ref, outs[0], outs[1],
                    ((gc_s, z.cw, 1), (gq_s, z.w, 1), (gkv_s, z.w, 1), (place_s, 16, 1)),
                )

    def lanes_of(rows):
        return pl.BlockSpec((rows, LANES), lambda i: (0, i + done))

    args = [meta, q, k, v, do, misc]
    in_specs = [smem(), lanes_of(T), lanes_of(K), lanes_of(K), lanes_of(T), whole(misc.shape)]
    if z.parts > 1:
        args += list(halo)
        in_specs += [whole((16, D))] * 2
    remote = (dq, dkv, x, spectral, stream, slope, normed, sn, mid)
    args += list(remote)
    in_specs += [anywhere()] * 9
    scratch = [pltpu.VMEM((T, W), bfloat), pltpu.VMEM((2, D, K), bfloat)]
    homes = (x.shape, (K, D)) + tuple(a.shape for a in remote[4:])
    scratch += [pltpu.VMEM(s, a.dtype) for s, a in zip(homes, remote[2:])]
    scratch += [
        pltpu.VMEM((T, D), float32),
        pltpu.VMEM((T, D), float32),
        pltpu.VMEM((T, D), bfloat),
        pltpu.VMEM((K, 2 * D), bfloat),
        pltpu.VMEM((hd, K), float32),
        pltpu.VMEM((hd, K), float32),
        pltpu.SemaphoreType.DMA((10 + z.segments + z.n,)),
    ]
    grads = [((taps, D), float32), ((D, D), float32), ((D, 2 * D), float32), ((8, D), float32)]
    if z.direct:
        args += weights[0]
        in_specs += [anywhere()] * z.n
        scratch += [pltpu.VMEM(s, d) for s, d in grads] + [
            pltpu.VMEM((z.n * 16, D), float32),
            pltpu.VMEM((z.n, z.first_rows - z.cw, D), bfloat),
            pltpu.VMEM((D, D), bfloat),
            pltpu.VMEM((D, 2 * D), bfloat),
        ]
        shapes = block_shapes(z, z.first_grads)
    else:
        for array in (weights[1], weights[2], weights[7]):
            args.append(array)
            in_specs.append(whole(array.shape))
        shapes = grads
    return pl.pallas_call(
        kernel,
        grid=(steps,),
        out_shape=[jax.ShapeDtypeStruct(s, d) for s, d in shapes],
        in_specs=in_specs,
        out_specs=[whole(s) for s, d in shapes],
        scratch_shapes=scratch,
        compiler_params=pltpu.CompilerParams(vmem_limit_bytes=VMEM_LIMIT),
        cost_estimate=pl.CostEstimate(flops=30_000_000_000, bytes_accessed=20_000_000, transcendentals=8_000_000),
        name="back",
    )(*args)


def pairs(count, mask):
    return [(i, i ^ mask) for i in range(count)]


def tree_sum(values):
    while len(values) > 1:
        values = [values[i] + values[i + 1] for i in range(0, len(values), 2)]
    return values[0]


def from_chips(z, own):
    return [own] + [lax.ppermute(own, "tm", pairs(z.n, 2 * m)) for m in range(1, z.n // 2)]


def with_core(z, same):
    other = [lax.ppermute(share, "tm", pairs(z.n, 1)) for share in same]
    return [share for pair in zip(same, other) for share in pair]


def over_core(z, keep, send):
    there = lax.ppermute(send, "tm", pairs(z.n, 1))
    sums = [keep[m] + there[m].astype(float32) for m in range(z.n // 2)]
    return sums[:1] + [value.astype(bfloat) for value in sums[1:]]


def over_plane(z, blocks):
    mine = blocks[:1]
    for m in range(1, z.n // 2):
        mine.append(lax.ppermute(blocks[m], "tm", pairs(z.n, 2 * m)).astype(float32))
    return tree_sum(mine)


def over_planes(z, mine):
    parts = [mine[0]]
    for m in range(1, z.planes):
        there = lax.ppermute(mine[m].astype(bfloat), "seg", pairs(z.planes, m))
        parts.append(there.astype(float32))
    low = tree_sum(parts).astype(bfloat)
    return [low] + [lax.ppermute(low, "seg", pairs(z.planes, m)) for m in range(1, z.planes)]


def adam_update(master, first, second, grad, factor, rate):
    clipped = grad * factor
    first_new = beta_first * first + (1.0 - beta_first) * clipped
    second_new = beta_second * second + (1.0 - beta_second) * clipped * clipped
    moment_hat = first_new / (1.0 - beta_first**STEP)
    square_hat = second_new / (1.0 - beta_second**STEP)
    master_new = master - rate * (
        moment_hat / (jnp.sqrt(square_hat) + adam_epsilon) + weight_decay * master
    )
    return (master_new, first_new, second_new)


RATES = (
    learn_rate, learn_rate, learn_rate, fast_rate, learn_rate, learn_rate, learn_rate, fast_rate,
)


def gather_quarters(z, meta_ref, refs, out_ref):
    quarter = refs[0].shape[0]
    for m, ref in enumerate(refs):
        start = pl.multiple_of((meta_ref[8] ^ m) * quarter, 16)
        out_ref[pl.ds(start, quarter), :] = ref[...].astype(float32)


def square_sums(z, meta, first, second):
    D = z.D

    def kernel(meta_ref, *refs):
        planes = z.planes
        a_o, b_o, sq_o = refs[2 * planes :]
        gather_quarters(z, meta_ref, refs[:planes], a_o)
        gather_quarters(z, meta_ref, refs[planes : 2 * planes], b_o)
        loss_row = z.cw + 3 * z.w + 5
        total = jnp.zeros((8, D), float32)
        for ref, skip in ((a_o, loss_row), (b_o, -1)):
            for r in range(0, ref.shape[0], 8):
                here = ref[r : r + 8, :]
                if r <= skip < r + 8:
                    here = jnp.where(iota((8, D), 0) == skip - r, 0.0, here)
                total = total + here * here
        sq_o[0:8, :] = total[:, :LANES] + total[:, LANES : 2 * LANES] + total[:, 2 * LANES :]
        loss = a_o[loss_row - 5 : loss_row + 3, :LANES]
        sq_o[8:16, :] = jnp.where(iota((8, LANES), 0) == 5, loss * (1.0 / z.n), 0.0)

    vmem = pl.BlockSpec(memory_space=pltpu.VMEM)
    shapes = [(z.first_grads, D), (z.second_grads, D), (16, LANES)]
    return pl.pallas_call(
        kernel,
        out_shape=[jax.ShapeDtypeStruct(s, float32) for s in shapes],
        in_specs=[smem()] + [vmem] * (2 * z.planes),
        out_specs=[vmem] * 3,
        compiler_params=pltpu.CompilerParams(vmem_limit_bytes=16 * 1024 * 1024),
        name="square_sums",
    )(meta, *first, *second)


def update(z, squares, first_sum, second_sum, masters, firsts, seconds):
    D, O, w, cw = z.D, z.out, z.w, z.cw
    given = len(squares)

    def kernel(*refs):
        sq_refs = refs[:given]
        a_ref, b_ref = refs[given : given + 2]
        ins = refs[given + 2 : given + 26]
        loss_o, norm_o = refs[given + 26 : given + 28]
        outs = refs[given + 28 :]
        sums = tree_sum([ref[...] for ref in sq_refs])
        norm = jnp.sqrt(jnp.sum(sums[0:8, :], keepdims=True))
        loss_o[...] = jnp.sum(sums[8:16, :], keepdims=True)
        norm_o[...] = norm
        factor = jnp.minimum(1.0, clip_limit / (norm + 1e-06))
        places = {
            0: [(a_ref, 0, cw, 0)],
            1: [(a_ref, cw, w, 0)],
            2: [(a_ref, cw + w + c * w, w, c * D) for c in range(2)],
            3: [(b_ref, 0, w, 0)],
            4: [(b_ref, w + c * w, w, c * D) for c in range(z.F // D)],
            5: [(b_ref, w + z.uw, z.fw, 0)],
        }

        def step(index, here, grad):
            values = adam_update(
                ins[index][here], ins[8 + index][here], ins[16 + index][here], grad, factor, RATES[index]
            )
            for kind, value in enumerate(values):
                outs[8 * kind + index][here] = value

        def block(index, ref, start, lane):
            def body(i, carry):
                here = pl.ds(pl.multiple_of(i * w, 16), w)
                step(index, (here, slice(lane, lane + D)), ref[pl.ds(pl.multiple_of(start + i * w, 16), w), :])
                return carry

            return body

        for index, pieces in places.items():
            for ref, start, count, lane in pieces:
                lax.fori_loop(0, count // w, block(index, ref, start, lane), 0)
        start = w + z.uw + z.fw
        for g in range(D // O):
            here = (slice(g * z.hw, (g + 1) * z.hw), slice(0, O))
            step(6, here, b_ref[start : start + z.hw, g * O : (g + 1) * O])
        gains = a_ref[cw + 3 * w : cw + 3 * w + 8, :][:5, :w]
        step(7, (slice(0, 5), slice(0, w)), gains)

    vmem = pl.BlockSpec(memory_space=pltpu.VMEM)
    outs = [jax.ShapeDtypeStruct((1, 1), float32)] * 2
    outs += [jax.ShapeDtypeStruct(m.shape, float32) for m in masters] * 3
    return pl.pallas_call(
        kernel,
        out_shape=outs,
        in_specs=[vmem] * (given + 26),
        out_specs=[vmem] * 26,
        compiler_params=pltpu.CompilerParams(vmem_limit_bytes=20 * 1024 * 1024),
        name="update",
    )(*squares, first_sum, second_sum, *masters, *firsts, *seconds)


def on_device(*arguments):
    feats, spectral, target, valid_samples, stem_weights = arguments[:5]
    masters, firsts, seconds = arguments[5:13], arguments[13:21], arguments[21:29]
    n = lax.axis_size("tm")
    planes = lax.axis_size("seg")
    z = Sizes(n, planes, feats, spectral, target, masters[0], masters[4])
    S, T, D = z.segments, z.tokens, z.D
    place = lax.axis_index("tm")
    portion, member = place // S, place % S

    if z.direct:
        blobs = pack_weights(z, jnp.reshape(place, (1,)).astype(jnp.int32), masters)
        same_first = from_chips(z, blobs[0])
    else:
        weights = [lax.all_gather(a.astype(bfloat), "tm", axis=0, tiled=True) for a in masters[:7]]
        gains = lax.all_gather(masters[7].astype(bfloat), "tm", axis=1, tiled=True)
        weights.append(jnp.pad(gains.astype(float32), ((0, 3), (0, 0))))
    groups = None if z.parts == 1 else [[p * S + i for i in range(S)] for p in range(z.parts)]

    packed = pack_tokens(z, jnp.transpose(feats, (0, 2, 1)), spectral, target)
    if z.direct:
        packed, *same_first = lax.optimization_barrier((packed, *same_first))
    moved = lax.all_to_all(packed, "tm", 0, 0, axis_index_groups=groups, tiled=True)
    if z.direct:
        weights = [with_core(z, same_first)]
        blob, valid_samples, _ = lax.optimization_barrier((blobs[1], valid_samples, weights[0][1]))
        same_second = from_chips(z, blob)
    rows = z.tokens_dev
    spectral_all, target, halo = moved, moved, None
    if z.parts > 1:
        target = moved[:, :rows, D:]
        spectral_all = lax.all_gather(
            moved[:, :rows, :D].reshape(T, D), "tm", axis=0, tiled=True,
            axis_index_groups=[[p * S + i for p in range(z.parts)] for i in range(S)],
        )
        last = moved[S - 1, rows:, 4 * rows - 2 :].T.reshape(1, -1)
        lead = moved[0, rows:, :2].T.reshape(1, -1)
        halo = (
            lax.ppermute(jnp.pad(last, ((0, 15), (0, 0))), "tm", [(i, i + S) for i in range(n - S)]),
            lax.ppermute(jnp.pad(lead, ((0, 15), (0, 0))), "tm", [(i + S, i) for i in range(n - S)]),
        )
    local_count = jnp.sum(valid_samples)[None]
    if z.direct:
        counts = [local_count] + [lax.ppermute(local_count, "seg", pairs(planes, m)) for m in range(1, planes)]
        sample_count = tree_sum(counts).astype(float32)
    else:
        sample_count = lax.psum(local_count, "seg").astype(float32)
    meta = jnp.concatenate(
        [
            jnp.stack([portion * T, lax.dynamic_index_in_dim(valid_samples, member, keepdims=False)]),
            lax.dynamic_index_in_dim(stem_weights, member, keepdims=False),
            jnp.stack([place // 2, place % 2, lax.axis_index("seg")]),
        ]
    ).astype(jnp.int32)
    meta, sample_count = lax.optimization_barrier((meta, sample_count))

    x, stream, slope, normed, sn, q, k, v, att = front(z, meta, moved, spectral_all, halo, weights)
    if z.direct:
        att, *same_second = lax.optimization_barrier((att, *same_second))
        weights.append(with_core(z, same_second))
    second = middle(z, meta, sample_count, stream, att, target, weights)
    do, mid, misc = second[:3]
    done = 2
    dq, dkv = attend_back(z, q, k, v, do, done)
    if z.direct:
        second_blocks = over_core(z, second[3], second[4])
        dq, *second_blocks = lax.optimization_barrier((dq, *second_blocks))
    first = back(
        z, done, meta, q, k, v, do, dq, dkv, x, spectral_all, halo, stream, slope, normed, sn, mid, misc, weights
    )

    if z.direct:
        second_mine = over_plane(z, second_blocks)
        send, second_mine = lax.optimization_barrier((first[1], second_mine))
        first_blocks = over_core(z, first[0], send)
        second_parts = over_planes(z, second_mine)
        first_parts = over_planes(z, over_plane(z, first_blocks))
        first_sum, second_sum, both = square_sums(z, meta, first_parts, second_parts)
        both = both + lax.ppermute(both, "tm", pairs(n, 1))
        squares = [both] + [lax.ppermute(both, "tm", pairs(n, 2 * m)) for m in range(1, n // 2)]
        result = update(z, squares, first_sum, second_sum, masters, firsts, seconds)
        return (result[0].reshape(()), sample_count.reshape(()), result[1].reshape(()), *result[2:])

    grads = (first[0], first[1], first[2], second[3], second[4], second[5], second[6])
    shards = [lax.psum_scatter(g, "tm", scatter_dimension=0, tiled=True) for g in grads]
    shards.append(lax.psum_scatter(first[3][:5], "tm", scatter_dimension=1, tiled=True))
    reduced = lax.psum(tuple(shards), "seg")
    loss_sum = lax.psum(jnp.sum(first[3][5]), ("seg", "tm"))
    squares = lax.psum(sum(jnp.sum(shard * shard) for shard in reduced), "tm")
    grad_norm = jnp.sqrt(squares)
    factor = jnp.minimum(1.0, clip_limit / (grad_norm + 1e-06))
    updated = [
        adam_update(m, f, s, g, factor, r)
        for m, f, s, g, r in zip(masters, firsts, seconds, reduced, RATES)
    ]
    return (
        loss_sum, sample_count.reshape(()), grad_norm,
        *[u[0] for u in updated], *[u[1] for u in updated], *[u[2] for u in updated],
    )


def solution(mesh):
    rows, columns = P("tm", None), P(None, "tm")
    leaves = (rows,) * 7 + (columns,)
    tokens = P("seg", "tm", None)
    return jax.shard_map(
        on_device,
        mesh=mesh,
        in_specs=(tokens, tokens, tokens, P("seg"), P("seg", None)) + leaves * 3,
        out_specs=(P(), P(), P()) + leaves * 3,
        check_vma=False,
    )
```

```python
import functools
import jax
import jax.numpy as jnp
from jax import lax
from jax.experimental import pallas as pl
from jax.experimental.pallas import tpu as pltpu
from jax.sharding import PartitionSpec as P

H = 8
STEMS = 4
SUB = 16
STEP = 10
LANES = 128

clip_limit = 0.001
beta_first = 0.9
beta_second = 0.999
learn_rate = 0.03
fast_rate = 0.5
weight_decay = 0.05
adam_epsilon = 1e-08
norm_epsilon = 1e-05

bfloat = jnp.bfloat16
float32 = jnp.float32
VMEM_LIMIT = 60 * 1024 * 1024


def mm(left, right):
    return lax.dot_general(left, right, (((1,), (0,)), ((), ())), preferred_element_type=float32)


def nt(left, right):
    return lax.dot_general(left, right, (((1,), (1,)), ((), ())), preferred_element_type=float32)


def tn(left, right):
    return lax.dot_general(left, right, (((0,), (0,)), ((), ())), preferred_element_type=float32)


def iota(shape, dim):
    return lax.broadcasted_iota(jnp.int32, shape, dim)


def norm_parts(values):
    centred = values - jnp.mean(values, -1, keepdims=True)
    scale = lax.rsqrt(jnp.mean(centred * centred, -1, keepdims=True) + norm_epsilon)
    return centred * scale, scale


def norm_back(unit, scale, gain, upstream):
    inner = upstream * gain
    value_grad = scale * (
        inner
        - jnp.mean(inner, -1, keepdims=True)
        - unit * jnp.mean(inner * unit, -1, keepdims=True)
    )
    return value_grad, jnp.sum(upstream * unit, 0, keepdims=True)


def gelu_both(values):
    upper = 0.5 * (1.0 + lax.erf(values * 0.7071067811865476))
    density = jnp.exp(-0.5 * values * values) * 0.3989422804014327
    return values * upper, upper + values * density


def spread_matrix(width, head_size):
    shape = (width, width // head_size * LANES)
    lane = iota(shape, 1)
    inside = lane % LANES
    source = (lane // LANES) * head_size + inside
    hit = jnp.logical_and(iota(shape, 0) == source, inside < head_size)
    return jnp.where(hit, 1.0, 0.0).astype(bfloat)


def with_column(block, column, head_size):
    lane = iota(block.shape, 1)
    high = column.astype(bfloat).astype(float32)
    rest = column - high
    middle = rest.astype(bfloat).astype(float32)
    low = rest - middle
    pieces = jnp.where(lane == head_size, high, jnp.where(lane == head_size + 1, middle, low))
    spare = jnp.logical_and(lane >= head_size, lane < head_size + 3)
    return jnp.where(spare, pieces, block.astype(float32)).astype(bfloat)


class Sizes:
    def __init__(self, n, planes, feats, spectral, target, conv_weight, up_weight):
        self.n = n
        self.planes = planes
        self.segments = feats.shape[0]
        self.parts = n // self.segments
        self.channels = feats.shape[2]
        self.tokens_dev = spectral.shape[1]
        self.D = spectral.shape[2]
        self.taps = conv_weight.shape[0] * n
        self.frame = self.taps // 2
        self.F = up_weight.shape[1]
        self.out = target.shape[2]
        self.tokens = self.segments * self.tokens_dev
        self.keys = self.tokens * self.parts
        self.hd = self.D // H
        self.wide = H * LANES
        self.w = self.D // n
        self.cw = self.taps // n
        self.uw = self.w * (self.F // self.D)
        self.fw = self.F // n
        self.hw = self.w * self.out // self.D
        self.first_rows = self.cw + 3 * self.w + 16
        self.second_rows = self.w + self.uw + self.fw + self.hw
        step = 16 * planes
        self.first_grads = -(-self.first_rows // step) * step
        self.second_grads = -(-self.second_rows // step) * step
        self.direct = self.parts == 1 and self.w % 16 == 0 and self.hw % 16 == 0 and self.hw > 0
        self.block = 256
        self.middle_block = 512
        self.query_block = 1024 if self.keys <= 1024 else 256


def smem():
    return pl.BlockSpec(memory_space=pltpu.SMEM)


def anywhere():
    return pl.BlockSpec(memory_space=pl.ANY)


def whole(shape):
    return pl.BlockSpec(shape, lambda i: (0,) * len(shape))


def pack_weights(z, tm_place, masters):
    D, w, O, cw = z.D, z.w, z.out, z.cw

    def kernel(place_ref, conv_r, query_r, keyval_r, out_r, up_r, down_r, head_r, gains_r, first_o, second_o):
        first_o[:cw, :] = conv_r[...].astype(bfloat)
        first_o[cw : cw + w, :] = query_r[...].astype(bfloat)
        first_o[cw + w : cw + 2 * w, :] = keyval_r[:, :D].astype(bfloat)
        first_o[cw + 2 * w : cw + 3 * w, :] = keyval_r[:, D:].astype(bfloat)
        start = place_ref[0] * w
        shift = jnp.where(iota((w, D), 1) == iota((w, D), 0) + start, 1.0, 0.0).astype(bfloat)
        placed = mm(gains_r[...].astype(bfloat), shift)
        padded = jnp.concatenate([placed, jnp.zeros((16 - placed.shape[0], D), float32)], 0)
        first_o[cw + 3 * w :, :] = padded.astype(bfloat)
        second_o[:w, :] = out_r[...].astype(bfloat)
        for c in range(z.F // D):
            second_o[w + c * w : 2 * w + c * w, :] = up_r[:, c * D : (c + 1) * D].astype(bfloat)
        row = w + z.uw
        second_o[row : row + z.fw, :] = down_r[...].astype(bfloat)
        row += z.fw
        for g in range(D // O):
            here = head_r[g * z.hw : (g + 1) * z.hw, :]
            second_o[row : row + z.hw, g * O : (g + 1) * O] = here.astype(bfloat)

    vmem = pl.BlockSpec(memory_space=pltpu.VMEM)
    return pl.pallas_call(
        kernel,
        out_shape=[
            jax.ShapeDtypeStruct((z.first_rows, D), bfloat),
            jax.ShapeDtypeStruct((z.second_rows, D), bfloat),
        ],
        in_specs=[smem()] + [vmem] * 8,
        out_specs=[vmem] * 2,
        name="pack_weights",
    )(tm_place, *masters)


def pack_tokens(z, feats, spectral, target):
    rows, D, C = z.tokens_dev, z.D, z.channels

    def kernel(f_ref, s_ref, t_ref, o_ref, buffer, in_sem, out_sem):
        arriving, leaving = [], []
        for i in range(z.segments):
            arriving.append(
                [
                    pltpu.make_async_copy(f_ref.at[i], buffer.at[i, rows:, :], in_sem.at[i, 0]),
                    pltpu.make_async_copy(s_ref.at[i], buffer.at[i, :rows, :D], in_sem.at[i, 1]),
                    pltpu.make_async_copy(t_ref.at[i], buffer.at[i, :rows, D:], in_sem.at[i, 2]),
                ]
            )
            leaving.append(pltpu.make_async_copy(buffer.at[i], o_ref.at[i], out_sem.at[i]))
            for copy in arriving[i]:
                copy.start()
        for i in range(z.segments):
            for copy in arriving[i]:
                copy.wait()
            leaving[i].start()
        for copy in leaving:
            copy.wait()

    shape = (z.segments, rows + C, 4 * rows)
    return pl.pallas_call(
        kernel,
        out_shape=jax.ShapeDtypeStruct(shape, bfloat),
        in_specs=[anywhere()] * 3,
        out_specs=anywhere(),
        scratch_shapes=[
            pltpu.VMEM(shape, bfloat),
            pltpu.SemaphoreType.DMA((z.segments, 3)),
            pltpu.SemaphoreType.DMA((z.segments,)),
        ],
        compiler_params=pltpu.CompilerParams(vmem_limit_bytes=VMEM_LIMIT),
        name="pack_tokens",
    )(feats, spectral, target)


def spectral_copies(z, source, home, sem, first):
    if z.parts > 1:
        return [pltpu.make_async_copy(source, home, sem.at[first])]
    rows = z.tokens_dev
    return [
        pltpu.make_async_copy(source.at[i, :rows, : z.D], home.at[i * rows : (i + 1) * rows, :], sem.at[first + i])
        for i in range(z.segments)
    ]


def share_copies(z, meta_ref, shares, home, rows, sem, first):
    place = meta_ref[6] * 2 + meta_ref[7]
    return [
        pltpu.make_async_copy(share.at[rows], home.at[place ^ x], sem.at[first + x])
        for x, share in enumerate(shares)
    ]


def front(z, meta, moved, spectral, halo, weights):
    D, T, K, W, B = z.D, z.tokens, z.keys, z.wide, z.block
    frame, taps, hd = z.frame, z.taps, z.hd
    half = frame // 2
    QB = z.query_block
    count = z.tokens_dev
    CB = 2 * LANES
    extra = 2 if z.parts > 1 else 0
    n_weights = z.n if z.direct else 4

    def kernel(meta_ref, *refs):
        refs = list(refs)
        frames_ref, sp_ref = refs[:2]
        before_after = refs[2 : 2 + extra]
        weight_refs = refs[2 + extra : 2 + extra + n_weights]
        refs = refs[2 + extra + n_weights :]
        (x_o, stream_o, slope_o, normed_o, sn_o, q_o, k_o, v_o, att_o) = refs[:9]
        (frames_s, sp_s, x_s, stream_s, slope_s, normed_s, sn_s) = refs[9:16]
        (conv_s, wq_s, wk_s, wv_s, q_s, k_s, v_s, in_sem, out_sem) = refs[16:25]
        refs = refs[25:]
        h = pl.program_id(0)
        outgoing = [
            pltpu.make_async_copy(src, dst, out_sem.at[i])
            for i, (src, dst) in enumerate(
                ((x_s, x_o), (stream_s, stream_o), (slope_s, slope_o), (normed_s, normed_o), (sn_s, sn_o))
            )
        ]

        @pl.when(h == 0)
        def _():
            frames_copy = pltpu.make_async_copy(frames_ref.at[:, count:, :], frames_s, in_sem.at[0])
            spectral_in = spectral_copies(z, sp_ref, sp_s, in_sem, 1)
            if z.direct:
                blob_s, wc, wqkv = refs
                blob_in = share_copies(z, meta_ref, weight_refs, blob_s, slice(0, z.first_rows), in_sem, 1 + z.segments)
                for copy in blob_in:
                    copy.start()
            for copy in spectral_in:
                copy.start()
            frames_copy.start()
            if z.direct:
                for copy in blob_in:
                    copy.wait()
                w, cw = z.w, z.cw
                total = jnp.zeros((16, D), float32)
                for j in range(z.n):
                    wc[j * cw : (j + 1) * cw, :] = blob_s[j, 0:cw, :]
                    for c in range(3):
                        first = cw + c * w
                        wqkv[j * w : (j + 1) * w, c * D : (c + 1) * D] = blob_s[j, first : first + w, :]
                    total = total + blob_s[j, cw + 3 * w : cw + 3 * w + 16, :].astype(float32)
                gain_query, gain_keys = total[0:1, :], total[1:2, :]
                parts_w = [wqkv[:, c * D : (c + 1) * D] for c in range(3)]
            else:
                wc, wq, wkv, gains_ref = weight_refs
                gain_query, gain_keys = gains_ref[0:1, :], gains_ref[1:2, :]
                parts_w = [wq[...], wkv[:, :D], wkv[:, D:]]
            spread = spread_matrix(D, hd)
            for target_s, part in zip((wq_s, wk_s, wv_s), parts_w):
                target_s[...] = mm(part, spread).astype(bfloat)
            for copy in spectral_in:
                copy.wait()

            def key_block(i, carry):
                rows = pl.ds(pl.multiple_of(i * B, B), B)
                unit, _ = norm_parts(sp_s[rows, :].astype(float32))
                sn_s[rows, :] = (unit * gain_keys).astype(bfloat)
                return carry

            lax.fori_loop(0, K // B, key_block, 0)
            outgoing[4].start()
            inside = iota((K, CB), 1) % LANES
            spare = jnp.logical_and(inside >= hd, inside < hd + 3)
            for home, part in ((k_s, wk_s), (v_s, wv_s)):
                for c in range(0, W, CB):
                    product = mm(sn_s[...], part[:, c : c + CB])
                    home[:, c : c + CB] = jnp.where(spare, -1.0, product).astype(bfloat)
            frames_copy.wait()
            shape = (4 * count, 4 * count)
            row, column = iota(shape, 0), iota(shape, 1)
            order = jnp.where(column == (row % count) * 4 + row // count, 1.0, 0.0).astype(bfloat)
            for i in range(z.segments):
                taps_rows = nt(order, frames_s[i])
                x_s[i * count : (i + 1) * count, :] = jnp.concatenate(
                    [taps_rows[j * count : (j + 1) * count, :] for j in range(4)], 1
                ).astype(bfloat)
            outgoing[0].start()
            conv_s[...] = mm(x_s[...], wc[half : half + frame, :])
            row = iota((T, D), 0)
            older = pltpu.roll(mm(x_s[:, half:], wc[:half, :]), 1, 0)
            first_row, last_row = 0.0, 0.0
            if z.parts > 1:
                first_row = mm(before_after[0][...], wc[:half, :])[0:1, :]
                last_row = mm(before_after[1][...], wc[half + frame :, :])[0:1, :]
            conv_s[...] += jnp.where(row == 0, first_row, older)
            newer = pltpu.roll(mm(x_s[:, :half], wc[half + frame :, :]), T - 1, 0)
            conv_s[...] += jnp.where(row == T - 1, last_row, newer)

            def token_block(i, carry):
                rows = pl.ds(pl.multiple_of(i * B, B), B)
                stream, slope = gelu_both(conv_s[rows, :])
                stream_s[rows, :] = stream
                slope_s[rows, :] = slope
                unit, _ = norm_parts(stream)
                normed = (unit * gain_query).astype(bfloat)
                normed_s[rows, :] = normed
                return carry

            lax.fori_loop(0, T // B, token_block, 0)
            for c in range(0, W, CB):
                q_s[:, c : c + CB] = mm(normed_s[...], wq_s[:, c : c + CB]).astype(bfloat)
            for copy in outgoing[1:4]:
                copy.start()

        lanes = pl.ds(pl.multiple_of(h * LANES, LANES), LANES)
        k_o[...] = k_s[:, lanes]
        v_o[...] = v_s[:, lanes]
        def finish(rows, count, grown, top):
            q = q_s[rows, lanes]
            mass = jnp.sum(grown, 0, keepdims=True)
            probs = (grown * (1.0 / mass)).astype(bfloat)
            total = top + jnp.log(mass)
            result = tn(v_o[...], probs)
            high = total.astype(bfloat).astype(float32)
            rest = total - high
            mid = rest.astype(bfloat).astype(float32)
            sub = iota((LANES, count), 0)
            spare = jnp.where(sub == hd, high, jnp.where(sub == hd + 1, mid, rest - mid))
            spare = jnp.where(sub < hd + 3, spare, 0.0)
            both = jnp.where(sub < hd, result, spare).T
            att_o[rows, :] = both.astype(bfloat)
            lane = iota((count, LANES), 1)
            q_o[rows, :] = jnp.where(lane < hd, q.astype(float32), both).astype(bfloat)
            return mass

        least, most = jnp.inf, 0.0
        for b in range(T // QB):
            rows = slice(b * QB, (b + 1) * QB)
            mass = finish(rows, QB, jnp.exp(nt(k_o[...], q_s[rows, lanes])), 0.0)
            least = jnp.minimum(least, jnp.min(mass))
            most = jnp.maximum(most, jnp.max(mass))
        safe = jnp.logical_and(least > 1e-20, most < 1e30)

        @pl.when(jnp.logical_not(safe))
        def _():
            def again(i, carry):
                rows = pl.ds(pl.multiple_of(i * LANES, LANES), LANES)
                scores = nt(k_o[...], q_s[rows, lanes])
                top = jnp.max(scores, 0, keepdims=True)
                finish(rows, LANES, jnp.exp(scores - top), top)
                return carry

            lax.fori_loop(0, T // LANES, again, 0)

        @pl.when(h == H - 1)
        def _():
            for copy in outgoing:
                copy.wait()

    def lanes_of(rows):
        return pl.BlockSpec((rows, LANES), lambda h: (0, h))

    in_specs = [smem(), anywhere(), anywhere()]
    args = [meta, moved, moved if z.parts == 1 else spectral]
    if z.parts > 1:
        args += list(halo)
        in_specs += [whole((16, D))] * 2
    scratch = [
        pltpu.VMEM((z.segments, z.channels, 4 * count), bfloat),
        pltpu.VMEM((K, D), bfloat),
        pltpu.VMEM((T, frame), bfloat),
        pltpu.VMEM((T, D), float32),
        pltpu.VMEM((T, D), float32),
        pltpu.VMEM((T, D), bfloat),
        pltpu.VMEM((K, D), bfloat),
        pltpu.VMEM((T, D), float32),
        pltpu.VMEM((D, W), bfloat),
        pltpu.VMEM((D, W), bfloat),
        pltpu.VMEM((D, W), bfloat),
        pltpu.VMEM((T, W), bfloat),
        pltpu.VMEM((K, W), bfloat),
        pltpu.VMEM((K, W), bfloat),
        pltpu.SemaphoreType.DMA((1 + z.segments + z.n,)),
        pltpu.SemaphoreType.DMA((5,)),
    ]
    if z.direct:
        args += weights[0]
        in_specs += [anywhere()] * z.n
        scratch += [
            pltpu.VMEM((z.n, z.first_rows, D), bfloat),
            pltpu.VMEM((taps, D), bfloat),
            pltpu.VMEM((D, 3 * D), bfloat),
        ]
    else:
        for array in (weights[0], weights[1], weights[2], weights[7]):
            args.append(array)
            in_specs.append(whole(array.shape))
    shapes = [
        ((T, frame), bfloat),
        ((T, D), float32),
        ((T, D), float32),
        ((T, D), bfloat),
        ((K, D), bfloat),
        ((T, W), bfloat),
        ((K, W), bfloat),
        ((K, W), bfloat),
        ((T, W), bfloat),
    ]
    return pl.pallas_call(
        kernel,
        grid=(H,),
        out_shape=[jax.ShapeDtypeStruct(s, d) for s, d in shapes],
        in_specs=in_specs,
        out_specs=[anywhere()] * 5 + [lanes_of(T), lanes_of(K), lanes_of(K), lanes_of(T)],
        scratch_shapes=scratch,
        compiler_params=pltpu.CompilerParams(vmem_limit_bytes=VMEM_LIMIT),
        cost_estimate=pl.CostEstimate(flops=20_000_000_000, bytes_accessed=20_000_000, transcendentals=10_000_000),
        name="front",
    )(*args)


def emit_blocks(z, meta_ref, keep_o, send_o, sources):
    chip, core, plane = meta_ref[6], meta_ref[7], meta_ref[8]
    quarter = keep_o.shape[2]

    def write(out, m, row, here, lanes):
        first = 0
        while first < here.shape[0]:
            part, inside = divmod(row + first, quarter)
            size = min(here.shape[0] - first, quarter - inside)
            out[m, part ^ plane, inside : inside + size, lanes] = here[first : first + size].astype(out.dtype)
            first += size

    for m in range(z.n // 2):
        owner = (chip ^ m) * 2
        for out, place in ((keep_o, owner + core), (send_o, owner + 1 - core)):
            row = 0
            for ref, rows, pieces in sources:
                width = ref.shape[-1]
                if width >= z.D:
                    start = pl.multiple_of(place * rows, 16)
                    for lane in range(0, width, z.D):
                        write(out, m, row, ref[pl.ds(start, rows), lane : lane + z.D], slice(0, z.D))
                        row += rows
                else:
                    size = rows // pieces
                    for g in range(pieces):
                        start = pl.multiple_of(place * rows + g * size, 16)
                        write(out, m, row, ref[pl.ds(start, size), :], slice(g * width, (g + 1) * width))
                    row += size
            if row < quarter * z.planes:
                rest = quarter * z.planes - row
                write(out, m, row, jnp.zeros((rest, z.D), float32), slice(0, z.D))


def block_shapes(z, rows):
    shape = (z.n // 2, z.planes, rows // z.planes, z.D)
    return [(shape, float32), (shape, bfloat)]


def middle(z, meta, count, stream, att, target, weights):
    D, T, W, F, O = z.D, z.tokens, z.wide, z.F, z.out
    B = z.middle_block
    hd = z.hd

    def kernel(meta_ref, count_ref, stream_ref, att_ref, target_ref, *refs):
        refs = list(refs)
        if z.direct:
            first_refs, second_refs = refs[: z.n], refs[z.n : 2 * z.n]
            refs = refs[2 * z.n :]
            do_out, mid_out, misc_o, keep_o, send_o = refs[:5]
            refs = refs[5:]
        else:
            wo, wu, wd, wh, gains_ref = refs[:5]
            do_out, mid_out, misc_o, go_s, gu_s, gd_s, gh_s = refs[5:12]
            refs = refs[12:]
        wop, att_s, stream_s, do_o, mid_o, act_s, hg_s, fin_s, fg_s, low_s, pg_s, bg_s, sem = refs[:13]
        refs = refs[13:]
        if z.direct:
            go_s, gu_s, gd_s, gh_s, blob_s, gain_s, wo, wu, wd, wh = refs

        att_copy = pltpu.make_async_copy(att_ref, att_s, sem.at[0])
        stream_copy = pltpu.make_async_copy(stream_ref, stream_s, sem.at[1])
        if z.direct:
            w, uw, fw, hw = z.w, z.uw, z.fw, z.hw
            ends = (0, w, w + uw, w + uw + fw, z.second_rows)
            pieces = [
                share_copies(z, meta_ref, second_refs, blob_s.at[:, p:q], slice(p, q), sem, 9 + c * z.n)
                for c, (p, q) in enumerate(zip(ends[:-1], ends[1:]))
            ]
            last = slice(z.first_rows - 16, z.first_rows)
            gain_in = share_copies(z, meta_ref, first_refs, gain_s, last, sem, 9 + 4 * z.n)
            for copy in pieces[0] + gain_in:
                copy.start()
        att_copy.start()
        stream_copy.start()
        if z.direct:
            for piece in pieces[1:]:
                for copy in piece:
                    copy.start()
            for copy in pieces[0] + gain_in:
                copy.wait()
            total = jnp.zeros((16, D), float32)
            for j in range(z.n):
                wo[j * w : (j + 1) * w, :] = blob_s[j, 0:w, :]
                total = total + gain_s[j].astype(float32)
        else:
            total = gains_ref[...]
        wop[...] = tn(spread_matrix(D, hd), wo[...]).astype(bfloat)
        misc_o[...] = jnp.zeros_like(misc_o)
        gain_ffn, scale_attn, scale_ffn = total[2:3, :], total[3:4, :], total[4:5, :]
        base, valid = meta_ref[0], meta_ref[1]
        samples = count_ref[0]
        att_copy.wait()
        stream_copy.wait()
        if z.direct:
            for copy in pieces[1]:
                copy.wait()
            for j in range(z.n):
                for c in range(F // D):
                    first = w + c * w
                    wu[j * w : (j + 1) * w, c * D : (c + 1) * D] = blob_s[j, first : first + w, :]
        if z.direct:
            for copy in pieces[2] + pieces[3]:
                copy.wait()
            for j in range(z.n):
                wd[j * fw : (j + 1) * fw, :] = blob_s[j, w + uw : w + uw + fw, :]
                for g in range(D // O):
                    start = j * w + g * hw
                    wh[start : start + hw, :] = blob_s[j, w + uw + fw :, g * O : (g + 1) * O]
        chunks = B // z.tokens_dev

        def block(i, carry):
            rows = pl.ds(pl.multiple_of(i * B, B), B)
            branch = mm(att_s[rows, :], wop[...])
            stream_mid = stream_s[rows, :] + scale_attn * branch
            unit, scale = norm_parts(stream_mid)
            ffn_in = (unit * gain_ffn).astype(bfloat)
            fin_s[rows, :] = ffn_in
            hidden = mm(ffn_in, wu[...])
            active, slope = gelu_both(hidden)
            active = active.astype(bfloat)
            act_s[rows, :] = active
            ffn_out = mm(active, wd[...])
            stream_low = (stream_mid + scale_ffn * ffn_out).astype(bfloat)
            low_s[rows, :] = stream_low
            predicted = mm(stream_low, wh[...])
            column = iota((B, O), 1)
            position = (base + i * B + iota((B, O), 0)) * SUB + column % SUB
            stem = column // (2 * SUB)
            weight = jnp.zeros((B, O), float32)
            for k in range(STEMS):
                weight = jnp.where(stem == k, meta_ref[2 + k].astype(float32), weight)
            weight = jnp.where(position < valid, weight, 0.0)
            error = predicted - target_ref[pl.ds(i * chunks, chunks)].reshape(B, O).astype(float32)
            root = jnp.sqrt(error * error + 1.0)
            misc_o[5:6, :O] += jnp.sum(weight * (root - 1.0), 0, keepdims=True)
            predicted_grad = (weight * error / root / samples).astype(bfloat)
            pg_s[rows, :] = predicted_grad
            end_grad = nt(predicted_grad, wh[...])
            misc_o[4:5, :] += jnp.sum(end_grad * ffn_out, 0, keepdims=True)
            ffn_grad = (scale_ffn * end_grad).astype(bfloat)
            fg_s[rows, :] = ffn_grad
            hidden_grad = (nt(ffn_grad, wd[...]) * slope).astype(bfloat)
            hg_s[rows, :] = hidden_grad
            mid_part, gain_grad = norm_back(unit, scale, gain_ffn, nt(hidden_grad, wu[...]))
            misc_o[2:3, :] += gain_grad
            mid_grad = end_grad + mid_part
            mid_o[rows, :] = mid_grad
            misc_o[3:4, :] += jnp.sum(mid_grad * branch, 0, keepdims=True)
            branch_grad = (scale_attn * mid_grad).astype(bfloat)
            bg_s[rows, :] = branch_grad
            att_grad = nt(branch_grad, wop[...]).astype(bfloat)
            for h in range(H):
                lanes = slice(h * LANES, (h + 1) * LANES)
                one = att_grad[:, lanes].astype(float32)
                delta = jnp.sum(one * att_s[rows, lanes].astype(float32), -1, keepdims=True)
                do_o[rows, lanes] = with_column(one, delta, hd)
            return carry

        lax.fori_loop(0, T // B, block, 0)
        outgoing = [
            pltpu.make_async_copy(do_o, do_out, sem.at[7]),
            pltpu.make_async_copy(mid_o, mid_out, sem.at[8]),
        ]
        for copy in outgoing:
            copy.start()
        spare_grad = tn(att_s[...], bg_s[...])
        for h in range(H):
            go_s[h * hd : (h + 1) * hd, :] = spare_grad[h * LANES : h * LANES + hd, :]
        gu_s[...] = tn(fin_s[...], hg_s[...])
        gd_s[...] = tn(act_s[...], fg_s[...])
        gh_s[...] = tn(low_s[...], pg_s[...])
        if z.direct:
            emit_blocks(
                z,
                meta_ref,
                keep_o,
                send_o,
                ((go_s, z.w, 1), (gu_s, z.w, 1), (gd_s, z.fw, 1), (gh_s, z.w, D // O)),
            )
        for copy in outgoing:
            copy.wait()

    if z.parts == 1:
        target_spec = pl.BlockSpec((z.segments, z.tokens_dev, O), lambda i: (0, 0, D // O))
    else:
        target_spec = whole(target.shape)
    in_specs = [smem(), smem(), anywhere(), anywhere(), target_spec]
    args = [meta, count, stream, att, target]
    scratch = [
        pltpu.VMEM((W, D), bfloat),
        pltpu.VMEM((T, W), bfloat),
        pltpu.VMEM((T, D), float32),
        pltpu.VMEM((T, W), bfloat),
        pltpu.VMEM((T, D), float32),
        pltpu.VMEM((T, F), bfloat),
        pltpu.VMEM((T, F), bfloat),
        pltpu.VMEM((T, D), bfloat),
        pltpu.VMEM((T, D), bfloat),
        pltpu.VMEM((T, D), bfloat),
        pltpu.VMEM((T, O), bfloat),
        pltpu.VMEM((T, D), bfloat),
        pltpu.SemaphoreType.DMA((9 + 5 * z.n,)),
    ]
    shapes = [((T, W), bfloat), ((T, D), float32), ((8, D), float32)]
    grads = [((D, D), float32), ((D, F), float32), ((F, D), float32), ((D, O), float32)]
    if z.direct:
        args += weights[0] + weights[1]
        in_specs += [anywhere()] * (2 * z.n)
        scratch += [pltpu.VMEM(s, d) for s, d in grads] + [
            pltpu.VMEM((z.n, z.second_rows, D), bfloat),
            pltpu.VMEM((z.n, 16, D), bfloat),
            pltpu.VMEM((D, D), bfloat),
            pltpu.VMEM((D, F), bfloat),
            pltpu.VMEM((F, D), bfloat),
            pltpu.VMEM((D, O), bfloat),
        ]
        shapes += block_shapes(z, z.second_grads)
    else:
        for array in weights[3:]:
            args.append(array)
            in_specs.append(whole(array.shape))
        shapes += grads
    return pl.pallas_call(
        kernel,
        grid=(1,),
        out_shape=[jax.ShapeDtypeStruct(s, d) for s, d in shapes],
        in_specs=in_specs,
        out_specs=[anywhere(), anywhere()] + [whole(s) for s, d in shapes[2:]],
        scratch_shapes=scratch,
        compiler_params=pltpu.CompilerParams(vmem_limit_bytes=VMEM_LIMIT),
        cost_estimate=pl.CostEstimate(flops=20_000_000_000, bytes_accessed=20_000_000, transcendentals=4_000_000),
        name="middle",
    )(*args)


def head_back(z, q_ref, k_ref, v_ref, do_ref, put_query, dk_s, dv_s):
    T, hd = z.tokens, z.hd
    QB = 256 if z.keys <= 1024 else 128
    dk_s[...] = jnp.zeros_like(dk_s)
    dv_s[...] = jnp.zeros_like(dv_s)

    def block(i, carry):
        for b in range(2):
            rows = pl.ds(pl.multiple_of((i * 2 + b) * QB, QB), QB)
            q, do = q_ref[rows, :], do_ref[rows, :]
            probs = jnp.exp(nt(q, k_ref[...]))
            score_grad = (probs * nt(do, v_ref[...])).astype(bfloat)
            low = probs.astype(bfloat)
            put_query(rows, mm(score_grad, k_ref[...]).astype(bfloat))
            dk_s[...] += tn(q, score_grad)[:hd, :]
            dv_s[...] += tn(do, low)[:hd, :]
        return carry

    lax.fori_loop(0, T // (2 * QB), block, 0)
    return dk_s[...].astype(bfloat), dv_s[...].astype(bfloat)


def attend_back(z, q, k, v, do, heads):
    T, K, W, D = z.tokens, z.keys, z.wide, z.D
    hd = z.hd

    def kernel(q_ref, k_ref, v_ref, do_ref, dq_o, dkv_o, dk_s, dv_s):
        def put_query(rows, value):
            dq_o[rows, :] = value

        dkv_o[0], dkv_o[1] = head_back(z, q_ref, k_ref, v_ref, do_ref, put_query, dk_s, dv_s)

    def lanes(rows):
        return pl.BlockSpec((rows, LANES), lambda h: (0, h))

    return pl.pallas_call(
        kernel,
        grid=(heads,),
        out_shape=[
            jax.ShapeDtypeStruct((T, heads * LANES), bfloat),
            jax.ShapeDtypeStruct((2, heads * hd, K), bfloat),
        ],
        in_specs=[lanes(T), lanes(K), lanes(K), lanes(T)],
        out_specs=[lanes(T), pl.BlockSpec((2, hd, K), lambda h: (0, h, 0))],
        scratch_shapes=[pltpu.VMEM((hd, K), float32)] * 2,
        compiler_params=pltpu.CompilerParams(vmem_limit_bytes=VMEM_LIMIT),
        cost_estimate=pl.CostEstimate(
            flops=heads * 4_000_000_000, bytes_accessed=12_000_000, transcendentals=heads * 1_000_000
        ),
        name="attend_back",
    )(q, k, v, do)


def back(z, done, meta, q, k, v, do, dq, dkv, x, spectral, halo, stream, slope, normed, sn, mid, misc, weights):
    D, T, K, W, B, O = z.D, z.tokens, z.keys, z.wide, z.block, z.out
    frame, taps, hd = z.frame, z.taps, z.hd
    half = frame // 2
    steps = H - done
    extra = 2 if z.parts > 1 else 0
    n_weights = z.n if z.direct else 3
    n_out = 2 if z.direct else 4

    def kernel(meta_ref, q_ref, k_ref, v_ref, do_ref, misc_ref, *refs):
        refs = list(refs)
        before_after = refs[:extra]
        remote = refs[extra : extra + 9]
        refs = refs[extra + 9 :]
        weight_refs, refs = refs[:n_weights], refs[n_weights:]
        outs, refs = refs[:n_out], refs[n_out:]
        (dq_s, dkv_s, x_ref, sp_ref, stream_ref, slope_ref, normed_ref, sn_ref, mid_ref) = refs[:9]
        refs = refs[9:]
        cg_s, dn_s, dqc_s, dkvt_s, dk_s, dv_s, sem = refs[:7]
        refs = refs[7:]
        if z.direct:
            gc_s, gq_s, gkv_s, misc_s, place_s, blob_s, wq, wkv = refs
        else:
            gc_s, gq_s, gkv_s, misc_s = outs
            wq, wkv, gains_ref = weight_refs
        i = pl.program_id(0)
        old = done * LANES
        homes = [dq_s.at[:, :old], dkv_s.at[:, : done * hd]] + [
            x_ref, sp_ref, stream_ref, slope_ref, normed_ref, sn_ref, mid_ref
        ]
        copies = [
            pltpu.make_async_copy(a, b, sem.at[c])
            for c, (a, b) in enumerate(zip(remote, homes))
            if c != 3
        ]
        copies += spectral_copies(z, remote[3], sp_ref, sem, 10)
        if z.direct:
            copies += share_copies(
                z, meta_ref, weight_refs, blob_s, slice(z.cw, z.first_rows), sem, 10 + z.segments
            )

        @pl.when(i == 0)
        def _():
            for copy in copies:
                copy.start()

        lanes = pl.ds(pl.multiple_of((i + done) * LANES, LANES), LANES)

        def put_query(rows, value):
            dq_s[rows, lanes] = value

        dk, dv = head_back(z, q_ref, k_ref, v_ref, do_ref, put_query, dk_s, dv_s)
        here = pl.ds(pl.multiple_of((i + done) * hd, 16), hd)
        dkv_s[0, here, :] = dk
        dkv_s[1, here, :] = dv

        @pl.when(i == steps - 1)
        def _():
            for copy in copies:
                copy.wait()
            if z.direct:
                w = z.w
                total = jnp.zeros((16, D), float32)
                for j in range(z.n):
                    here = slice(j * w, (j + 1) * w)
                    wq[here, :] = blob_s[j, 0:w, :]
                    wkv[here, :D] = blob_s[j, w : 2 * w, :]
                    wkv[here, D:] = blob_s[j, 2 * w : 3 * w, :]
                    total = total + blob_s[j, 3 * w :, :].astype(float32)
            else:
                total = gains_ref[...]
            gain_query = total[0:1, :]
            misc_s[...] = misc_ref[...]
            dqc_s[...] = nt(dq_s[...], spread_matrix(D, hd)).astype(bfloat)
            dkvt_s[:, :D] = dkv_s[0].T
            dkvt_s[:, D:] = dkv_s[1].T
            gkv_s[...] = tn(sn_ref[...], dkvt_s[...])
            gq_s[...] = tn(normed_ref[...], dqc_s[...])

            for c in range(K // T):
                cg_s[...] = nt(dkvt_s[c * T : (c + 1) * T, :], wkv[...])
                for i in range(T // B):
                    rows = slice(i * B, (i + 1) * B)
                    unit, _ = norm_parts(sp_ref[c * T + i * B : c * T + (i + 1) * B, :].astype(float32))
                    misc_s[1:2, :] += jnp.sum(cg_s[rows, :] * unit, 0, keepdims=True)
            dn_s[...] = nt(dqc_s[...], wq[...])
            for i in range(T // B):
                rows = slice(i * B, (i + 1) * B)
                unit, scale = norm_parts(stream_ref[rows, :])
                part, gain_grad = norm_back(unit, scale, gain_query, dn_s[rows, :])
                misc_s[0:1, :] += gain_grad
                conv_grad = (mid_ref[rows, :] + part) * slope_ref[rows, :]
                cg_s[rows, :] = conv_grad.astype(bfloat).astype(float32)
            conv_grad = cg_s[...]
            gc_s[half : half + frame, :] = tn(x_ref[...], conv_grad.astype(bfloat))
            row = iota((T, D), 0)
            later = jnp.where(row == T - 1, 0.0, pltpu.roll(conv_grad, T - 1, 0)).astype(bfloat)
            gc_s[:half, :] = tn(x_ref[:, half:], later)
            sooner = jnp.where(row == 0, 0.0, pltpu.roll(conv_grad, 1, 0)).astype(bfloat)
            gc_s[half + frame :, :] = tn(x_ref[:, :half], sooner)
            if z.parts > 1:
                first = iota((16, D), 0) == 0
                top = jnp.where(first, conv_grad[0:16, :], 0.0).astype(bfloat)
                gc_s[:half, :] += tn(before_after[0][...], top)
                tail = jnp.where(first, pltpu.roll(conv_grad[T - 16 :, :], 1, 0), 0.0)
                gc_s[half + frame :, :] += tn(before_after[1][...], tail.astype(bfloat))
            if z.direct:
                for j in range(z.n):
                    row, lane = iota((D, LANES), 0), iota((D, LANES), 1)
                    hit = jnp.logical_and(row == lane + j * z.w, lane < z.w)
                    chosen = lax.dot_general(
                        misc_s[...], jnp.where(hit, 1.0, 0.0), (((1,), (0,)), ((), ())),
                        precision=lax.Precision.HIGHEST, preferred_element_type=float32,
                    )
                    low_rows = jnp.where(iota((8, LANES), 0) == 5, misc_s[:, :LANES], chosen)
                    place_s[j * 16 : (j + 1) * 16, :] = jnp.zeros((16, D), float32)
                    place_s[j * 16 : j * 16 + 8, :LANES] = low_rows
                emit_blocks(
                    z, meta_ref, outs[0], outs[1],
                    ((gc_s, z.cw, 1), (gq_s, z.w, 1), (gkv_s, z.w, 1), (place_s, 16, 1)),
                )

    def lanes_of(rows):
        return pl.BlockSpec((rows, LANES), lambda i: (0, i + done))

    args = [meta, q, k, v, do, misc]
    in_specs = [smem(), lanes_of(T), lanes_of(K), lanes_of(K), lanes_of(T), whole(misc.shape)]
    if z.parts > 1:
        args += list(halo)
        in_specs += [whole((16, D))] * 2
    remote = (dq, dkv, x, spectral, stream, slope, normed, sn, mid)
    args += list(remote)
    in_specs += [anywhere()] * 9
    scratch = [pltpu.VMEM((T, W), bfloat), pltpu.VMEM((2, D, K), bfloat)]
    homes = (x.shape, (K, D)) + tuple(a.shape for a in remote[4:])
    scratch += [pltpu.VMEM(s, a.dtype) for s, a in zip(homes, remote[2:])]
    scratch += [
        pltpu.VMEM((T, D), float32),
        pltpu.VMEM((T, D), float32),
        pltpu.VMEM((T, D), bfloat),
        pltpu.VMEM((K, 2 * D), bfloat),
        pltpu.VMEM((hd, K), float32),
        pltpu.VMEM((hd, K), float32),
        pltpu.SemaphoreType.DMA((10 + z.segments + z.n,)),
    ]
    grads = [((taps, D), float32), ((D, D), float32), ((D, 2 * D), float32), ((8, D), float32)]
    if z.direct:
        args += weights[0]
        in_specs += [anywhere()] * z.n
        scratch += [pltpu.VMEM(s, d) for s, d in grads] + [
            pltpu.VMEM((z.n * 16, D), float32),
            pltpu.VMEM((z.n, z.first_rows - z.cw, D), bfloat),
            pltpu.VMEM((D, D), bfloat),
            pltpu.VMEM((D, 2 * D), bfloat),
        ]
        shapes = block_shapes(z, z.first_grads)
    else:
        for array in (weights[1], weights[2], weights[7]):
            args.append(array)
            in_specs.append(whole(array.shape))
        shapes = grads
    return pl.pallas_call(
        kernel,
        grid=(steps,),
        out_shape=[jax.ShapeDtypeStruct(s, d) for s, d in shapes],
        in_specs=in_specs,
        out_specs=[whole(s) for s, d in shapes],
        scratch_shapes=scratch,
        compiler_params=pltpu.CompilerParams(vmem_limit_bytes=VMEM_LIMIT),
        cost_estimate=pl.CostEstimate(flops=30_000_000_000, bytes_accessed=20_000_000, transcendentals=8_000_000),
        name="back",
    )(*args)


def place_meta(meta):
    def kernel(meta_ref, o_ref):
        for i in range(meta.shape[0]):
            o_ref[i] = meta_ref[i]

    return pl.pallas_call(
        kernel,
        out_shape=jax.ShapeDtypeStruct(meta.shape, meta.dtype),
        in_specs=[smem()],
        out_specs=smem(),
        compiler_params=pltpu.CompilerParams(vmem_limit_bytes=63 * 1024 * 1024),
        name="place_meta",
    )(meta)


def pairs(count, mask):
    return [(i, i ^ mask) for i in range(count)]


def tree_sum(values):
    while len(values) > 1:
        values = [values[i] + values[i + 1] for i in range(0, len(values), 2)]
    return values[0]


def from_chips(z, own):
    return [own] + [lax.ppermute(own, "tm", pairs(z.n, 2 * m)) for m in range(1, z.n // 2)]


def with_core(z, same):
    other = [lax.ppermute(share, "tm", pairs(z.n, 1)) for share in same]
    return [share for pair in zip(same, other) for share in pair]


def over_core(z, keep, send):
    there = lax.ppermute(send, "tm", pairs(z.n, 1))
    sums = [keep[m] + there[m].astype(float32) for m in range(z.n // 2)]
    return sums[:1] + [value.astype(bfloat) for value in sums[1:]]


def over_plane(z, blocks):
    mine = blocks[:1]
    for m in range(1, z.n // 2):
        mine.append(lax.ppermute(blocks[m], "tm", pairs(z.n, 2 * m)).astype(float32))
    return tree_sum(mine)


def over_planes(z, mine):
    parts = [mine[0]]
    for m in range(1, z.planes):
        there = lax.ppermute(mine[m].astype(bfloat), "seg", pairs(z.planes, m))
        parts.append(there.astype(float32))
    low = tree_sum(parts).astype(bfloat)
    return [low] + [lax.ppermute(low, "seg", pairs(z.planes, m)) for m in range(1, z.planes)]


def adam_update(master, first, second, grad, factor, rate):
    clipped = grad * factor
    first_new = beta_first * first + (1.0 - beta_first) * clipped
    second_new = beta_second * second + (1.0 - beta_second) * clipped * clipped
    moment_hat = first_new / (1.0 - beta_first**STEP)
    square_hat = second_new / (1.0 - beta_second**STEP)
    master_new = master - rate * (
        moment_hat / (jnp.sqrt(square_hat) + adam_epsilon) + weight_decay * master
    )
    return (master_new, first_new, second_new)


RATES = (
    learn_rate, learn_rate, learn_rate, fast_rate, learn_rate, learn_rate, learn_rate, fast_rate,
)


def gather_quarters(z, meta_ref, refs, out_ref):
    quarter = refs[0].shape[0]
    for m, ref in enumerate(refs):
        start = pl.multiple_of((meta_ref[8] ^ m) * quarter, 16)
        out_ref[pl.ds(start, quarter), :] = ref[...].astype(float32)


def square_sums(z, meta, first, second):
    D = z.D

    def kernel(meta_ref, *refs):
        planes = z.planes
        a_o, b_o, sq_o = refs[2 * planes :]
        gather_quarters(z, meta_ref, refs[:planes], a_o)
        gather_quarters(z, meta_ref, refs[planes : 2 * planes], b_o)
        loss_row = z.cw + 3 * z.w + 5
        total = jnp.zeros((8, D), float32)
        for ref, skip in ((a_o, loss_row), (b_o, -1)):
            for r in range(0, ref.shape[0], 8):
                here = ref[r : r + 8, :]
                if r <= skip < r + 8:
                    here = jnp.where(iota((8, D), 0) == skip - r, 0.0, here)
                total = total + here * here
        sq_o[0:8, :] = total[:, :LANES] + total[:, LANES : 2 * LANES] + total[:, 2 * LANES :]
        loss = a_o[loss_row - 5 : loss_row + 3, :LANES]
        sq_o[8:16, :] = jnp.where(iota((8, LANES), 0) == 5, loss * (1.0 / z.n), 0.0)

    vmem = pl.BlockSpec(memory_space=pltpu.VMEM)
    shapes = [(z.first_grads, D), (z.second_grads, D), (16, LANES)]
    return pl.pallas_call(
        kernel,
        out_shape=[jax.ShapeDtypeStruct(s, float32) for s in shapes],
        in_specs=[smem()] + [vmem] * (2 * z.planes),
        out_specs=[vmem] * 3,
        compiler_params=pltpu.CompilerParams(vmem_limit_bytes=16 * 1024 * 1024),
        name="square_sums",
    )(meta, *first, *second)


def update(z, squares, first_sum, second_sum, masters, firsts, seconds):
    D, O, w, cw = z.D, z.out, z.w, z.cw
    given = len(squares)

    def kernel(*refs):
        sq_refs = refs[:given]
        a_ref, b_ref = refs[given : given + 2]
        ins = refs[given + 2 : given + 26]
        loss_o, norm_o = refs[given + 26 : given + 28]
        outs = refs[given + 28 :]
        sums = tree_sum([ref[...] for ref in sq_refs])
        norm = jnp.sqrt(jnp.sum(sums[0:8, :], keepdims=True))
        loss_o[...] = jnp.sum(sums[8:16, :], keepdims=True)
        norm_o[...] = norm
        factor = jnp.minimum(1.0, clip_limit / (norm + 1e-06))
        places = {
            0: [(a_ref, 0, cw, 0)],
            1: [(a_ref, cw, w, 0)],
            2: [(a_ref, cw + w + c * w, w, c * D) for c in range(2)],
            3: [(b_ref, 0, w, 0)],
            4: [(b_ref, w + c * w, w, c * D) for c in range(z.F // D)],
            5: [(b_ref, w + z.uw, z.fw, 0)],
        }

        def step(index, here, grad):
            values = adam_update(
                ins[index][here], ins[8 + index][here], ins[16 + index][here], grad, factor, RATES[index]
            )
            for kind, value in enumerate(values):
                outs[8 * kind + index][here] = value

        def block(index, ref, start, lane):
            def body(i, carry):
                here = pl.ds(pl.multiple_of(i * w, 16), w)
                step(index, (here, slice(lane, lane + D)), ref[pl.ds(pl.multiple_of(start + i * w, 16), w), :])
                return carry

            return body

        for index, pieces in places.items():
            for ref, start, count, lane in pieces:
                lax.fori_loop(0, count // w, block(index, ref, start, lane), 0)
        start = w + z.uw + z.fw
        for g in range(D // O):
            here = (slice(g * z.hw, (g + 1) * z.hw), slice(0, O))
            step(6, here, b_ref[start : start + z.hw, g * O : (g + 1) * O])
        gains = a_ref[cw + 3 * w : cw + 3 * w + 8, :][:5, :w]
        step(7, (slice(0, 5), slice(0, w)), gains)

    vmem = pl.BlockSpec(memory_space=pltpu.VMEM)
    outs = [jax.ShapeDtypeStruct((1, 1), float32)] * 2
    outs += [jax.ShapeDtypeStruct(m.shape, float32) for m in masters] * 3
    return pl.pallas_call(
        kernel,
        out_shape=outs,
        in_specs=[vmem] * (given + 26),
        out_specs=[vmem] * 26,
        compiler_params=pltpu.CompilerParams(vmem_limit_bytes=20 * 1024 * 1024),
        name="update",
    )(*squares, first_sum, second_sum, *masters, *firsts, *seconds)


def on_device(*arguments):
    feats, spectral, target, valid_samples, stem_weights = arguments[:5]
    masters, firsts, seconds = arguments[5:13], arguments[13:21], arguments[21:29]
    n = lax.axis_size("tm")
    planes = lax.axis_size("seg")
    z = Sizes(n, planes, feats, spectral, target, masters[0], masters[4])
    S, T, D = z.segments, z.tokens, z.D
    place = lax.axis_index("tm")
    portion, member = place // S, place % S

    if z.direct:
        blobs = pack_weights(z, jnp.reshape(place, (1,)).astype(jnp.int32), masters)
        same_first = from_chips(z, blobs[0])
    else:
        weights = [lax.all_gather(a.astype(bfloat), "tm", axis=0, tiled=True) for a in masters[:7]]
        gains = lax.all_gather(masters[7].astype(bfloat), "tm", axis=1, tiled=True)
        weights.append(jnp.pad(gains.astype(float32), ((0, 3), (0, 0))))
    groups = None if z.parts == 1 else [[p * S + i for i in range(S)] for p in range(z.parts)]

    packed = pack_tokens(z, jnp.transpose(feats, (0, 2, 1)), spectral, target)
    if z.direct:
        packed, *same_first = lax.optimization_barrier((packed, *same_first))
    moved = lax.all_to_all(packed, "tm", 0, 0, axis_index_groups=groups, tiled=True)
    if z.direct:
        weights = [with_core(z, same_first)]
        blob, valid_samples, _ = lax.optimization_barrier((blobs[1], valid_samples, weights[0][1]))
        same_second = from_chips(z, blob)
    rows = z.tokens_dev
    spectral_all, target, halo = moved, moved, None
    if z.parts > 1:
        target = moved[:, :rows, D:]
        spectral_all = lax.all_gather(
            moved[:, :rows, :D].reshape(T, D), "tm", axis=0, tiled=True,
            axis_index_groups=[[p * S + i for p in range(z.parts)] for i in range(S)],
        )
        last = moved[S - 1, rows:, 4 * rows - 2 :].T.reshape(1, -1)
        lead = moved[0, rows:, :2].T.reshape(1, -1)
        halo = (
            lax.ppermute(jnp.pad(last, ((0, 15), (0, 0))), "tm", [(i, i + S) for i in range(n - S)]),
            lax.ppermute(jnp.pad(lead, ((0, 15), (0, 0))), "tm", [(i + S, i) for i in range(n - S)]),
        )
    local_count = jnp.sum(valid_samples)[None]
    if z.direct:
        counts = [local_count] + [lax.ppermute(local_count, "seg", pairs(planes, m)) for m in range(1, planes)]
        sample_count = tree_sum(counts).astype(float32)
    else:
        sample_count = lax.psum(local_count, "seg").astype(float32)
    meta = jnp.concatenate(
        [
            jnp.stack([portion * T, lax.dynamic_index_in_dim(valid_samples, member, keepdims=False)]),
            lax.dynamic_index_in_dim(stem_weights, member, keepdims=False),
            jnp.stack([place // 2, place % 2, lax.axis_index("seg")]),
        ]
    ).astype(jnp.int32)
    meta, sample_count = lax.optimization_barrier((meta, sample_count))
    if z.direct:
        meta = place_meta(meta)

    x, stream, slope, normed, sn, q, k, v, att = front(z, meta, moved, spectral_all, halo, weights)
    if z.direct:
        att, *same_second = lax.optimization_barrier((att, *same_second))
        weights.append(with_core(z, same_second))
    second = middle(z, meta, sample_count, stream, att, target, weights)
    do, mid, misc = second[:3]
    done = 2
    dq, dkv = attend_back(z, q, k, v, do, done)
    if z.direct:
        second_blocks = over_core(z, second[3], second[4])
        dq, *second_blocks = lax.optimization_barrier((dq, *second_blocks))
    first = back(
        z, done, meta, q, k, v, do, dq, dkv, x, spectral_all, halo, stream, slope, normed, sn, mid, misc, weights
    )

    if z.direct:
        second_mine = over_plane(z, second_blocks)
        send, second_mine = lax.optimization_barrier((first[1], second_mine))
        first_blocks = over_core(z, first[0], send)
        second_parts = over_planes(z, second_mine)
        first_parts = over_planes(z, over_plane(z, first_blocks))
        first_sum, second_sum, both = square_sums(z, meta, first_parts, second_parts)
        both = both + lax.ppermute(both, "tm", pairs(n, 1))
        squares = [both] + [lax.ppermute(both, "tm", pairs(n, 2 * m)) for m in range(1, n // 2)]
        result = update(z, squares, first_sum, second_sum, masters, firsts, seconds)
        return (result[0].reshape(()), sample_count.reshape(()), result[1].reshape(()), *result[2:])

    grads = (first[0], first[1], first[2], second[3], second[4], second[5], second[6])
    shards = [lax.psum_scatter(g, "tm", scatter_dimension=0, tiled=True) for g in grads]
    shards.append(lax.psum_scatter(first[3][:5], "tm", scatter_dimension=1, tiled=True))
    reduced = lax.psum(tuple(shards), "seg")
    loss_sum = lax.psum(jnp.sum(first[3][5]), ("seg", "tm"))
    squares = lax.psum(sum(jnp.sum(shard * shard) for shard in reduced), "tm")
    grad_norm = jnp.sqrt(squares)
    factor = jnp.minimum(1.0, clip_limit / (grad_norm + 1e-06))
    updated = [
        adam_update(m, f, s, g, factor, r)
        for m, f, s, g, r in zip(masters, firsts, seconds, reduced, RATES)
    ]
    return (
        loss_sum, sample_count.reshape(()), grad_norm,
        *[u[0] for u in updated], *[u[1] for u in updated], *[u[2] for u in updated],
    )


def solution(mesh):
    rows, columns = P("tm", None), P(None, "tm")
    leaves = (rows,) * 7 + (columns,)
    tokens = P("seg", "tm", None)
    return jax.shard_map(
        on_device,
        mesh=mesh,
        in_specs=(tokens, tokens, tokens, P("seg"), P("seg", None)) + leaves * 3,
        out_specs=(P(), P(), P()) + leaves * 3,
        check_vma=False,
    )
```
